32 devices in a mesh: row: 8 (over y, x, core), rep: 4 (over z).
Axes of the slice: x: 2, y: 2, z: 4, core: 2. Of those that a mesh axis runs over, the one named last changes fastest.
Arguments:
- features: bfloat16 [4096, 256], P('row'), may hold values from -6 to 6
- w_self: bfloat16 [256, 256], replicated, may hold values from -0.375 to 0.375
- w_neigh: bfloat16 [256, 256], replicated, may hold values from -0.375 to 0.375
- bias_vector: float32 [256], replicated, may hold values from -3 to 3
- cotangent: bfloat16 [4096, 256], P('row'), may hold values from -6 to 6
- adj_values: bfloat16 [8, 4, 32, 128, 128], P('row', 'rep'), may hold values from 0 to 1.25, as said below
- src_slots: int32 [8, 4, 32], P('row', 'rep'), may hold values from 0 to 7, as said below
- dst_slots: int32 [8, 4, 32], P('row', 'rep'), may hold values from 0 to 3
- slot_counts: int32 [8, 4], P('row', 'rep'), may hold values from 0 to 32, as said below
Outputs:
- activations: bfloat16 [4096, 256], P(('row', 'rep'))
- grad_features: bfloat16 [4096, 256], P(('row', 'rep'))
- grad_self: float32 [256, 256], replicated
- grad_neigh: float32 [256, 256], replicated
- grad_bias: float32 [256], replicated
The draws below stay inside these ranges and needn't reach their ends.
Inputs may be any that keep to these rules, and one draw needn't show every extreme that they name: `adj_values`: A is symmetric: whenever source tile b appears in a live slot of destination tile a, destination tile b lists source tile a in a live slot with the transposed tile, and a tile whose destination and source coincide is symmetric. Entries are zero or between 0.125 and 1.25. `src_slots`: an entry q names tile q % 4 of row block c * 2 + q // 4, where c is the replica index. `slot_counts`: live slots come first; at most 16 live slots of a row block and replica name one source row block; no pair of destination and source tiles repeats among them; they are ordered by source block, then destination tile, then source tile.
All inputs are finite; a program needn't handle non-finite values.
Results may differ from the reference program's by a relative error of at most 0.015.
Values may be sent and summed in bfloat16 or wider, within the bound.
No kernel may reach another device: no remote copies, remote signals or barrier semaphores. Data moves between devices by JAX's collectives and lax.ppermute only.
A program may use at most 64 MiB of HBM per device.

```python
import math
import jax
import jax.numpy as jnp
from jax import lax

F = 256
H = 256
TILE = 128
PAIR_SLOTS = 16
NB = 512
ROW_BLOCKS = 8
REPLICAS = 4
SECTIONS = 2
TILES_BLK = 4
SLOTS = 32
NODES = 4096


def slot_layout(key):
    base_key = jax.random.fold_in(key, 11)
    tiles_total = ROW_BLOCKS * TILES_BLK
    square = TILES_BLK * TILES_BLK
    level = jax.random.randint(jax.random.fold_in(base_key, 1), (ROW_BLOCKS,), 0, 4)
    outer_shape = (ROW_BLOCKS, REPLICAS, SECTIONS)
    owner = jnp.broadcast_to(jnp.arange(ROW_BLOCKS, dtype=jnp.int32)[:, None, None], outer_shape)
    replica = jnp.broadcast_to(jnp.arange(REPLICAS, dtype=jnp.int32)[None, :, None], outer_shape)
    section = jnp.broadcast_to(jnp.arange(SECTIONS, dtype=jnp.int32)[None, None, :], outer_shape)
    source_block = replica * SECTIONS + section
    lower = jnp.minimum(owner, source_block)
    upper = jnp.maximum(owner, source_block)
    block_pair = lower * ROW_BLOCKS + upper
    wanted = jnp.minimum(PAIR_SLOTS, PAIR_SLOTS * (2 + level[lower] + level[upper]) // 8)
    hub = (lower == 0) & (upper >= SECTIONS) & (upper < 2 * SECTIONS)
    wanted = jnp.where(hub, PAIR_SLOTS, wanted)
    rank_key = jax.random.fold_in(base_key, 2)
    ranks = jax.vmap(lambda pair_one: jnp.argsort(jax.random.permutation(jax.random.fold_in(rank_key, pair_one), square)).astype(jnp.int32))(block_pair.reshape(-1)).reshape(outer_shape + (square,))
    dest_tile = jnp.broadcast_to(jnp.arange(TILES_BLK, dtype=jnp.int32)[:, None], (TILES_BLK, TILES_BLK)).reshape(-1)
    source_tile = jnp.broadcast_to(jnp.arange(TILES_BLK, dtype=jnp.int32)[None, :], (TILES_BLK, TILES_BLK)).reshape(-1)
    forward_pos = dest_tile * TILES_BLK + source_tile
    mirror_pos = source_tile * TILES_BLK + dest_tile
    lower_side = (owner < source_block)[..., None]
    position = jnp.where(lower_side, forward_pos[None, None, None, :], mirror_pos[None, None, None, :])
    rank_here = jnp.take_along_axis(ranks, position, axis=-1)
    same_block = (owner == source_block)[..., None]
    on_diagonal = (dest_tile == source_tile) & (dest_tile < PAIR_SLOTS)
    present = jnp.where(same_block, on_diagonal[None, None, None, :], rank_here < wanted[..., None])
    full_shape = (ROW_BLOCKS, REPLICAS, SECTIONS * square)
    present = present.reshape(full_shape)
    dest_full = jnp.broadcast_to(dest_tile[None, None, None, :], outer_shape + (square,)).reshape(full_shape)
    source_full = jnp.broadcast_to(source_tile[None, None, None, :], outer_shape + (square,)).reshape(full_shape)
    section_full = jnp.broadcast_to(section[..., None], outer_shape + (square,)).reshape(full_shape)
    owner_full = jnp.broadcast_to(owner[..., None], outer_shape + (square,)).reshape(full_shape)
    block_full = jnp.broadcast_to(source_block[..., None], outer_shape + (square,)).reshape(full_shape)
    dest_global = owner_full * TILES_BLK + dest_full
    source_global = block_full * TILES_BLK + source_full
    pair_id = jnp.minimum(dest_global, source_global) * tiles_total + jnp.maximum(dest_global, source_global)
    candidate = jnp.broadcast_to(jnp.arange(SECTIONS * square, dtype=jnp.int32)[None, None, :], full_shape)
    sort_keys = jnp.where(present, 0, SECTIONS * square) + candidate
    order = jnp.argsort(sort_keys, axis=-1)[..., :SLOTS]
    counts = jnp.sum(present.astype(jnp.int32), axis=-1)

    def reorder(values):
        return jnp.take_along_axis(values, order, axis=-1)
    return (reorder(section_full * TILES_BLK + source_full), reorder(dest_full), counts, reorder(pair_id), reorder(dest_global > source_global), reorder(dest_global == source_global))


def draw_adj_values(key, part):
    layout = slot_layout(key)
    value_key = jax.random.fold_in(jax.random.fold_in(key, 11), 3)

    def one_tile(pair_one, flipped, diagonal):
        tile_key = jax.random.fold_in(value_key, pair_one)
        matching = jax.random.permutation(jax.random.fold_in(tile_key, 1), TILE)
        scatter_hits = jax.random.randint(jax.random.fold_in(tile_key, 2), (TILE, TILE), 0, TILE) < 3
        column_ids = jnp.arange(TILE, dtype=jnp.int32)
        nonzero = scatter_hits | (matching[:, None] == column_ids[None, :])
        magnitudes = jax.random.uniform(jax.random.fold_in(tile_key, 3), (TILE, TILE), jnp.float32, 0.25, 1.25)
        tile_values = jnp.where(nonzero, magnitudes, 0.0)
        return jnp.where(diagonal, 0.5 * (tile_values + tile_values.T), jnp.where(flipped, tile_values.T, tile_values))

    def one_block(block_args):
        pair_block, flip_block, diag_block = block_args
        tiles_out = jax.vmap(one_tile)(pair_block.reshape(-1), flip_block.reshape(-1), diag_block.reshape(-1))
        return tiles_out.reshape(REPLICAS, SLOTS, TILE, TILE).astype(jnp.bfloat16)
    return lax.map(one_block, (layout[3], layout[4], layout[5]))


def draw_src_slots(key, part):
    return slot_layout(key)[0]


def draw_dst_slots(key, part):
    return slot_layout(key)[1]


def draw_slot_counts(key, part):
    return slot_layout(key)[2]


def levels(own_key, shape, shards, low, top_value):
    def one(dim, blocks):
        draws = jax.random.uniform(jax.random.fold_in(jax.random.fold_in(own_key, 6), dim), (blocks,), jnp.float32, low / len(shards), top_value / len(shards))
        return jnp.repeat(jnp.exp(draws), shape[dim] // blocks).reshape((-1,) + (1,) * (len(shape) - dim - 1))

    loudness = one(*shards[0])
    for cut in shards[1:]:
        loudness = loudness * one(*cut)
    return loudness


def scatter_about(key, dims, spread, most, cuts=(), kind=jnp.bfloat16):
    result = spread * jax.random.normal(key, dims, jnp.float32)
    if cuts:
        result = result * levels(key, dims, cuts, -0.22, 0.18)
    return jnp.clip(result, -most, most).astype(kind)


def setup_inputs(seed: int = 0) -> dict:
    seeds = jax.random.split(jax.random.key(seed), 10)
    features = scatter_about(seeds[0], (NODES, F), 1.0, 6.0, ((0, 8),))
    w_self = scatter_about(seeds[1], (F, H), F ** -0.5, 0.375)
    w_neigh = scatter_about(seeds[2], (F, H), F ** -0.5, 0.375)
    bias_vector = scatter_about(seeds[3], (H,), 0.5, 3.0, (), jnp.float32)
    cotangent = scatter_about(seeds[4], (NODES, H), 1.0, 6.0, ((0, 8),))
    adj_values = draw_adj_values(jax.random.fold_in(seeds[9], 71), 0)
    src_slots = draw_src_slots(jax.random.fold_in(seeds[9], 71), 0)
    dst_slots = draw_dst_slots(jax.random.fold_in(seeds[9], 71), 0)
    slot_counts = draw_slot_counts(jax.random.fold_in(seeds[9], 71), 0)
    return {"features": features, "w_self": w_self, "w_neigh": w_neigh, "bias_vector": bias_vector, "cotangent": cotangent, "adj_values": adj_values, "src_slots": src_slots, "dst_slots": dst_slots, "slot_counts": slot_counts}


def aggregate_raw(adj_values, src_slots, dst_slots, slot_counts, field):
    field_tiles = field.reshape(ROW_BLOCKS * TILES_BLK, TILE, F)
    replica_base = jnp.arange(REPLICAS, dtype=jnp.int32)[:, None] * (SECTIONS * TILES_BLK)
    slot_index = jnp.arange(SLOTS, dtype=jnp.int32)[None, :]
    dest_range = jnp.arange(TILES_BLK, dtype=jnp.int32)

    def one_block(block_no):
        values = adj_values[block_no].astype(field.dtype)
        sources = replica_base + src_slots[block_no]
        gathered = field_tiles[sources]
        products = jnp.einsum('csab,csbf->csaf', values, gathered, precision=lax.Precision.HIGHEST)
        alive = slot_index < slot_counts[block_no][:, None]
        chosen = ((dst_slots[block_no][:, :, None] == dest_range[None, None, :]) & alive[:, :, None]).astype(field.dtype)
        return jnp.einsum('cst,csaf->taf', chosen, products, precision=lax.Precision.HIGHEST).reshape(NB, F)
    blocks_out = lax.map(one_block, jnp.arange(ROW_BLOCKS, dtype=jnp.int32))
    return blocks_out.reshape(NODES, F)

def transpose_raw(adj_values, src_slots, dst_slots, slot_counts, field):
    field_tiles = field.reshape(ROW_BLOCKS, TILES_BLK, TILE, F)
    replica_base = jnp.arange(REPLICAS, dtype=jnp.int32)[:, None] * (SECTIONS * TILES_BLK)
    slot_index = jnp.arange(SLOTS, dtype=jnp.int32)[None, :]
    dest_range = jnp.arange(TILES_BLK, dtype=jnp.int32)

    def one_block(carried, block_no):
        values = adj_values[block_no].astype(field.dtype)
        alive = slot_index < slot_counts[block_no][:, None]
        chosen = ((dst_slots[block_no][:, :, None] == dest_range[None, None, :]) & alive[:, :, None]).astype(field.dtype)
        dest_rows = jnp.einsum('cst,taf->csaf', chosen, field_tiles[block_no], precision=lax.Precision.HIGHEST)
        sent = jnp.einsum('csab,csaf->csbf', values, dest_rows, precision=lax.Precision.HIGHEST)
        sources = (replica_base + src_slots[block_no]).reshape(-1)
        return (carried.at[sources].add(sent.reshape(-1, TILE, F)), None)
    start_value = jnp.zeros((ROW_BLOCKS * TILES_BLK, TILE, F), field.dtype)
    summed, _ = lax.scan(one_block, start_value, jnp.arange(ROW_BLOCKS, dtype=jnp.int32))
    return summed.reshape(NODES, F)

def reference(features, w_self, w_neigh, bias_vector, cotangent, adj_values, src_slots, dst_slots, slot_counts):
    norm_factor = 1.0 / math.sqrt(SLOTS * REPLICAS / TILES_BLK)
    grad_factor = 1.0 / math.sqrt(NODES)
    raw_sum = aggregate_raw(adj_values, src_slots, dst_slots, slot_counts, features.astype(jnp.float32))
    aggregate = (raw_sum * norm_factor).astype(jnp.bfloat16)
    pre_act = jnp.dot(features, w_self, preferred_element_type=jnp.float32) + jnp.dot(aggregate, w_neigh, preferred_element_type=jnp.float32) + bias_vector
    activations = jax.nn.elu(pre_act).astype(jnp.bfloat16)
    grad_pre = (cotangent.astype(jnp.float32) * jnp.exp(jnp.minimum(pre_act, 0.0))).astype(jnp.bfloat16)
    grad_self = jnp.dot(features.T, grad_pre, preferred_element_type=jnp.float32) * grad_factor
    grad_neigh = jnp.dot(aggregate.T, grad_pre, preferred_element_type=jnp.float32) * grad_factor
    grad_bias = lax.optimization_barrier(jnp.sum(grad_pre.astype(jnp.float32), axis=0)) * grad_factor
    message = jnp.dot(grad_pre, w_neigh.T, preferred_element_type=jnp.float32).astype(jnp.bfloat16)
    returned = transpose_raw(adj_values, src_slots, dst_slots, slot_counts, message.astype(jnp.float32))
    self_term = jnp.dot(grad_pre, w_self.T, preferred_element_type=jnp.float32)
    grad_features = (self_term + returned * norm_factor).astype(jnp.bfloat16)
    return (activations, grad_features, grad_self, grad_neigh, grad_bias)
```

```python
import functools
import math

import jax
import jax.numpy as jnp
from jax import lax
from jax.experimental import pallas as pl
from jax.experimental.pallas import tpu as pltpu
from jax.sharding import PartitionSpec as P

F32 = jnp.float32
BF16 = jnp.bfloat16
VMEM = pl.BlockSpec(memory_space=pltpu.VMEM)
SMEM = pl.BlockSpec(memory_space=pltpu.SMEM)
LIMIT = 16 * 1024 * 1024


def call(body, outs, ins, scratch=()):
    return pl.pallas_call(
        body,
        out_shape=outs,
        in_specs=ins,
        out_specs=[VMEM] * len(outs),
        scratch_shapes=list(scratch),
        compiler_params=pltpu.CompilerParams(vmem_limit_bytes=LIMIT),
    )


def shape(dims, kind):
    return jax.ShapeDtypeStruct(tuple(dims), kind)


def swap(value, axis, step):
    return lax.ppermute(value, axis, [(i, i ^ step) for i in range(lax.axis_size(axis))])


def contract(left, right, left_dim, right_dim):
    return lax.dot_general(
        left, right, (((left_dim,), (right_dim,)), ((), ())), preferred_element_type=F32
    )


def tree_sum(parts):
    while len(parts) > 1:
        parts = [parts[i] + parts[i + 1] for i in range(0, len(parts), 2)]
    return parts[0]


def first_kernel(share, src, dst, count, tiles, field, dense, own, *rest):
    others, total = rest[:-1], rest[-1]
    size = tiles.shape[-1]
    me = lax.axis_index("row")
    dense[...] = jnp.zeros_like(dense)

    def place(e, carry):
        row = pl.multiple_of(dst[0, 0, e] * size, size)
        col = pl.multiple_of(src[0, 0, e] * size, size)
        dense[pl.ds(row, size), pl.ds(col, size)] = tiles[0, 0, e]
        return carry

    lax.fori_loop(0, count[0, 0], place, 0)
    for s in range(dense.shape[1] // size):
        cols = pl.ds(s * size, size)
        total[cols, :] = contract(dense[:, cols], field[...], 0, 0)
    own[...] = total[pl.ds(pl.multiple_of(me * share, share), share), :]
    for k, out in enumerate(others, 1):
        start = pl.multiple_of((me ^ k) * share, share)
        out[...] = total[pl.ds(start, share), :].astype(BF16)


def middle_kernel(count, norm, parts, *refs):
    own, received = refs[0], refs[1:count]
    field, cotangent, w_self, w_neigh, bias = refs[count : count + 5]
    act, grad_out = refs[count + 5 : count + 7]
    letters = refs[count + 7 : 2 * count + 7]
    turned_f, turned_a = refs[2 * count + 7 :]
    share = field.shape[0]
    rows = field.shape[1] // parts
    me = lax.axis_index("row")
    total = own[...]
    for ref in received:
        total = total + ref[...].astype(F32)
    aggregate = (total * norm).astype(BF16)
    pre = contract(field[...], w_self[...], 1, 0) + contract(aggregate, w_neigh[...], 1, 0)
    pre = pre + bias[...]
    slope = jnp.exp(jnp.minimum(pre, 0.0))
    act[...] = jnp.where(pre > 0.0, pre, slope - 1.0).astype(BF16)
    grad = (cotangent[...].astype(F32) * slope).astype(BF16)
    grad_out[...] = grad
    turned_f[...] = field[...].T
    turned_a[...] = aggregate.T
    for k, letter in enumerate(letters):
        first = pl.multiple_of(((me ^ k) % parts) * rows, rows)
        letter[pl.ds(0, share), :] = grad
        letter[pl.ds(share, rows), pl.ds(0, share)] = turned_f[pl.ds(first, rows), :]
        letter[pl.ds(share, rows), pl.ds(128, share)] = turned_a[pl.ds(first, rows), :]


def back_kernel(count, share, rows, *refs):
    letters = refs[:count]
    dense, w_neigh = refs[count : count + 2]
    own = refs[count + 2]
    others = refs[count + 3 : -4]
    terms, sorted_letters, message, total = refs[-4:]
    me_row, me_rep = lax.axis_index("row"), lax.axis_index("rep")
    width = w_neigh.shape[0]
    for k, letter in enumerate(letters):
        sorted_letters[me_row ^ k] = letter[...]
    self_sum = jnp.zeros((rows, width), F32)
    neigh_sum = jnp.zeros((rows, width), F32)
    bias_sum = jnp.zeros((16, width), F32)
    ones = jnp.ones((16, share), BF16)
    for j in range(count):
        grad = sorted_letters[j, pl.ds(0, share), :]
        message[pl.ds(j * share, share), :] = contract(grad, w_neigh[...], 1, 1).astype(BF16)
        self_sum += contract(sorted_letters[j, pl.ds(share, rows), pl.ds(0, share)], grad, 1, 0)
        neigh_sum += contract(sorted_letters[j, pl.ds(share, rows), pl.ds(128, share)], grad, 1, 0)
        bias_sum += contract(ones, grad, 1, 0)
    total[...] = contract(dense[...], message[...], 1, 0)
    own[...] = total[pl.ds(pl.multiple_of(me_rep * share, share), share), :]
    for k, out in enumerate(others, 1):
        start = pl.multiple_of((me_rep ^ k) * share, share)
        out[...] = total[pl.ds(start, share), :].astype(BF16)
    high = bias_sum.astype(BF16).astype(F32)
    low = bias_sum - high
    line = lax.broadcasted_iota(jnp.int32, bias_sum.shape, 0)
    terms[pl.ds(0, rows), :] = self_sum.astype(BF16)
    terms[pl.ds(rows, rows), :] = neigh_sum.astype(BF16)
    terms[pl.ds(2 * rows, 16), :] = jnp.where(line == 0, high, low).astype(BF16)


def level_kernel(rows, factor, *refs):
    terms, (summed, bias) = refs[:-2], refs[-2:]
    values = [ref[...].astype(F32) for ref in terms]
    summed[...] = tree_sum([v[: 2 * rows] for v in values]).astype(BF16)
    tails = [v[2 * rows : 2 * rows + 8] for v in values]
    bias[...] = tree_sum([t[0:1] + t[1:2] for t in tails]) * factor


def collect_kernel(rows, factor, *refs):
    pieces, (grad_self, grad_neigh) = refs[:-2], refs[-2:]
    me = lax.axis_index("row") % len(pieces)
    for k, piece in enumerate(pieces):
        place = pl.ds(pl.multiple_of((me ^ k) * rows, rows), rows)
        grad_self[place, :] = piece[pl.ds(0, rows), :].astype(F32) * factor
        grad_neigh[place, :] = piece[pl.ds(rows, rows), :].astype(F32) * factor


def last_kernel(norm, *refs):
    own, received = refs[0], refs[1:-3]
    grad, w_self, out = refs[-3:]
    total = own[...]
    for ref in received:
        total = total + ref[...].astype(F32)
    out[...] = (contract(grad[...], w_self[...], 1, 1) + total * norm).astype(BF16)


def shards(
    features, w_self, w_neigh, bias_vector, cotangent, adj_values, src_slots, dst_slots, slot_counts
):
    block_rows, width = features.shape
    blocks, replicas = lax.axis_size("row"), lax.axis_size("rep")
    sections = blocks // replicas
    share = block_rows // replicas
    slot_total, size = adj_values.shape[2], adj_values.shape[-1]
    norm = 1.0 / math.sqrt(slot_total * replicas / (block_rows // size))
    factor = 1.0 / math.sqrt(block_rows * blocks)
    parts = min(blocks, width // 16)
    rows = width // parts
    piece = (share, width)

    devices = blocks * replicas
    away = [(t, (t % blocks) * replicas + t // blocks) for t in range(devices)]
    home = [(b, a) for a, b in away]
    offset = lax.axis_index("rep") * share
    field_here = lax.ppermute(
        lax.dynamic_slice_in_dim(features, offset, share, 0), ("row", "rep"), away
    )
    cotangent_here = lax.ppermute(
        lax.dynamic_slice_in_dim(cotangent, offset, share, 0), ("row", "rep"), away
    )

    dense, own, *sent = call(
        functools.partial(first_kernel, share),
        [shape((block_rows, sections * block_rows), BF16), shape(piece, F32)]
        + [shape(piece, BF16)] * (blocks - 1),
        [SMEM] * 3 + [VMEM] * 2,
        [pltpu.VMEM((sections * block_rows, width), F32)],
    )(src_slots, dst_slots, slot_counts, adj_values, features)
    received = [swap(value, "row", k) for k, value in enumerate(sent, 1)]

    act, grad, *letters = call(
        functools.partial(middle_kernel, blocks, norm, parts),
        [shape(piece, BF16)] * 2 + [shape((share + rows, width), BF16)] * blocks,
        [VMEM] * (blocks + 5),
        [pltpu.VMEM((width, share), BF16)] * 2,
    )(own, *received, field_here, cotangent_here, w_self, w_neigh, bias_vector[None, :])
    letters = letters[:1] + [swap(value, "row", k) for k, value in enumerate(letters[1:], 1)]
    activations = lax.ppermute(act, ("row", "rep"), home)
    grad_home = lax.ppermute(grad, ("row", "rep"), home)

    back_own, *rest = call(
        functools.partial(back_kernel, blocks, share, rows),
        [shape(piece, F32)]
        + [shape(piece, BF16)] * (replicas - 1)
        + [shape((2 * rows + 16, width), BF16)],
        [VMEM] * (blocks + 2),
        [
            pltpu.VMEM((blocks, share + rows, width), BF16),
            pltpu.VMEM((sections * block_rows, width), BF16),
            pltpu.VMEM((block_rows, width), F32),
        ],
    )(*letters, dense, w_neigh)
    back_sent, terms = rest[:-1], rest[-1]
    terms_here = [terms] + [swap(terms, "rep", k) for k in range(1, replicas)]
    back_received = [swap(value, "rep", k) for k, value in enumerate(back_sent, 1)]

    summed, grad_bias = call(
        functools.partial(level_kernel, rows, factor),
        [shape((2 * rows, width), BF16), shape((1, width), F32)],
        [VMEM] * replicas,
    )(*terms_here)
    pieces = [summed] + [swap(summed, "row", k) for k in range(1, parts)]
    (grad_features,) = call(
        functools.partial(last_kernel, norm),
        [shape(piece, BF16)],
        [VMEM] * (replicas + 2),
    )(back_own, *back_received, grad_home, w_self)
    grad_self, grad_neigh = call(
        functools.partial(collect_kernel, rows, factor),
        [shape((width, width), F32)] * 2,
        [VMEM] * parts,
    )(*pieces)
    return activations, grad_features, grad_self, grad_neigh, grad_bias[0]


def solution(mesh):
    placed = (
        P("row", None),
        P(),
        P(),
        P(),
        P("row", None),
        P("row", "rep", None, None, None),
        P("row", "rep", None),
        P("row", "rep", None),
        P("row", "rep"),
    )
    return jax.shard_map(
        shards,
        mesh=mesh,
        in_specs=placed,
        out_specs=(P(("row", "rep"), None), P(("row", "rep"), None), P(), P(), P()),
        check_vma=False,
    )
```

```python
import functools
import math

import jax
import jax.numpy as jnp
from jax import lax
from jax.experimental import pallas as pl
from jax.experimental.pallas import tpu as pltpu
from jax.sharding import PartitionSpec as P

F32 = jnp.float32
BF16 = jnp.bfloat16
VMEM = pl.BlockSpec(memory_space=pltpu.VMEM)
SMEM = pl.BlockSpec(memory_space=pltpu.SMEM)
LIMIT = 16 * 1024 * 1024


def call(body, outs, ins, scratch=()):
    return pl.pallas_call(
        body,
        out_shape=outs,
        in_specs=ins,
        out_specs=[VMEM] * len(outs),
        scratch_shapes=list(scratch),
        compiler_params=pltpu.CompilerParams(vmem_limit_bytes=LIMIT),
    )


def shape(dims, kind):
    return jax.ShapeDtypeStruct(tuple(dims), kind)


def exchange(value, axis):
    return lax.all_to_all(value, axis, split_axis=0, concat_axis=0, tiled=True)


def contract(left, right, left_dim, right_dim):
    return lax.dot_general(
        left, right, (((left_dim,), (right_dim,)), ((), ())), preferred_element_type=F32
    )


def first_kernel(src, dst, count, tiles, field, dense, out):
    size = tiles.shape[-1]
    dense[...] = jnp.zeros_like(dense)

    def place(e, carry):
        row = pl.multiple_of(dst[0, 0, e] * size, size)
        col = pl.multiple_of(src[0, 0, e] * size, size)
        dense[pl.ds(row, size), pl.ds(col, size)] = tiles[0, 0, e]
        return carry

    lax.fori_loop(0, count[0, 0], place, 0)
    for s in range(dense.shape[1] // size):
        cols = pl.ds(s * size, size)
        out[cols, :] = contract(dense[:, cols], field[...], 0, 0).astype(BF16)


def middle_kernel(
    norm, blocks, parts, received, pair, w_self, w_neigh, bias, act, letters, turned_f, turned_a
):
    share, width = act.shape
    rows = width // parts
    total = jnp.zeros((share, width), F32)
    for j in range(blocks):
        total = total + received[pl.ds(j * share, share), :].astype(F32)
    aggregate = (total * norm).astype(BF16)
    field = pair[pl.ds(0, share), :]
    pre = contract(field, w_self[...], 1, 0) + contract(aggregate, w_neigh[...], 1, 0)
    pre = pre + bias[...]
    slope = jnp.exp(jnp.minimum(pre, 0.0))
    act[...] = jnp.where(pre > 0.0, pre, slope - 1.0).astype(BF16)
    grad = (pair[pl.ds(share, share), :].astype(F32) * slope).astype(BF16)
    turned_f[...] = field.T
    turned_a[...] = aggregate.T
    for j in range(blocks):
        base = j * (share + rows)
        slots = pl.ds((j % parts) * rows, rows)
        letters[pl.ds(base, share), :] = grad
        letters[pl.ds(base + share, rows), pl.ds(0, share)] = turned_f[slots, :]
        letters[pl.ds(base + share, rows), pl.ds(128, share)] = turned_a[slots, :]


def back_kernel(norm, blocks, replicas, rows, letters, dense, w_self, w_neigh, out, message, total):
    me_row, me_rep = lax.axis_index("row"), lax.axis_index("rep")
    width = w_neigh.shape[0]
    block_rows = dense.shape[0]
    share = block_rows // replicas
    sections = blocks // replicas
    step = share + rows
    self_sum = jnp.zeros((rows, width), F32)
    neigh_sum = jnp.zeros((rows, width), F32)
    bias_sum = jnp.zeros((16, width), F32)
    ones = jnp.ones((16, share), BF16)
    for j in range(blocks):
        grad = letters[pl.ds(j * step, share), :]
        message[pl.ds(j * share, share), :] = contract(grad, w_neigh[...], 1, 1).astype(BF16)
        turned = pl.ds(j * step + share, rows)
        self_sum += contract(letters[turned, pl.ds(0, share)], grad, 1, 0)
        neigh_sum += contract(letters[turned, pl.ds(128, share)], grad, 1, 0)
        bias_sum += contract(ones, grad, 1, 0)
    total[...] = contract(dense[...], message[...], 1, 0) * norm

    @pl.when(me_rep == me_row // sections)
    def _():
        for i in range(replicas):
            j = (me_row % sections) * replicas + i
            grad = letters[pl.ds(pl.multiple_of(j * step, 16), share), :]
            total[pl.ds(i * share, share), :] += contract(grad, w_self[...], 1, 1)

    high = bias_sum.astype(BF16).astype(F32)
    line = lax.broadcasted_iota(jnp.int32, bias_sum.shape, 0)
    tail = jnp.where(line == 0, high, bias_sum - high).astype(BF16)
    span = share + 2 * rows + 16
    for i in range(replicas):
        base = i * span
        out[pl.ds(base, share), :] = total[pl.ds(i * share, share), :].astype(BF16)
        out[pl.ds(base + share, rows), :] = self_sum.astype(BF16)
        out[pl.ds(base + share + rows, rows), :] = neigh_sum.astype(BF16)
        out[pl.ds(base + share + 2 * rows, 16), :] = tail


def level_kernel(replicas, copies, rows, factor, received, grad_features, bias, summed):
    share, width = grad_features.shape
    span = share + 2 * rows + 16
    total = jnp.zeros((share, width), F32)
    terms = jnp.zeros((2 * rows + 16, width), F32)
    for i in range(replicas):
        total = total + received[pl.ds(i * span, share), :].astype(F32)
        terms = terms + received[pl.ds(i * span + share, 2 * rows + 16), :].astype(F32)
    grad_features[...] = total.astype(BF16)
    tail = terms[2 * rows : 2 * rows + 8]
    bias[...] = (tail[0:1] + tail[1:2]) * factor
    half = terms[: 2 * rows].astype(BF16)
    for j in range(copies):
        summed[pl.ds(j * 2 * rows, 2 * rows), :] = half


def collect_kernel(parts, rows, factor, pieces, grad_self, grad_neigh):
    for j in range(parts):
        place = pl.ds(j * rows, rows)
        base = j * 2 * rows
        grad_self[place, :] = pieces[pl.ds(base, rows), :].astype(F32) * factor
        grad_neigh[place, :] = pieces[pl.ds(base + rows, rows), :].astype(F32) * factor


def shards(
    features, w_self, w_neigh, bias_vector, cotangent, adj_values, src_slots, dst_slots, slot_counts
):
    block_rows, width = features.shape
    blocks, replicas = lax.axis_size("row"), lax.axis_size("rep")
    sections = blocks // replicas
    share = block_rows // replicas
    slot_total, size = adj_values.shape[2], adj_values.shape[-1]
    norm = 1.0 / math.sqrt(slot_total * replicas / (block_rows // size))
    factor = 1.0 / math.sqrt(block_rows * blocks)
    parts = min(blocks, width // 16)
    rows = width // parts

    devices = blocks * replicas
    away = [(t, (t % blocks) * replicas + t // blocks) for t in range(devices)]
    home = [(b, a) for a, b in away]
    offset = lax.axis_index("rep") * share
    pair = jnp.concatenate(
        [
            lax.dynamic_slice_in_dim(features, offset, share, 0),
            lax.dynamic_slice_in_dim(cotangent, offset, share, 0),
        ]
    )
    pair = lax.ppermute(pair, ("row", "rep"), away)

    plane_rows = sections * block_rows
    dense, sent = call(
        first_kernel,
        [shape((block_rows, plane_rows), BF16), shape((plane_rows, width), BF16)],
        [SMEM] * 3 + [VMEM] * 2,
    )(src_slots, dst_slots, slot_counts, adj_values, features)
    received = exchange(sent, "row")

    act, letters = call(
        functools.partial(middle_kernel, norm, blocks, parts),
        [shape((share, width), BF16), shape((blocks * (share + rows), width), BF16)],
        [VMEM] * 5,
        [pltpu.VMEM((width, share), BF16)] * 2,
    )(received, pair, w_self, w_neigh, bias_vector[None, :])
    letters = exchange(letters, "row")
    activations = lax.ppermute(act, ("row", "rep"), home)

    (sent,) = call(
        functools.partial(back_kernel, norm, blocks, replicas, rows),
        [shape((replicas * (share + 2 * rows + 16), width), BF16)],
        [VMEM] * 4,
        [pltpu.VMEM((plane_rows, width), BF16), pltpu.VMEM((block_rows, width), F32)],
    )(letters, dense, w_self, w_neigh)
    received = exchange(sent, "rep")

    grad_features, grad_bias, summed = call(
        functools.partial(level_kernel, replicas, blocks, rows, factor),
        [
            shape((share, width), BF16),
            shape((1, width), F32),
            shape((blocks * 2 * rows, width), BF16),
        ],
        [VMEM],
    )(received)
    pieces = exchange(summed, "row")
    grad_self, grad_neigh = call(
        functools.partial(collect_kernel, parts, rows, factor),
        [shape((width, width), F32)] * 2,
        [VMEM],
    )(pieces)
    return activations, grad_features, grad_self, grad_neigh, grad_bias[0]


def solution(mesh):
    placed = (
        P("row", None),
        P(),
        P(),
        P(),
        P("row", None),
        P("row", "rep", None, None, None),
        P("row", "rep", None),
        P("row", "rep", None),
        P("row", "rep"),
    )
    return jax.shard_map(
        shards,
        mesh=mesh,
        in_specs=placed,
        out_specs=(P(("row", "rep"), None), P(("row", "rep"), None), P(), P(), P()),
        check_vma=False,
    )
```

```python
import functools
import math

import jax
import jax.numpy as jnp
from jax import lax
from jax.experimental import pallas as pl
from jax.experimental.pallas import tpu as pltpu
from jax.sharding import PartitionSpec as P

F32 = jnp.float32
BF16 = jnp.bfloat16
VMEM = pl.BlockSpec(memory_space=pltpu.VMEM)
SMEM = pl.BlockSpec(memory_space=pltpu.SMEM)
LIMIT = 16 * 1024 * 1024


def call(body, outs, ins, scratch=()):
    kernel = pl.pallas_call(
        body,
        out_shape=outs,
        in_specs=ins,
        out_specs=[VMEM] * len(outs),
        scratch_shapes=list(scratch),
        compiler_params=pltpu.CompilerParams(vmem_limit_bytes=LIMIT),
    )
    return lambda *operands: list(kernel(*operands))


def shape(dims, kind):
    return jax.ShapeDtypeStruct(tuple(dims), kind)


def swap(value, step):
    return lax.ppermute(value, "row", [(i, i ^ step) for i in range(lax.axis_size("row"))])


def swap_rep(value, step):
    return lax.ppermute(value, "rep", [(i, i ^ step) for i in range(lax.axis_size("rep"))])


def contract(left, right, left_dim, right_dim):
    return lax.dot_general(
        left, right, (((left_dim,), (right_dim,)), ((), ())), preferred_element_type=F32
    )


def tree_sum(parts):
    while len(parts) > 1:
        parts = [parts[i] + parts[i + 1] for i in range(0, len(parts), 2)]
    return parts[0]


def place_of(sections):
    me = lax.axis_index("row")
    return me // sections, me % sections


def piece_of(ref, index, span):
    return ref[pl.ds(pl.multiple_of(index * span, span), span), :]


def first_kernel(sections, src, dst, count, tiles, field, dense, own, *rest):
    others, total = rest[:-1], rest[-1]
    size = tiles.shape[-1]
    block_rows = field.shape[0]
    _, s = place_of(sections)
    dense[...] = jnp.zeros_like(dense)

    def place(e, carry):
        row = pl.multiple_of(dst[0, 0, e] * size, size)
        col = pl.multiple_of(src[0, 0, e] * size, size)
        dense[pl.ds(row, size), pl.ds(col, size)] = tiles[0, 0, e]
        return carry

    lax.fori_loop(0, count[0, 0], place, 0)
    for t in range(dense.shape[1] // size):
        cols = pl.ds(t * size, size)
        total[cols, :] = contract(dense[:, cols], field[...], 0, 0)
    own[...] = piece_of(total, s, block_rows)
    for k, out in enumerate(others, 1):
        out[...] = piece_of(total, s ^ k, block_rows).astype(BF16)


def block_kernel(sections, *refs):
    parts, own, others, total = refs[:sections], refs[sections], refs[sections + 1 : -1], refs[-1]
    share = own.shape[0]
    q, _ = place_of(sections)
    value = parts[0][...]
    for ref in parts[1:]:
        value = value + ref[...].astype(F32)
    total[...] = value
    own[...] = piece_of(total, q, share)
    for k, out in enumerate(others, 1):
        out[...] = piece_of(total, q ^ k, share).astype(BF16)


def middle_kernel(norm, sections, replicas, parts, *refs):
    tiles, (pair, w_self, w_neigh, bias, act) = refs[:replicas], refs[replicas : replicas + 5]
    letters, (turned_f, turned_a) = refs[replicas + 5 : -2], refs[-2:]
    share, width = act.shape
    rows = width // parts
    q, _ = place_of(sections)
    total = tiles[0][...]
    for ref in tiles[1:]:
        total = total + ref[...].astype(F32)
    aggregate = (total * norm).astype(BF16)
    field = pair[pl.ds(0, share), :]
    pre = contract(field, w_self[...], 1, 0) + contract(aggregate, w_neigh[...], 1, 0)
    pre = pre + bias[...]
    slope = jnp.exp(jnp.minimum(pre, 0.0))
    act[...] = jnp.where(pre > 0.0, pre, slope - 1.0).astype(BF16)
    grad = (pair[pl.ds(share, share), :].astype(F32) * slope).astype(BF16)
    turned_f[...] = field.T
    turned_a[...] = aggregate.T
    span = sections * rows
    for k, letter in enumerate(letters):
        slot = (q ^ k) % (parts // sections)
        letter[pl.ds(0, share), :] = grad
        letter[pl.ds(share, span), pl.ds(0, share)] = piece_of(turned_f, slot, span)
        letter[pl.ds(share, span), pl.ds(128, share)] = piece_of(turned_a, slot, span)


def pack_kernel(sections, share, rows, *refs):
    letters, packs = refs[:-sections], refs[-sections:]
    q, s = place_of(sections)
    step = share + rows
    for k, letter in enumerate(letters):
        base = pl.multiple_of((q ^ k) * step, 16)
        for m, pack in enumerate(packs):
            first = pl.multiple_of(share + (s ^ m) * rows, 16)
            pack[pl.ds(base, share), :] = letter[pl.ds(0, share), :]
            pack[pl.ds(base + share, rows), :] = letter[pl.ds(first, rows), :]


def back_kernel(norm, sections, replicas, rows, *refs):
    packs, (dense, w_self, w_neigh) = refs[:sections], refs[sections : sections + 3]
    outs, (letters, message, total) = refs[sections + 3 : -3], refs[-3:]
    me_rep = lax.axis_index("rep")
    q, s = place_of(sections)
    width = w_neigh.shape[0]
    share = dense.shape[0] // replicas
    step = share + rows
    block_span = replicas * step
    for k, pack in enumerate(packs):
        letters[pl.ds(pl.multiple_of((s ^ k) * block_span, 16), block_span), :] = pack[...]
    self_sum = jnp.zeros((rows, width), F32)
    neigh_sum = jnp.zeros((rows, width), F32)
    bias_sum = jnp.zeros((16, width), F32)
    ones = jnp.ones((16, share), BF16)
    for j in range(sections * replicas):
        grad = letters[pl.ds(j * step, share), :]
        message[pl.ds(j * share, share), :] = contract(grad, w_neigh[...], 1, 1).astype(BF16)
        turned = pl.ds(j * step + share, rows)
        self_sum += contract(letters[turned, pl.ds(0, share)], grad, 1, 0)
        neigh_sum += contract(letters[turned, pl.ds(128, share)], grad, 1, 0)
        bias_sum += contract(ones, grad, 1, 0)
    total[...] = contract(dense[...], message[...], 1, 0) * norm

    @pl.when(me_rep == q)
    def _():
        for i in range(replicas):
            grad = packs[0][pl.ds(i * step, share), :]
            total[pl.ds(i * share, share), :] += contract(grad, w_self[...], 1, 1)

    high = bias_sum.astype(BF16).astype(F32)
    line = lax.broadcasted_iota(jnp.int32, bias_sum.shape, 0)
    tail = jnp.where(line == 0, high, bias_sum - high).astype(BF16)
    for k, out in enumerate(outs):
        out[pl.ds(0, share), :] = piece_of(total, me_rep ^ k, share).astype(BF16)
        out[pl.ds(share, rows), :] = self_sum.astype(BF16)
        out[pl.ds(share + rows, rows), :] = neigh_sum.astype(BF16)
        out[pl.ds(share + 2 * rows, 16), :] = tail


def level_kernel(rows, factor, *refs):
    parts, (grad_features, bias, summed) = refs[:-3], refs[-3:]
    share = grad_features.shape[0]
    total = tree_sum([ref[pl.ds(0, share), :].astype(F32) for ref in parts])
    grad_features[...] = total.astype(BF16)
    terms = tree_sum([ref[pl.ds(share, 2 * rows + 16), :].astype(F32) for ref in parts])
    tail = terms[2 * rows : 2 * rows + 8]
    bias[...] = (tail[0:1] + tail[1:2]) * factor
    summed[...] = terms[: 2 * rows].astype(BF16)


def join_kernel(sections, *refs):
    pieces, out = refs[:-1], refs[-1]
    span = pieces[0].shape[0]
    q, _ = place_of(sections)
    for k, piece in enumerate(pieces):
        slot = (q % len(pieces)) ^ k
        out[pl.ds(pl.multiple_of(slot * span, 16), span), :] = piece[...]


def collect_kernel(rows, factor, *refs):
    joined, (grad_self, grad_neigh) = refs[:-2], refs[-2:]
    sections = len(joined)
    _, s = place_of(sections)
    for k, ref in enumerate(joined):
        for j in range(ref.shape[0] // (2 * rows)):
            place = pl.ds(pl.multiple_of((j * sections + (s ^ k)) * rows, rows), rows)
            base = j * 2 * rows
            grad_self[place, :] = ref[pl.ds(base, rows), :].astype(F32) * factor
            grad_neigh[place, :] = ref[pl.ds(base + rows, rows), :].astype(F32) * factor


def shards(
    features, w_self, w_neigh, bias_vector, cotangent, adj_values, src_slots, dst_slots, slot_counts
):
    block_rows, width = features.shape
    blocks, replicas = lax.axis_size("row"), lax.axis_size("rep")
    sections = blocks // replicas
    share = block_rows // replicas
    slot_total, size = adj_values.shape[2], adj_values.shape[-1]
    norm = 1.0 / math.sqrt(slot_total * replicas / (block_rows // size))
    factor = 1.0 / math.sqrt(block_rows * blocks)
    parts = min(blocks, width // 16)
    rows = width // parts

    across = [
        ((q * sections + s) * replicas + c, (c * sections + s) * replicas + q)
        for q in range(replicas)
        for s in range(sections)
        for c in range(replicas)
    ]
    offset = lax.axis_index("rep") * share
    pair = jnp.concatenate(
        [
            lax.dynamic_slice_in_dim(features, offset, share, 0),
            lax.dynamic_slice_in_dim(cotangent, offset, share, 0),
        ]
    )
    pair = lax.ppermute(pair, ("row", "rep"), across)

    plane_rows = sections * block_rows
    dense, own, *sent = call(
        functools.partial(first_kernel, sections),
        [shape((block_rows, plane_rows), BF16), shape((block_rows, width), F32)]
        + [shape((block_rows, width), BF16)] * (sections - 1),
        [SMEM] * 3 + [VMEM] * 2,
        [pltpu.VMEM((plane_rows, width), F32)],
    )(src_slots, dst_slots, slot_counts, adj_values, features)
    received = [swap(value, k) for k, value in enumerate(sent, 1)]

    own, *sent = call(
        functools.partial(block_kernel, sections),
        [shape((share, width), F32)] + [shape((share, width), BF16)] * (replicas - 1),
        [VMEM] * sections,
        [pltpu.VMEM((block_rows, width), F32)],
    )(own, *received)
    received = [swap(value, k * sections) for k, value in enumerate(sent, 1)]

    act, *letters = call(
        functools.partial(middle_kernel, norm, sections, replicas, parts),
        [shape((share, width), BF16)]
        + [shape((share + sections * rows, width), BF16)] * replicas,
        [VMEM] * (replicas + 4),
        [pltpu.VMEM((width, share), BF16)] * 2,
    )(own, *received, pair, w_self, w_neigh, bias_vector[None, :])
    letters = letters[:1] + [swap(v, k * sections) for k, v in enumerate(letters[1:], 1)]
    activations = lax.ppermute(act, ("row", "rep"), across)

    packs = call(
        functools.partial(pack_kernel, sections, share, rows),
        [shape((replicas * (share + rows), width), BF16)] * sections,
        [VMEM] * replicas,
    )(*letters)
    packs = packs[:1] + [swap(value, k) for k, value in enumerate(packs[1:], 1)]

    sent = call(
        functools.partial(back_kernel, norm, sections, replicas, rows),
        [shape((share + 2 * rows + 16, width), BF16)] * replicas,
        [VMEM] * (sections + 3),
        [
            pltpu.VMEM((blocks * (share + rows), width), BF16),
            pltpu.VMEM((plane_rows, width), BF16),
            pltpu.VMEM((block_rows, width), F32),
        ],
    )(*packs, dense, w_self, w_neigh)
    received = sent[:1] + [swap_rep(value, k) for k, value in enumerate(sent[1:], 1)]

    grad_features, grad_bias, summed = call(
        functools.partial(level_kernel, rows, factor),
        [
            shape((share, width), BF16),
            shape((1, width), F32),
            shape((2 * rows, width), BF16),
        ],
        [VMEM] * replicas,
    )(*received)
    spread = parts // sections
    pieces = [summed] + [swap(summed, k * sections) for k in range(1, spread)]
    (joined,) = call(
        functools.partial(join_kernel, sections),
        [shape((spread * 2 * rows, width), BF16)],
        [VMEM] * spread,
    )(*pieces)
    joined = [joined] + [swap(joined, k) for k in range(1, sections)]
    grad_self, grad_neigh = call(
        functools.partial(collect_kernel, rows, factor),
        [shape((width, width), F32)] * 2,
        [VMEM] * sections,
    )(*joined)
    return activations, grad_features, grad_self, grad_neigh, grad_bias[0]


def solution(mesh):
    placed = (
        P("row", None),
        P(),
        P(),
        P(),
        P("row", None),
        P("row", "rep", None, None, None),
        P("row", "rep", None),
        P("row", "rep", None),
        P("row", "rep"),
    )
    return jax.shard_map(
        shards,
        mesh=mesh,
        in_specs=placed,
        out_specs=(P(("row", "rep"), None), P(("row", "rep"), None), P(), P(), P()),
        check_vma=False,
    )
```

```python
import functools
import math

import jax
import jax.numpy as jnp
from jax import lax
from jax.experimental import pallas as pl
from jax.experimental.pallas import tpu as pltpu
from jax.sharding import PartitionSpec as P

F32 = jnp.float32
BF16 = jnp.bfloat16
VMEM = pl.BlockSpec(memory_space=pltpu.VMEM)
SMEM = pl.BlockSpec(memory_space=pltpu.SMEM)
LIMIT = 16 * 1024 * 1024


def call(body, outs, ins, scratch=(), flops=0):
    size = sum(math.prod(out.shape) * out.dtype.itemsize for out in outs)
    kernel = pl.pallas_call(
        body,
        out_shape=outs,
        in_specs=ins,
        out_specs=[VMEM] * len(outs),
        scratch_shapes=list(scratch),
        compiler_params=pltpu.CompilerParams(vmem_limit_bytes=LIMIT),
        cost_estimate=pl.CostEstimate(flops=flops, bytes_accessed=2 * size, transcendentals=0),
    )
    return lambda *operands: list(kernel(*operands))


def shape(dims, kind):
    return jax.ShapeDtypeStruct(tuple(dims), kind)


def swap(value, step):
    return lax.ppermute(value, "row", [(i, i ^ step) for i in range(lax.axis_size("row"))])


def swap_rep(value, step):
    return lax.ppermute(value, "rep", [(i, i ^ step) for i in range(lax.axis_size("rep"))])


def contract(left, right, left_dim, right_dim):
    return lax.dot_general(
        left, right, (((left_dim,), (right_dim,)), ((), ())), preferred_element_type=F32
    )


def tree_sum(parts):
    while len(parts) > 1:
        parts = [parts[i] + parts[i + 1] for i in range(0, len(parts), 2)]
    return parts[0]


def place_of(sections):
    me = lax.axis_index("row")
    return me // sections, me % sections


def piece_of(ref, index, span):
    return ref[pl.ds(pl.multiple_of(index * span, span), span), :]


def first_kernel(sections, src, dst, count, tiles, field, dense, own, *rest):
    others, total = rest[:-1], rest[-1]
    size = tiles.shape[-1]
    block_rows = field.shape[0]
    _, s = place_of(sections)
    dense[...] = jnp.zeros_like(dense)

    def place(e, carry):
        row = pl.multiple_of(dst[0, 0, e] * size, size)
        col = pl.multiple_of(src[0, 0, e] * size, size)
        dense[pl.ds(row, size), pl.ds(col, size)] = tiles[0, 0, e]
        return carry

    lax.fori_loop(0, count[0, 0], place, 0)
    for t in range(dense.shape[1] // size):
        cols = pl.ds(t * size, size)
        total[cols, :] = contract(dense[:, cols], field[...], 0, 0)
    own[...] = piece_of(total, s, block_rows)
    for k, out in enumerate(others, 1):
        out[...] = piece_of(total, s ^ k, block_rows).astype(BF16)


def block_kernel(sections, *refs):
    parts, own, others, total = refs[:sections], refs[sections], refs[sections + 1 : -1], refs[-1]
    share = own.shape[0]
    q, _ = place_of(sections)
    value = parts[0][...]
    for ref in parts[1:]:
        value = value + ref[...].astype(F32)
    total[...] = value
    own[...] = piece_of(total, q, share)
    for k, out in enumerate(others, 1):
        out[...] = piece_of(total, q ^ k, share).astype(BF16)


def middle_kernel(norm, sections, replicas, parts, *refs):
    tiles, (pair, w_self, w_neigh, bias, act) = refs[:replicas], refs[replicas : replicas + 5]
    letters, (turned_f, turned_a) = refs[replicas + 5 : -2], refs[-2:]
    share, width = act.shape
    rows = width // parts
    q, _ = place_of(sections)
    total = tiles[0][...]
    for ref in tiles[1:]:
        total = total + ref[...].astype(F32)
    aggregate = (total * norm).astype(BF16)
    field = pair[pl.ds(0, share), :]
    pre = contract(field, w_self[...], 1, 0) + contract(aggregate, w_neigh[...], 1, 0)
    pre = pre + bias[...]
    slope = jnp.exp(jnp.minimum(pre, 0.0))
    act[...] = jnp.where(pre > 0.0, pre, slope - 1.0).astype(BF16)
    grad = (pair[pl.ds(share, share), :].astype(F32) * slope).astype(BF16)
    turned_f[...] = field.T
    turned_a[...] = aggregate.T
    span = sections * rows
    for k, letter in enumerate(letters):
        slot = (q ^ k) % (parts // sections)
        letter[pl.ds(0, share), :] = grad
        letter[pl.ds(share, span), pl.ds(0, share)] = piece_of(turned_f, slot, span)
        letter[pl.ds(share, span), pl.ds(128, share)] = piece_of(turned_a, slot, span)


def pack_kernel(sections, share, rows, *refs):
    letters, packs = refs[:-sections], refs[-sections:]
    q, s = place_of(sections)
    block_rows = len(letters) * share
    for k, letter in enumerate(letters):
        here = pl.ds(pl.multiple_of((q ^ k) * share, share), share)
        turned = pl.ds(pl.multiple_of(block_rows + (q ^ k) * rows, rows), rows)
        for m, pack in enumerate(packs):
            first = pl.multiple_of(share + (s ^ m) * rows, 16)
            pack[here, :] = letter[pl.ds(0, share), :]
            pack[turned, :] = letter[pl.ds(first, rows), :]


def terms_kernel(share, rows, *refs):
    packs, out = refs[:-1], refs[-1]
    width = out.shape[1]
    replicas = packs[0].shape[0] // (share + rows)
    ones = jnp.ones((16, share), BF16)
    sums = []
    for pack in packs:
        total = jnp.zeros((2 * rows + 16, width), F32)
        for i in range(replicas):
            turned = pl.ds(replicas * share + i * rows, rows)
            field, aggregate = pack[turned, pl.ds(0, share)], pack[turned, pl.ds(128, share)]
            left = jnp.concatenate([field, aggregate, ones])
            total += contract(left, pack[pl.ds(i * share, share), :], 1, 0)
        sums.append(total)
    total = tree_sum(sums)
    tail = total[2 * rows :]
    high = tail.astype(BF16).astype(F32)
    line = lax.broadcasted_iota(jnp.int32, tail.shape, 0)
    out[pl.ds(0, 2 * rows), :] = total[: 2 * rows].astype(BF16)
    out[pl.ds(2 * rows, 16), :] = jnp.where(line == 0, high, tail - high).astype(BF16)


def back_kernel(norm, sections, replicas, *refs):
    packs, (dense, w_self, w_neigh) = refs[:sections], refs[sections : sections + 3]
    outs, (message, total) = refs[sections + 3 : -2], refs[-2:]
    me_rep = lax.axis_index("rep")
    q, s = place_of(sections)
    block_rows = dense.shape[0]
    share = block_rows // replicas
    for k, pack in enumerate(packs):
        here = pl.ds(pl.multiple_of((s ^ k) * block_rows, block_rows), block_rows)
        grad = pack[pl.ds(0, block_rows), :]
        message[here, :] = contract(grad, w_neigh[...], 1, 1).astype(BF16)
    total[...] = contract(dense[...], message[...], 1, 0) * norm

    @pl.when(me_rep == q)
    def _():
        total[...] += contract(packs[0][pl.ds(0, block_rows), :], w_self[...], 1, 1)

    for k, out in enumerate(outs):
        out[...] = piece_of(total, me_rep ^ k, share).astype(BF16)


def level_kernel(rows, factor, *refs):
    parts, (bias, summed) = refs[:-2], refs[-2:]
    terms = tree_sum([ref[...].astype(F32) for ref in parts])
    tail = terms[2 * rows : 2 * rows + 8]
    bias[...] = (tail[0:1] + tail[1:2]) * factor
    summed[...] = terms[: 2 * rows].astype(BF16)


def last_kernel(*refs):
    parts, (act, grad_features, activations) = refs[:-3], refs[-3:]
    grad_features[...] = tree_sum([ref[...].astype(F32) for ref in parts]).astype(BF16)
    activations[...] = act[...]


def join_kernel(sections, *refs):
    pieces, out = refs[:-1], refs[-1]
    span = pieces[0].shape[0]
    q, _ = place_of(sections)
    for k, piece in enumerate(pieces):
        slot = (q % len(pieces)) ^ k
        out[pl.ds(pl.multiple_of(slot * span, 16), span), :] = piece[...]


def collect_kernel(rows, factor, *refs):
    joined, (grad_self, grad_neigh) = refs[:-2], refs[-2:]
    sections = len(joined)
    _, s = place_of(sections)
    for k, ref in enumerate(joined):
        for j in range(ref.shape[0] // (2 * rows)):
            place = pl.ds(pl.multiple_of((j * sections + (s ^ k)) * rows, rows), rows)
            base = j * 2 * rows
            grad_self[place, :] = ref[pl.ds(base, rows), :].astype(F32) * factor
            grad_neigh[place, :] = ref[pl.ds(base + rows, rows), :].astype(F32) * factor


def shards(
    features, w_self, w_neigh, bias_vector, cotangent, adj_values, src_slots, dst_slots, slot_counts
):
    block_rows, width = features.shape
    blocks, replicas = lax.axis_size("row"), lax.axis_size("rep")
    sections = blocks // replicas
    share = block_rows // replicas
    slot_total, size = adj_values.shape[2], adj_values.shape[-1]
    norm = 1.0 / math.sqrt(slot_total * replicas / (block_rows // size))
    factor = 1.0 / math.sqrt(block_rows * blocks)
    parts = min(blocks, width // 16)
    rows = width // parts

    across = [
        ((q * sections + s) * replicas + c, (c * sections + s) * replicas + q)
        for q in range(replicas)
        for s in range(sections)
        for c in range(replicas)
    ]
    offset = lax.axis_index("rep") * share
    pair = jnp.concatenate(
        [
            lax.dynamic_slice_in_dim(features, offset, share, 0),
            lax.dynamic_slice_in_dim(cotangent, offset, share, 0),
        ]
    )
    features, pair = lax.optimization_barrier((features, pair))
    pair = lax.ppermute(pair, ("row", "rep"), across)

    plane_rows = sections * block_rows
    dense, own, *sent = call(
        functools.partial(first_kernel, sections),
        [shape((block_rows, plane_rows), BF16), shape((block_rows, width), F32)]
        + [shape((block_rows, width), BF16)] * (sections - 1),
        [SMEM] * 3 + [VMEM] * 2,
        [pltpu.VMEM((plane_rows, width), F32)],
        flops=2 * plane_rows * block_rows * width,
    )(src_slots, dst_slots, slot_counts, adj_values, features)
    received = [swap(value, k) for k, value in enumerate(sent, 1)]
    pair, *received = lax.optimization_barrier((pair, *received))

    own, *sent = call(
        functools.partial(block_kernel, sections),
        [shape((share, width), F32)] + [shape((share, width), BF16)] * (replicas - 1),
        [VMEM] * sections,
        [pltpu.VMEM((block_rows, width), F32)],
    )(own, *received)
    received = [swap(value, k * sections) for k, value in enumerate(sent, 1)]

    act, *letters = call(
        functools.partial(middle_kernel, norm, sections, replicas, parts),
        [shape((share, width), BF16)]
        + [shape((share + sections * rows, width), BF16)] * replicas,
        [VMEM] * (replicas + 4),
        [pltpu.VMEM((width, share), BF16)] * 2,
    )(own, *received, pair, w_self, w_neigh, bias_vector[None, :])
    letters = letters[:1] + [swap(v, k * sections) for k, v in enumerate(letters[1:], 1)]
    act = lax.ppermute(act, ("row", "rep"), across)

    packs = call(
        functools.partial(pack_kernel, sections, share, rows),
        [shape((replicas * (share + rows), width), BF16)] * sections,
        [VMEM] * replicas,
    )(*letters)
    packs = packs[:1] + [swap(value, k) for k, value in enumerate(packs[1:], 1)]
    act, *packs = lax.optimization_barrier((act, *packs))

    (terms,) = call(
        functools.partial(terms_kernel, share, rows),
        [shape((2 * rows + 16, width), BF16)],
        [VMEM] * sections,
        flops=2 * plane_rows * width * (2 * rows + 16),
    )(*packs)
    terms = [terms] + [swap_rep(terms, k) for k in range(1, replicas)]

    sent = call(
        functools.partial(back_kernel, norm, sections, replicas),
        [shape((share, width), BF16)] * replicas,
        [VMEM] * (sections + 3),
        [pltpu.VMEM((plane_rows, width), BF16), pltpu.VMEM((block_rows, width), F32)],
        flops=2 * plane_rows * width * (block_rows + width),
    )(*packs, dense, w_self, w_neigh)
    received = sent[:1] + [swap_rep(value, k) for k, value in enumerate(sent[1:], 1)]
    *terms, _ = lax.optimization_barrier((*terms, sent[0]))

    grad_bias, summed = call(
        functools.partial(level_kernel, rows, factor),
        [shape((1, width), F32), shape((2 * rows, width), BF16)],
        [VMEM] * replicas,
    )(*terms)
    spread = parts // sections
    pieces = [summed] + [swap(summed, k * sections) for k in range(1, spread)]
    count = len(pieces)
    together = lax.optimization_barrier((*pieces, *received))
    pieces, received = together[:count], together[count:]
    (joined,) = call(
        functools.partial(join_kernel, sections),
        [shape((spread * 2 * rows, width), BF16)],
        [VMEM] * spread,
    )(*pieces)
    joined = [joined] + [swap(joined, k) for k in range(1, sections)]
    grad_self, grad_neigh = call(
        functools.partial(collect_kernel, rows, factor),
        [shape((width, width), F32)] * 2,
        [VMEM] * sections,
    )(*joined)
    grad_features, activations = call(
        last_kernel, [shape((share, width), BF16)] * 2, [VMEM] * (replicas + 1)
    )(*received, act)
    return activations, grad_features, grad_self, grad_neigh, grad_bias[0]


def solution(mesh):
    placed = (
        P("row", None),
        P(),
        P(),
        P(),
        P("row", None),
        P("row", "rep", None, None, None),
        P("row", "rep", None),
        P("row", "rep", None),
        P("row", "rep"),
    )
    return jax.shard_map(
        shards,
        mesh=mesh,
        in_specs=placed,
        out_specs=(P(("row", "rep"), None), P(("row", "rep"), None), P(), P(), P()),
        check_vma=False,
    )
```

```python
import functools
import math

import jax
import jax.numpy as jnp
from jax import lax
from jax.experimental import pallas as pl
from jax.experimental.pallas import tpu as pltpu
from jax.sharding import PartitionSpec as P

F32 = jnp.float32
BF16 = jnp.bfloat16
VMEM = pl.BlockSpec(memory_space=pltpu.VMEM)
HBM = pl.BlockSpec(memory_space=pltpu.HBM)
SMEM = pl.BlockSpec(memory_space=pltpu.SMEM)
LIMIT = 16 * 1024 * 1024


def call(body, outs, ins, scratch=(), flops=0):
    size = sum(math.prod(out.shape) * out.dtype.itemsize for out in outs)
    kernel = pl.pallas_call(
        body,
        out_shape=outs,
        in_specs=ins,
        out_specs=[VMEM] * len(outs),
        scratch_shapes=list(scratch),
        compiler_params=pltpu.CompilerParams(vmem_limit_bytes=LIMIT),
        cost_estimate=pl.CostEstimate(flops=flops, bytes_accessed=2 * size, transcendentals=0),
    )
    return lambda *operands: list(kernel(*operands))


def shape(dims, kind):
    return jax.ShapeDtypeStruct(tuple(dims), kind)


def swap(value, step):
    return lax.ppermute(value, "row", [(i, i ^ step) for i in range(lax.axis_size("row"))])


def swap_rep(value, step):
    return lax.ppermute(value, "rep", [(i, i ^ step) for i in range(lax.axis_size("rep"))])


def contract(left, right, left_dim, right_dim):
    return lax.dot_general(
        left, right, (((left_dim,), (right_dim,)), ((), ())), preferred_element_type=F32
    )


def tree_sum(parts):
    while len(parts) > 1:
        parts = [parts[i] + parts[i + 1] for i in range(0, len(parts), 2)]
    return parts[0]


def place_of(sections):
    me = lax.axis_index("row")
    return me // sections, me % sections


def turn(c, replicas):
    out, bits = 0, replicas.bit_length() - 1
    for i in range(bits):
        out = out | ((c >> i) & 1) << (bits - 1 - i)
    return out


def tile_of(sections, replicas):
    return place_of(sections)[0] ^ turn(lax.axis_index("rep"), replicas)


def piece_of(ref, index, span):
    return ref[pl.ds(pl.multiple_of(index * span, span), span), :]


def first_kernel(sections, src, dst, count, tiles, field, cotangent, dense, pair, own, *rest):
    others, (total, held, sems) = rest[:-3], rest[-3:]
    size = tiles.shape[-1]
    block_rows = field.shape[0]
    share = pair.shape[0] // 2
    _, s = place_of(sections)
    live = count[0, 0]
    offset = pl.multiple_of(lax.axis_index("rep") * share, share)
    field_copy = pltpu.make_async_copy(field, held, sems.at[0])
    field_copy.start()
    cotangent_copy = pltpu.make_async_copy(
        cotangent.at[pl.ds(offset, share), :], pair.at[pl.ds(share, share), :], sems.at[1]
    )
    cotangent_copy.start()
    dense[...] = jnp.zeros_like(dense)

    def tile_copy(e):
        row = pl.multiple_of(dst[0, 0, e] * size, size)
        col = pl.multiple_of(src[0, 0, e] * size, size)
        target = dense.at[pl.ds(row, size), pl.ds(col, size)]
        return pltpu.make_async_copy(tiles.at[0, 0, e], target, sems.at[e + 2])

    lax.fori_loop(0, live, lambda e, carry: (tile_copy(e).start(), carry)[1], 0)
    field_copy.wait()
    pair[pl.ds(0, share), :] = held[pl.ds(offset, share), :]
    lax.fori_loop(0, live, lambda e, carry: (tile_copy(e).wait(), carry)[1], 0)
    for t in range(dense.shape[1] // size):
        cols = pl.ds(t * size, size)
        total[cols, :] = contract(dense[:, cols], held[...], 0, 0)
    own[...] = piece_of(total, s, block_rows)
    for k, out in enumerate(others, 1):
        out[...] = piece_of(total, s ^ k, block_rows).astype(BF16)
    cotangent_copy.wait()


def block_kernel(sections, *refs):
    parts, own, others, total = refs[:sections], refs[sections], refs[sections + 1 : -1], refs[-1]
    share = own.shape[0]
    tile = tile_of(sections, len(others) + 1)
    value = parts[0][...]
    for ref in parts[1:]:
        value = value + ref[...].astype(F32)
    total[...] = value
    own[...] = piece_of(total, tile, share)
    for k, out in enumerate(others, 1):
        out[...] = piece_of(total, tile ^ k, share).astype(BF16)


def middle_kernel(norm, sections, replicas, parts, *refs):
    tiles, (pair, w_self, w_neigh, bias, act) = refs[:replicas], refs[replicas : replicas + 5]
    letters, (turned_f, turned_a) = refs[replicas + 5 : -2], refs[-2:]
    share, width = act.shape
    rows = width // parts
    q, _ = place_of(sections)
    total = tiles[0][...]
    for ref in tiles[1:]:
        total = total + ref[...].astype(F32)
    aggregate = (total * norm).astype(BF16)
    field = pair[pl.ds(0, share), :]
    pre = contract(field, w_self[...], 1, 0) + contract(aggregate, w_neigh[...], 1, 0)
    pre = pre + bias[...]
    slope = jnp.exp(jnp.minimum(pre, 0.0))
    act[...] = jnp.where(pre > 0.0, pre, slope - 1.0).astype(BF16)
    grad = (pair[pl.ds(share, share), :].astype(F32) * slope).astype(BF16)
    turned_f[...] = field.T
    turned_a[...] = aggregate.T
    span = sections * rows
    for k, letter in enumerate(letters):
        slot = (q ^ k) % (parts // sections)
        letter[pl.ds(0, share), :] = grad
        letter[pl.ds(share, span), pl.ds(0, share)] = piece_of(turned_f, slot, span)
        letter[pl.ds(share, span), pl.ds(128, share)] = piece_of(turned_a, slot, span)


def pack_kernel(sections, share, rows, *refs):
    letters, packs = refs[:-sections], refs[-sections:]
    _, s = place_of(sections)
    tile = tile_of(sections, len(letters))
    block_rows = len(letters) * share
    for k, letter in enumerate(letters):
        here = pl.ds(pl.multiple_of((tile ^ k) * share, share), share)
        turned = pl.ds(pl.multiple_of(block_rows + (tile ^ k) * rows, rows), rows)
        for m, pack in enumerate(packs):
            first = pl.multiple_of(share + (s ^ m) * rows, 16)
            pack[here, :] = letter[pl.ds(0, share), :]
            pack[turned, :] = letter[pl.ds(first, rows), :]


def terms_kernel(share, rows, *refs):
    packs, out = refs[:-1], refs[-1]
    width = out.shape[1]
    replicas = packs[0].shape[0] // (share + rows)
    ones = jnp.ones((16, share), BF16)
    sums = []
    for pack in packs:
        total = jnp.zeros((2 * rows + 16, width), F32)
        for i in range(replicas):
            turned = pl.ds(replicas * share + i * rows, rows)
            field, aggregate = pack[turned, pl.ds(0, share)], pack[turned, pl.ds(128, share)]
            left = jnp.concatenate([field, aggregate, ones])
            total += contract(left, pack[pl.ds(i * share, share), :], 1, 0)
        sums.append(total)
    total = tree_sum(sums)
    tail = total[2 * rows :]
    high = tail.astype(BF16).astype(F32)
    line = lax.broadcasted_iota(jnp.int32, tail.shape, 0)
    out[pl.ds(0, 2 * rows), :] = total[: 2 * rows].astype(BF16)
    out[pl.ds(2 * rows, 16), :] = jnp.where(line == 0, high, tail - high).astype(BF16)


def back_kernel(norm, sections, replicas, *refs):
    packs, (dense, w_self, w_neigh) = refs[:sections], refs[sections : sections + 3]
    outs, (message, total) = refs[sections + 3 : -2], refs[-2:]
    me_rep = lax.axis_index("rep")
    q, s = place_of(sections)
    block_rows = dense.shape[0]
    share = block_rows // replicas
    for k, pack in enumerate(packs):
        here = pl.ds(pl.multiple_of((s ^ k) * block_rows, block_rows), block_rows)
        grad = pack[pl.ds(0, block_rows), :]
        message[here, :] = contract(grad, w_neigh[...], 1, 1).astype(BF16)
    total[...] = contract(dense[...], message[...], 1, 0) * norm

    @pl.when(me_rep == q)
    def _():
        total[...] += contract(packs[0][pl.ds(0, block_rows), :], w_self[...], 1, 1)

    for k, out in enumerate(outs):
        out[...] = piece_of(total, me_rep ^ k, share).astype(BF16)


def level_kernel(rows, factor, *refs):
    parts, (bias, summed) = refs[:-2], refs[-2:]
    terms = tree_sum([ref[...].astype(F32) for ref in parts])
    tail = terms[2 * rows : 2 * rows + 8]
    bias[...] = (tail[0:1] + tail[1:2]) * factor
    summed[...] = terms[: 2 * rows].astype(BF16)


def last_kernel(*refs):
    parts, (act, grad_features, activations) = refs[:-3], refs[-3:]
    grad_features[...] = tree_sum([ref[...].astype(F32) for ref in parts]).astype(BF16)
    activations[...] = act[...]


def join_kernel(sections, *refs):
    pieces, out = refs[:-1], refs[-1]
    span = pieces[0].shape[0]
    q, _ = place_of(sections)
    for k, piece in enumerate(pieces):
        slot = (q % len(pieces)) ^ k
        out[pl.ds(pl.multiple_of(slot * span, 16), span), :] = piece[...]


def collect_kernel(rows, factor, *refs):
    joined, (grad_self, grad_neigh) = refs[:-2], refs[-2:]
    sections = len(joined)
    _, s = place_of(sections)
    for k, ref in enumerate(joined):
        for j in range(ref.shape[0] // (2 * rows)):
            place = pl.ds(pl.multiple_of((j * sections + (s ^ k)) * rows, rows), rows)
            base = j * 2 * rows
            grad_self[place, :] = ref[pl.ds(base, rows), :].astype(F32) * factor
            grad_neigh[place, :] = ref[pl.ds(base + rows, rows), :].astype(F32) * factor


def shards(
    features, w_self, w_neigh, bias_vector, cotangent, adj_values, src_slots, dst_slots, slot_counts
):
    block_rows, width = features.shape
    blocks, replicas = lax.axis_size("row"), lax.axis_size("rep")
    sections = blocks // replicas
    share = block_rows // replicas
    slot_total, size = adj_values.shape[2], adj_values.shape[-1]
    norm = 1.0 / math.sqrt(slot_total * replicas / (block_rows // size))
    factor = 1.0 / math.sqrt(block_rows * blocks)
    parts = min(blocks, width // 16)
    rows = width // parts

    def flat(q, s, c):
        return (q * sections + s) * replicas + c

    places = [
        (q, s, c) for q in range(replicas) for s in range(sections) for c in range(replicas)
    ]
    here = [flat(q, s, c) for q, s, c in places]
    level = [flat(q, s, q ^ turn(c, replicas)) for q, s, c in places]
    home = [flat(c, s, q ^ turn(c, replicas)) for q, s, c in places]

    plane_rows = sections * block_rows
    dense, pair, own, *sent = call(
        functools.partial(first_kernel, sections),
        [
            shape((block_rows, plane_rows), BF16),
            shape((2 * share, width), BF16),
            shape((block_rows, width), F32),
        ]
        + [shape((block_rows, width), BF16)] * (sections - 1),
        [SMEM] * 3 + [HBM] * 3,
        [
            pltpu.VMEM((plane_rows, width), F32),
            pltpu.VMEM((block_rows, width), BF16),
            pltpu.SemaphoreType.DMA((slot_total + 2,)),
        ],
        flops=2 * plane_rows * block_rows * width,
    )(src_slots, dst_slots, slot_counts, adj_values, features, cotangent)
    pair = lax.ppermute(pair, ("row", "rep"), list(zip(home, here)))
    received = [swap(value, k) for k, value in enumerate(sent, 1)]

    own, *sent = call(
        functools.partial(block_kernel, sections),
        [shape((share, width), F32)] + [shape((share, width), BF16)] * (replicas - 1),
        [VMEM] * sections,
        [pltpu.VMEM((block_rows, width), F32)],
    )(own, *received)
    received = [swap(value, k * sections) for k, value in enumerate(sent, 1)]

    act, *letters = call(
        functools.partial(middle_kernel, norm, sections, replicas, parts),
        [shape((share, width), BF16)]
        + [shape((share + sections * rows, width), BF16)] * replicas,
        [VMEM] * (replicas + 4),
        [pltpu.VMEM((width, share), BF16)] * 2,
    )(own, *received, pair, w_self, w_neigh, bias_vector[None, :])
    letters = letters[:1] + [swap(v, k * sections) for k, v in enumerate(letters[1:], 1)]
    act = lax.ppermute(act, ("row", "rep"), list(zip(here, level)))
    act, *letters = lax.optimization_barrier((act, *letters))
    act = lax.ppermute(act, ("row", "rep"), list(zip(level, home)))

    packs = call(
        functools.partial(pack_kernel, sections, share, rows),
        [shape((replicas * (share + rows), width), BF16)] * sections,
        [VMEM] * replicas,
    )(*letters)
    packs = packs[:1] + [swap(value, k) for k, value in enumerate(packs[1:], 1)]

    (terms,) = call(
        functools.partial(terms_kernel, share, rows),
        [shape((2 * rows + 16, width), BF16)],
        [VMEM] * sections,
        flops=2 * plane_rows * width * (2 * rows + 16),
    )(*packs)
    terms = [terms] + [swap_rep(terms, k) for k in range(1, replicas)]

    sent = call(
        functools.partial(back_kernel, norm, sections, replicas),
        [shape((share, width), BF16)] * replicas,
        [VMEM] * (sections + 3),
        [pltpu.VMEM((plane_rows, width), BF16), pltpu.VMEM((block_rows, width), F32)],
        flops=2 * plane_rows * width * (block_rows + width),
    )(*packs, dense, w_self, w_neigh)
    together = lax.optimization_barrier((*terms, act, *sent))
    terms, act, sent = together[:replicas], together[replicas], together[replicas + 1 :]
    received = [sent[0]] + [swap_rep(value, k) for k, value in enumerate(sent[1:], 1)]

    grad_bias, summed = call(
        functools.partial(level_kernel, rows, factor),
        [shape((1, width), F32), shape((2 * rows, width), BF16)],
        [VMEM] * replicas,
    )(*terms)
    spread = parts // sections
    pieces = [summed] + [swap(summed, k * sections) for k in range(1, spread)]
    count = len(pieces)
    together = lax.optimization_barrier((*pieces, *received))
    pieces, received = together[:count], together[count:]
    (joined,) = call(
        functools.partial(join_kernel, sections),
        [shape((spread * 2 * rows, width), BF16)],
        [VMEM] * spread,
    )(*pieces)
    joined = [joined] + [swap(joined, k) for k in range(1, sections)]
    grad_self, grad_neigh = call(
        functools.partial(collect_kernel, rows, factor),
        [shape((width, width), F32)] * 2,
        [VMEM] * sections,
    )(*joined)
    grad_features, activations = call(
        last_kernel, [shape((share, width), BF16)] * 2, [VMEM] * (replicas + 1)
    )(*received, act)
    return activations, grad_features, grad_self, grad_neigh, grad_bias[0]


def solution(mesh):
    placed = (
        P("row", None),
        P(),
        P(),
        P(),
        P("row", None),
        P("row", "rep", None, None, None),
        P("row", "rep", None),
        P("row", "rep", None),
        P("row", "rep"),
    )
    return jax.shard_map(
        shards,
        mesh=mesh,
        in_specs=placed,
        out_specs=(P(("row", "rep"), None), P(("row", "rep"), None), P(), P(), P()),
        check_vma=False,
    )
```

```python
import functools
import math

import jax
import jax.numpy as jnp
from jax import lax
from jax.experimental import pallas as pl
from jax.experimental.pallas import tpu as pltpu
from jax.sharding import PartitionSpec as P

F32 = jnp.float32
BF16 = jnp.bfloat16
VMEM = pl.BlockSpec(memory_space=pltpu.VMEM)
HBM = pl.BlockSpec(memory_space=pltpu.HBM)
SMEM = pl.BlockSpec(memory_space=pltpu.SMEM)
LIMIT = 16 * 1024 * 1024


def call(body, outs, ins, scratch=(), flops=0, limit=LIMIT):
    size = sum(math.prod(out.shape) * out.dtype.itemsize for out in outs)
    kernel = pl.pallas_call(
        body,
        out_shape=outs,
        in_specs=ins,
        out_specs=[VMEM] * len(outs),
        scratch_shapes=list(scratch),
        compiler_params=pltpu.CompilerParams(vmem_limit_bytes=limit),
        cost_estimate=pl.CostEstimate(flops=flops, bytes_accessed=2 * size, transcendentals=0),
    )
    return lambda *operands: list(kernel(*operands))


def shape(dims, kind):
    return jax.ShapeDtypeStruct(tuple(dims), kind)


def swap(value, step):
    return lax.ppermute(value, "row", [(i, i ^ step) for i in range(lax.axis_size("row"))])


def swap_rep(value, step):
    return lax.ppermute(value, "rep", [(i, i ^ step) for i in range(lax.axis_size("rep"))])


def contract(left, right, left_dim, right_dim):
    return lax.dot_general(
        left, right, (((left_dim,), (right_dim,)), ((), ())), preferred_element_type=F32
    )


def tree_sum(parts):
    while len(parts) > 1:
        parts = [parts[i] + parts[i + 1] for i in range(0, len(parts), 2)]
    return parts[0]


def place_of(sections):
    me = lax.axis_index("row")
    return me // sections, me % sections


def turn(c, replicas):
    out, bits = 0, replicas.bit_length() - 1
    for i in range(bits):
        out = out | ((c >> i) & 1) << (bits - 1 - i)
    return out


def tile_of(sections, replicas):
    return place_of(sections)[0] ^ turn(lax.axis_index("rep"), replicas)


def piece_of(ref, index, span):
    return ref[pl.ds(pl.multiple_of(index * span, span), span), :]


def first_kernel(sections, src, dst, count, tiles, field, bias, dense, bias_out, own, *rest):
    others, (total, sems) = rest[:-2], rest[-2:]
    size = tiles.shape[-1]
    block_rows = field.shape[0]
    _, s = place_of(sections)
    live = count[0, 0]
    dense[...] = jnp.zeros_like(dense)

    def tile_copy(e):
        row = pl.multiple_of(dst[0, 0, e] * size, size)
        col = pl.multiple_of(src[0, 0, e] * size, size)
        target = dense.at[pl.ds(row, size), pl.ds(col, size)]
        return pltpu.make_async_copy(tiles.at[0, 0, e], target, sems.at[e])

    lax.fori_loop(0, live, lambda e, carry: (tile_copy(e).start(), carry)[1], 0)
    bias_out[...] = bias[...]
    lax.fori_loop(0, live, lambda e, carry: (tile_copy(e).wait(), carry)[1], 0)
    for t in range(dense.shape[1] // size):
        cols = pl.ds(t * size, size)
        total[cols, :] = contract(dense[:, cols], field[...], 0, 0)
    own[...] = piece_of(total, s, block_rows)
    for k, out in enumerate(others, 1):
        out[...] = piece_of(total, s ^ k, block_rows).astype(BF16)


def block_kernel(sections, *refs):
    parts, own, others, total = refs[:sections], refs[sections], refs[sections + 1 : -1], refs[-1]
    share = own.shape[0]
    tile = tile_of(sections, len(others) + 1)
    value = parts[0][...]
    for ref in parts[1:]:
        value = value + ref[...].astype(F32)
    total[...] = value
    own[...] = piece_of(total, tile, share)
    for k, out in enumerate(others, 1):
        out[...] = piece_of(total, tile ^ k, share).astype(BF16)


def middle_kernel(norm, sections, replicas, parts, *refs):
    tiles, (pair, w_self, w_neigh, bias, act) = refs[:replicas], refs[replicas : replicas + 5]
    letters, (turned_f, turned_a) = refs[replicas + 5 : -2], refs[-2:]
    share, width = act.shape
    rows = width // parts
    q, _ = place_of(sections)
    total = tiles[0][...]
    for ref in tiles[1:]:
        total = total + ref[...].astype(F32)
    aggregate = (total * norm).astype(BF16)
    field = pair[pl.ds(0, share), :]
    pre = contract(field, w_self[...], 1, 0) + contract(aggregate, w_neigh[...], 1, 0)
    pre = pre + bias[...]
    slope = jnp.exp(jnp.minimum(pre, 0.0))
    act[...] = jnp.where(pre > 0.0, pre, slope - 1.0).astype(BF16)
    grad = (pair[pl.ds(share, share), :].astype(F32) * slope).astype(BF16)
    turned_f[...] = field.T
    turned_a[...] = aggregate.T
    span = sections * rows
    for k, letter in enumerate(letters):
        slot = (q ^ k) % (parts // sections)
        letter[pl.ds(0, share), :] = grad
        letter[pl.ds(share, span), pl.ds(0, share)] = piece_of(turned_f, slot, span)
        letter[pl.ds(share, span), pl.ds(128, share)] = piece_of(turned_a, slot, span)


def pack_kernel(sections, share, rows, *refs):
    letters, packs = refs[:-sections], refs[-sections:]
    _, s = place_of(sections)
    tile = tile_of(sections, len(letters))
    block_rows = len(letters) * share
    for k, letter in enumerate(letters):
        here = pl.ds(pl.multiple_of((tile ^ k) * share, share), share)
        turned = pl.ds(pl.multiple_of(block_rows + (tile ^ k) * rows, rows), rows)
        for m, pack in enumerate(packs):
            first = pl.multiple_of(share + (s ^ m) * rows, 16)
            pack[here, :] = letter[pl.ds(0, share), :]
            pack[turned, :] = letter[pl.ds(first, rows), :]


def terms_kernel(share, rows, *refs):
    packs, out = refs[:-1], refs[-1]
    width = out.shape[1]
    replicas = packs[0].shape[0] // (share + rows)
    ones = jnp.ones((16, share), BF16)
    sums = []
    for pack in packs:
        total = jnp.zeros((2 * rows + 16, width), F32)
        for i in range(replicas):
            turned = pl.ds(replicas * share + i * rows, rows)
            field, aggregate = pack[turned, pl.ds(0, share)], pack[turned, pl.ds(128, share)]
            left = jnp.concatenate([field, aggregate, ones])
            total += contract(left, pack[pl.ds(i * share, share), :], 1, 0)
        sums.append(total)
    total = tree_sum(sums)
    tail = total[2 * rows :]
    high = tail.astype(BF16).astype(F32)
    line = lax.broadcasted_iota(jnp.int32, tail.shape, 0)
    out[pl.ds(0, 2 * rows), :] = total[: 2 * rows].astype(BF16)
    out[pl.ds(2 * rows, 16), :] = jnp.where(line == 0, high, tail - high).astype(BF16)


def back_kernel(norm, sections, replicas, *refs):
    packs, (dense, w_self, w_neigh) = refs[:sections], refs[sections : sections + 3]
    outs, (message, total) = refs[sections + 3 : -2], refs[-2:]
    me_rep = lax.axis_index("rep")
    q, s = place_of(sections)
    block_rows = dense.shape[0]
    share = block_rows // replicas
    for k, pack in enumerate(packs):
        here = pl.ds(pl.multiple_of((s ^ k) * block_rows, block_rows), block_rows)
        grad = pack[pl.ds(0, block_rows), :]
        message[here, :] = contract(grad, w_neigh[...], 1, 1).astype(BF16)
    total[...] = contract(dense[...], message[...], 1, 0) * norm

    @pl.when(me_rep == q)
    def _():
        total[...] += contract(packs[0][pl.ds(0, block_rows), :], w_self[...], 1, 1)

    for k, out in enumerate(outs):
        out[...] = piece_of(total, me_rep ^ k, share).astype(BF16)


def level_kernel(rows, factor, *refs):
    parts, (bias, summed) = refs[:-2], refs[-2:]
    terms = tree_sum([ref[...].astype(F32) for ref in parts])
    tail = terms[2 * rows : 2 * rows + 8]
    bias[...] = (tail[0:1] + tail[1:2]) * factor
    summed[...] = terms[: 2 * rows].astype(BF16)


def last_kernel(*refs):
    parts, (act, grad_features, activations) = refs[:-3], refs[-3:]
    grad_features[...] = tree_sum([ref[...].astype(F32) for ref in parts]).astype(BF16)
    activations[...] = act[...]


def join_kernel(sections, *refs):
    pieces, out = refs[:-1], refs[-1]
    span = pieces[0].shape[0]
    q, _ = place_of(sections)
    for k, piece in enumerate(pieces):
        slot = (q % len(pieces)) ^ k
        out[pl.ds(pl.multiple_of(slot * span, 16), span), :] = piece[...]


def collect_kernel(rows, factor, *refs):
    joined, (grad_self, grad_neigh) = refs[:-2], refs[-2:]
    sections = len(joined)
    _, s = place_of(sections)
    for k, ref in enumerate(joined):
        for j in range(ref.shape[0] // (2 * rows)):
            place = pl.ds(pl.multiple_of((j * sections + (s ^ k)) * rows, rows), rows)
            base = j * 2 * rows
            grad_self[place, :] = ref[pl.ds(base, rows), :].astype(F32) * factor
            grad_neigh[place, :] = ref[pl.ds(base + rows, rows), :].astype(F32) * factor


def shards(
    features, w_self, w_neigh, bias_vector, cotangent, adj_values, src_slots, dst_slots, slot_counts
):
    block_rows, width = features.shape
    blocks, replicas = lax.axis_size("row"), lax.axis_size("rep")
    sections = blocks // replicas
    share = block_rows // replicas
    slot_total, size = adj_values.shape[2], adj_values.shape[-1]
    norm = 1.0 / math.sqrt(slot_total * replicas / (block_rows // size))
    factor = 1.0 / math.sqrt(block_rows * blocks)
    parts = min(blocks, width // 16)
    rows = width // parts

    def flat(q, s, c):
        return (q * sections + s) * replicas + c

    places = [
        (q, s, c) for q in range(replicas) for s in range(sections) for c in range(replicas)
    ]
    here = [flat(q, s, c) for q, s, c in places]
    level = [flat(q, s, q ^ turn(c, replicas)) for q, s, c in places]
    home = [flat(c, s, q ^ turn(c, replicas)) for q, s, c in places]

    plane_rows = sections * block_rows
    offset = lax.axis_index("rep") * share
    pair = jnp.concatenate(
        [
            lax.dynamic_slice_in_dim(features, offset, share, 0),
            lax.dynamic_slice_in_dim(cotangent, offset, share, 0),
        ]
    )
    features, pair = lax.optimization_barrier((features, pair))
    pair = lax.ppermute(pair, ("row", "rep"), list(zip(home, here)))
    dense, bias, own, *sent = call(
        functools.partial(first_kernel, sections),
        [
            shape((block_rows, plane_rows), BF16),
            shape((1, width), F32),
            shape((block_rows, width), F32),
        ]
        + [shape((block_rows, width), BF16)] * (sections - 1),
        [SMEM] * 3 + [HBM, VMEM, VMEM],
        [
            pltpu.VMEM((plane_rows, width), F32),
            pltpu.SemaphoreType.DMA((slot_total,)),
        ],
        flops=2 * plane_rows * block_rows * width,
        limit=51 * 1024 * 1024,
    )(src_slots, dst_slots, slot_counts, adj_values, features, bias_vector[None, :])
    pair, *sent = lax.optimization_barrier((pair, *sent))
    received = [swap(value, k) for k, value in enumerate(sent, 1)]

    own, *sent = call(
        functools.partial(block_kernel, sections),
        [shape((share, width), F32)] + [shape((share, width), BF16)] * (replicas - 1),
        [VMEM] * sections,
        [pltpu.VMEM((block_rows, width), F32)],
    )(own, *received)
    received = [swap(value, k * sections) for k, value in enumerate(sent, 1)]

    act, *letters = call(
        functools.partial(middle_kernel, norm, sections, replicas, parts),
        [shape((share, width), BF16)]
        + [shape((share + sections * rows, width), BF16)] * replicas,
        [VMEM] * (replicas + 4),
        [pltpu.VMEM((width, share), BF16)] * 2,
    )(own, *received, pair, w_self, w_neigh, bias)
    letters = letters[:1] + [swap(v, k * sections) for k, v in enumerate(letters[1:], 1)]
    act = lax.ppermute(act, ("row", "rep"), list(zip(here, level)))

    packs = call(
        functools.partial(pack_kernel, sections, share, rows),
        [shape((replicas * (share + rows), width), BF16)] * sections,
        [VMEM] * replicas,
    )(*letters)
    packs = packs[:1] + [swap(value, k) for k, value in enumerate(packs[1:], 1)]
    act, *packs = lax.optimization_barrier((act, *packs))
    act = lax.ppermute(act, ("row", "rep"), list(zip(level, home)))

    (terms,) = call(
        functools.partial(terms_kernel, share, rows),
        [shape((2 * rows + 16, width), BF16)],
        [VMEM] * sections,
        flops=2 * plane_rows * width * (2 * rows + 16),
    )(*packs)
    terms = [terms] + [swap_rep(terms, k) for k in range(1, replicas)]

    sent = call(
        functools.partial(back_kernel, norm, sections, replicas),
        [shape((share, width), BF16)] * replicas,
        [VMEM] * (sections + 3),
        [pltpu.VMEM((plane_rows, width), BF16), pltpu.VMEM((block_rows, width), F32)],
        flops=2 * plane_rows * width * (block_rows + width),
    )(*packs, dense, w_self, w_neigh)
    received = sent[:1] + [swap_rep(value, k) for k, value in enumerate(sent[1:], 1)]
    act, *terms = lax.optimization_barrier((act, sent[0], *terms))
    terms = terms[1:]

    grad_bias, summed = call(
        functools.partial(level_kernel, rows, factor),
        [shape((1, width), F32), shape((2 * rows, width), BF16)],
        [VMEM] * replicas,
    )(*terms)
    spread = parts // sections
    pieces = [summed] + [swap(summed, k * sections) for k in range(1, spread)]
    count = len(pieces)
    together = lax.optimization_barrier((*pieces, *received))
    pieces, received = together[:count], together[count:]
    (joined,) = call(
        functools.partial(join_kernel, sections),
        [shape((spread * 2 * rows, width), BF16)],
        [VMEM] * spread,
    )(*pieces)
    joined = [joined] + [swap(joined, k) for k in range(1, sections)]
    grad_self, grad_neigh = call(
        functools.partial(collect_kernel, rows, factor),
        [shape((width, width), F32)] * 2,
        [VMEM] * sections,
    )(*joined)
    grad_features, activations = call(
        last_kernel, [shape((share, width), BF16)] * 2, [VMEM] * (replicas + 1)
    )(*received, act)
    return activations, grad_features, grad_self, grad_neigh, grad_bias[0]


def solution(mesh):
    placed = (
        P("row", None),
        P(),
        P(),
        P(),
        P("row", None),
        P("row", "rep", None, None, None),
        P("row", "rep", None),
        P("row", "rep", None),
        P("row", "rep"),
    )
    return jax.shard_map(
        shards,
        mesh=mesh,
        in_specs=placed,
        out_specs=(P(("row", "rep"), None), P(("row", "rep"), None), P(), P(), P()),
        check_vma=False,
    )
```

```python
import functools
import math

import jax
import jax.numpy as jnp
from jax import lax
from jax.experimental import pallas as pl
from jax.experimental.pallas import tpu as pltpu
from jax.sharding import PartitionSpec as P

F32 = jnp.float32
BF16 = jnp.bfloat16
VMEM = pl.BlockSpec(memory_space=pltpu.VMEM)
HBM = pl.BlockSpec(memory_space=pltpu.HBM)
SMEM = pl.BlockSpec(memory_space=pltpu.SMEM)
LIMIT = 16 * 1024 * 1024


def call(body, outs, ins, scratch=(), flops=0, limit=LIMIT):
    size = sum(math.prod(out.shape) * out.dtype.itemsize for out in outs)
    kernel = pl.pallas_call(
        body,
        out_shape=outs,
        in_specs=ins,
        out_specs=[VMEM] * len(outs),
        scratch_shapes=list(scratch),
        compiler_params=pltpu.CompilerParams(vmem_limit_bytes=limit),
        cost_estimate=pl.CostEstimate(flops=flops, bytes_accessed=2 * size, transcendentals=0),
    )
    return lambda *operands: list(kernel(*operands))


def shape(dims, kind):
    return jax.ShapeDtypeStruct(tuple(dims), kind)


def swap(value, step):
    return lax.ppermute(value, "row", [(i, i ^ step) for i in range(lax.axis_size("row"))])


def swap_rep(value, step):
    return lax.ppermute(value, "rep", [(i, i ^ step) for i in range(lax.axis_size("rep"))])


def contract(left, right, left_dim, right_dim):
    return lax.dot_general(
        left, right, (((left_dim,), (right_dim,)), ((), ())), preferred_element_type=F32
    )


def tree_sum(parts):
    while len(parts) > 1:
        parts = [parts[i] + parts[i + 1] for i in range(0, len(parts), 2)]
    return parts[0]


def place_of(sections):
    me = lax.axis_index("row")
    return me // sections, me % sections


def turn(c, replicas):
    out, bits = 0, replicas.bit_length() - 1
    for i in range(bits):
        out = out | ((c >> i) & 1) << (bits - 1 - i)
    return out


def tile_of(sections):
    return place_of(sections)[0] ^ lax.axis_index("rep")


def masks(first, count):
    first = first or 1
    return [first] + [m for m in range(1, count) if m != first]


def mask_of(first, j):
    first = jnp.where(first == 0, 1, first)
    return first if j == 0 else jnp.where(j >= first, j + 1, j)


def piece_of(ref, index, span):
    return ref[pl.ds(pl.multiple_of(index * span, span), span), :]


def first_kernel(sections, src, dst, count, tiles, field, bias, dense, bias_out, own, *rest):
    others, (total, sems) = rest[:-2], rest[-2:]
    size = tiles.shape[-1]
    block_rows = field.shape[0]
    _, s = place_of(sections)
    live = count[0, 0]
    dense[...] = jnp.zeros_like(dense)

    def tile_copy(e):
        row = pl.multiple_of(dst[0, 0, e] * size, size)
        col = pl.multiple_of(src[0, 0, e] * size, size)
        target = dense.at[pl.ds(row, size), pl.ds(col, size)]
        return pltpu.make_async_copy(tiles.at[0, 0, e], target, sems.at[e])

    lax.fori_loop(0, live, lambda e, carry: (tile_copy(e).start(), carry)[1], 0)
    bias_out[...] = bias[...]
    lax.fori_loop(0, live, lambda e, carry: (tile_copy(e).wait(), carry)[1], 0)
    for t in range(dense.shape[1] // size):
        cols = pl.ds(t * size, size)
        total[cols, :] = contract(dense[:, cols], field[...], 0, 0)
    own[...] = piece_of(total, s, block_rows)
    for k, out in enumerate(others, 1):
        out[...] = piece_of(total, s ^ k, block_rows).astype(BF16)


def block_kernel(sections, *refs):
    parts, own, others, total = refs[:sections], refs[sections], refs[sections + 1 : -1], refs[-1]
    share = own.shape[0]
    tile = tile_of(sections)
    value = parts[0][...]
    for ref in parts[1:]:
        value = value + ref[...].astype(F32)
    total[...] = value
    own[...] = piece_of(total, tile, share)
    for k, out in enumerate(others, 1):
        out[...] = piece_of(total, tile ^ k, share).astype(BF16)


def middle_kernel(norm, sections, replicas, parts, *refs):
    tiles, (pair, w_self, w_neigh, bias, act) = refs[:replicas], refs[replicas : replicas + 5]
    letters, (turned_f, turned_a) = refs[replicas + 5 : -2], refs[-2:]
    share, width = act.shape
    rows = width // parts
    q, _ = place_of(sections)
    total = tiles[0][...]
    for ref in tiles[1:]:
        total = total + ref[...].astype(F32)
    aggregate = (total * norm).astype(BF16)
    field = pair[pl.ds(0, share), :]
    pre = contract(field, w_self[...], 1, 0) + contract(aggregate, w_neigh[...], 1, 0)
    pre = pre + bias[...]
    slope = jnp.exp(jnp.minimum(pre, 0.0))
    act[...] = jnp.where(pre > 0.0, pre, slope - 1.0).astype(BF16)
    grad = (pair[pl.ds(share, share), :].astype(F32) * slope).astype(BF16)
    turned_f[...] = field.T
    turned_a[...] = aggregate.T
    span = sections * rows
    for k, letter in enumerate(letters):
        slot = (q ^ k) % (parts // sections)
        letter[pl.ds(0, share), :] = grad
        letter[pl.ds(share, span), pl.ds(0, share)] = piece_of(turned_f, slot, span)
        letter[pl.ds(share, span), pl.ds(128, share)] = piece_of(turned_a, slot, span)


def pack_kernel(sections, share, rows, *refs):
    letters, packs = refs[:-sections], refs[-sections:]
    _, s = place_of(sections)
    tile = tile_of(sections)
    block_rows = len(letters) * share
    for k, letter in enumerate(letters):
        here = pl.ds(pl.multiple_of((tile ^ k) * share, share), share)
        turned = pl.ds(pl.multiple_of(block_rows + (tile ^ k) * rows, rows), rows)
        for m, pack in enumerate(packs):
            first = pl.multiple_of(share + (s ^ m) * rows, 16)
            pack[here, :] = letter[pl.ds(0, share), :]
            pack[turned, :] = letter[pl.ds(first, rows), :]


def terms_kernel(share, rows, *refs):
    packs, (act, out, loaded) = refs[:-3], refs[-3:]
    width = out.shape[1]
    replicas = packs[0].shape[0] // (share + rows)
    ones = jnp.ones((16, share), BF16)
    sums = []
    for pack in packs:
        total = jnp.zeros((2 * rows + 16, width), F32)
        for i in range(replicas):
            turned = pl.ds(replicas * share + i * rows, rows)
            field, aggregate = pack[turned, pl.ds(0, share)], pack[turned, pl.ds(128, share)]
            left = jnp.concatenate([field, aggregate, ones])
            total += contract(left, pack[pl.ds(i * share, share), :], 1, 0)
        sums.append(total)
    total = tree_sum(sums)
    tail = total[2 * rows :]
    high = tail.astype(BF16).astype(F32)
    line = lax.broadcasted_iota(jnp.int32, tail.shape, 0)
    out[pl.ds(0, 2 * rows), :] = total[: 2 * rows].astype(BF16)
    out[pl.ds(2 * rows, 16), :] = jnp.where(line == 0, high, tail - high).astype(BF16)
    loaded[pl.ds(0, 2 * rows + 16), :] = out[...]
    loaded[pl.ds(2 * rows + 16, share), :] = act[...]


def back_kernel(norm, sections, replicas, *refs):
    packs, (dense, w_self, w_neigh) = refs[:sections], refs[sections : sections + 3]
    outs, (message, total) = refs[sections + 3 : -2], refs[-2:]
    me_rep = lax.axis_index("rep")
    q, s = place_of(sections)
    block_rows = dense.shape[0]
    share = block_rows // replicas
    for k, pack in enumerate(packs):
        here = pl.ds(pl.multiple_of((s ^ k) * block_rows, block_rows), block_rows)
        grad = pack[pl.ds(0, block_rows), :]
        message[here, :] = contract(grad, w_neigh[...], 1, 1).astype(BF16)
    total[...] = contract(dense[...], message[...], 1, 0) * norm

    @pl.when(me_rep == q)
    def _():
        total[...] += contract(packs[0][pl.ds(0, block_rows), :], w_self[...], 1, 1)

    for k, out in enumerate(outs):
        out[...] = piece_of(total, me_rep ^ k, share).astype(BF16)


def level_kernel(sections, rows, factor, *refs):
    parts, (act, bias, summed, act_out, sorted_parts) = refs[:-5], refs[-5:]
    q, _ = place_of(sections)
    me = lax.axis_index("rep")
    span = 2 * rows + 16
    sorted_parts[me] = parts[0][...]
    for j, part in enumerate(parts[1:]):
        sorted_parts[me ^ mask_of(q, j)] = part[pl.ds(0, span), :]
    terms = tree_sum([sorted_parts[c].astype(F32) for c in range(len(parts))])
    tail = terms[2 * rows : 2 * rows + 8]
    bias[...] = (tail[0:1] + tail[1:2]) * factor
    summed[...] = terms[: 2 * rows].astype(BF16)
    came = parts[1][pl.ds(span, act.shape[0]), :]
    act_out[...] = jnp.where(q == 0, act[...].astype(F32), came.astype(F32)).astype(BF16)


def last_kernel(*refs):
    parts, (act, grad_features, activations) = refs[:-3], refs[-3:]
    grad_features[...] = tree_sum([ref[...].astype(F32) for ref in parts]).astype(BF16)
    activations[...] = act[...]


def join_kernel(sections, *refs):
    pieces, out = refs[:-1], refs[-1]
    span = pieces[0].shape[0]
    q, _ = place_of(sections)
    for k, piece in enumerate(pieces):
        slot = (q % len(pieces)) ^ k
        out[pl.ds(pl.multiple_of(slot * span, 16), span), :] = piece[...]


def collect_kernel(rows, factor, *refs):
    joined, (grad_self, grad_neigh) = refs[:-2], refs[-2:]
    sections = len(joined)
    _, s = place_of(sections)
    for k, ref in enumerate(joined):
        for j in range(ref.shape[0] // (2 * rows)):
            place = pl.ds(pl.multiple_of((j * sections + (s ^ k)) * rows, rows), rows)
            base = j * 2 * rows
            grad_self[place, :] = ref[pl.ds(base, rows), :].astype(F32) * factor
            grad_neigh[place, :] = ref[pl.ds(base + rows, rows), :].astype(F32) * factor


def shards(
    features, w_self, w_neigh, bias_vector, cotangent, adj_values, src_slots, dst_slots, slot_counts
):
    block_rows, width = features.shape
    blocks, replicas = lax.axis_size("row"), lax.axis_size("rep")
    sections = blocks // replicas
    share = block_rows // replicas
    slot_total, size = adj_values.shape[2], adj_values.shape[-1]
    norm = 1.0 / math.sqrt(slot_total * replicas / (block_rows // size))
    factor = 1.0 / math.sqrt(block_rows * blocks)
    parts = min(blocks, width // 16)
    rows = width // parts

    def flat(q, s, c):
        return (q * sections + s) * replicas + c

    places = [
        (q, s, c) for q in range(replicas) for s in range(sections) for c in range(replicas)
    ]
    here = [flat(q, s, c) for q, s, c in places]
    source = [flat(c, s, q ^ turn(c, replicas)) for q, s, c in places]
    inside = [flat(q ^ c, s, c) for q, s, c in places]

    def swap_level(value, j):
        level = [flat(q, s, c ^ masks(q, replicas)[j]) for q, s, c in places]
        return lax.ppermute(value, ("row", "rep"), list(zip(here, level)))

    plane_rows = sections * block_rows
    chip, plane = place_of(sections)[0], lax.axis_index("rep")
    offset = (plane ^ turn(chip, replicas) ^ chip) * share
    pair = jnp.concatenate(
        [
            lax.dynamic_slice_in_dim(features, offset, share, 0),
            lax.dynamic_slice_in_dim(cotangent, offset, share, 0),
        ]
    )
    features, pair = lax.optimization_barrier((features, pair))
    dense, bias, own, *sent = call(
        functools.partial(first_kernel, sections),
        [
            shape((block_rows, plane_rows), BF16),
            shape((1, width), F32),
            shape((block_rows, width), F32),
        ]
        + [shape((block_rows, width), BF16)] * (sections - 1),
        [SMEM] * 3 + [HBM, VMEM, VMEM],
        [
            pltpu.VMEM((plane_rows, width), F32),
            pltpu.SemaphoreType.DMA((slot_total,)),
        ],
        flops=2 * plane_rows * block_rows * width,
        limit=51 * 1024 * 1024,
    )(src_slots, dst_slots, slot_counts, adj_values, features, bias_vector[None, :])
    pair, *sent = lax.optimization_barrier((pair, *sent))
    pair = lax.ppermute(pair, ("row", "rep"), list(zip(source, here)))
    received = [swap(value, k) for k, value in enumerate(sent, 1)]

    own, *sent = call(
        functools.partial(block_kernel, sections),
        [shape((share, width), F32)] + [shape((share, width), BF16)] * (replicas - 1),
        [VMEM] * sections,
        [pltpu.VMEM((block_rows, width), F32)],
    )(own, *received)
    received = [swap(value, k * sections) for k, value in enumerate(sent, 1)]

    act, *letters = call(
        functools.partial(middle_kernel, norm, sections, replicas, parts),
        [shape((share, width), BF16)]
        + [shape((share + sections * rows, width), BF16)] * replicas,
        [VMEM] * (replicas + 4),
        [pltpu.VMEM((width, share), BF16)] * 2,
    )(own, *received, pair, w_self, w_neigh, bias)
    letters = letters[:1] + [swap(v, k * sections) for k, v in enumerate(letters[1:], 1)]

    packs = call(
        functools.partial(pack_kernel, sections, share, rows),
        [shape((replicas * (share + rows), width), BF16)] * sections,
        [VMEM] * replicas,
    )(*letters)
    packs = packs[:1] + [swap(value, k) for k, value in enumerate(packs[1:], 1)]

    span = 2 * rows + 16
    terms, loaded = call(
        functools.partial(terms_kernel, share, rows),
        [shape((span, width), BF16), shape((span + share, width), BF16)],
        [VMEM] * (sections + 1),
        flops=2 * plane_rows * width * span,
    )(*packs, act)
    parts_here = [terms, swap_level(loaded, 0)]
    parts_here += [swap_level(terms, j) for j in range(1, replicas - 1)]

    sent = call(
        functools.partial(back_kernel, norm, sections, replicas),
        [shape((share, width), BF16)] * replicas,
        [VMEM] * (sections + 3),
        [pltpu.VMEM((plane_rows, width), BF16), pltpu.VMEM((block_rows, width), F32)],
        flops=2 * plane_rows * width * (block_rows + width),
    )(*packs, dense, w_self, w_neigh)
    received = sent[:1] + [swap_rep(value, k) for k, value in enumerate(sent[1:], 1)]
    _, *parts_here = lax.optimization_barrier((sent[0], *parts_here))

    grad_bias, summed, act = call(
        functools.partial(level_kernel, sections, rows, factor),
        [
            shape((1, width), F32),
            shape((2 * rows, width), BF16),
            shape((share, width), BF16),
        ],
        [VMEM] * (replicas + 1),
        [pltpu.VMEM((replicas, span, width), BF16)],
    )(*parts_here, act)
    act = lax.ppermute(act, ("row", "rep"), list(zip(here, inside)))
    spread = parts // sections
    pieces = [summed] + [swap(summed, k * sections) for k in range(1, spread)]
    count = len(pieces)
    together = lax.optimization_barrier((*pieces, act, *received))
    pieces, act, received = together[:count], together[count], together[count + 1 :]
    (joined,) = call(
        functools.partial(join_kernel, sections),
        [shape((spread * 2 * rows, width), BF16)],
        [VMEM] * spread,
    )(*pieces)
    joined = [joined] + [swap(joined, k) for k in range(1, sections)]
    grad_self, grad_neigh = call(
        functools.partial(collect_kernel, rows, factor),
        [shape((width, width), F32)] * 2,
        [VMEM] * sections,
    )(*joined)
    grad_features, activations = call(
        last_kernel, [shape((share, width), BF16)] * 2, [VMEM] * (replicas + 1)
    )(*received, act)
    return activations, grad_features, grad_self, grad_neigh, grad_bias[0]


def solution(mesh):
    placed = (
        P("row", None),
        P(),
        P(),
        P(),
        P("row", None),
        P("row", "rep", None, None, None),
        P("row", "rep", None),
        P("row", "rep", None),
        P("row", "rep"),
    )
    return jax.shard_map(
        shards,
        mesh=mesh,
        in_specs=placed,
        out_specs=(P(("row", "rep"), None), P(("row", "rep"), None), P(), P(), P()),
        check_vma=False,
    )
```

```python
import functools
import math

import jax
import jax.numpy as jnp
from jax import lax
from jax.experimental import pallas as pl
from jax.experimental.pallas import tpu as pltpu
from jax.sharding import PartitionSpec as P

F32 = jnp.float32
BF16 = jnp.bfloat16
VMEM = pl.BlockSpec(memory_space=pltpu.VMEM)
HBM = pl.BlockSpec(memory_space=pltpu.HBM)
SMEM = pl.BlockSpec(memory_space=pltpu.SMEM)
LIMIT = 16 * 1024 * 1024


def call(body, outs, ins, scratch=(), flops=0, limit=LIMIT):
    size = sum(math.prod(out.shape) * out.dtype.itemsize for out in outs)
    kernel = pl.pallas_call(
        body,
        out_shape=outs,
        in_specs=ins,
        out_specs=[VMEM] * len(outs),
        scratch_shapes=list(scratch),
        compiler_params=pltpu.CompilerParams(vmem_limit_bytes=limit),
        cost_estimate=pl.CostEstimate(flops=flops, bytes_accessed=2 * size, transcendentals=0),
    )
    return lambda *operands: list(kernel(*operands))


def shape(dims, kind):
    return jax.ShapeDtypeStruct(tuple(dims), kind)


def swap(value, step):
    return lax.ppermute(value, "row", [(i, i ^ step) for i in range(lax.axis_size("row"))])


def swap_rep(value, step):
    return lax.ppermute(value, "rep", [(i, i ^ step) for i in range(lax.axis_size("rep"))])


def contract(left, right, left_dim, right_dim):
    return lax.dot_general(
        left, right, (((left_dim,), (right_dim,)), ((), ())), preferred_element_type=F32
    )


def tree_sum(parts):
    while len(parts) > 1:
        parts = [parts[i] + parts[i + 1] for i in range(0, len(parts), 2)]
    return parts[0]


def place_of(sections):
    me = lax.axis_index("row")
    return me // sections, me % sections


def turn(c, replicas):
    out, bits = 0, replicas.bit_length() - 1
    for i in range(bits):
        out = out | ((c >> i) & 1) << (bits - 1 - i)
    return out


def tile_of(sections):
    return place_of(sections)[0] ^ lax.axis_index("rep")


def masks(first, count):
    first = first or 1
    return [first] + [m for m in range(1, count) if m != first]


def mask_of(first, j):
    first = jnp.where(first == 0, 1, first)
    return first if j == 0 else jnp.where(j >= first, j + 1, j)


def piece_of(ref, index, span):
    return ref[pl.ds(pl.multiple_of(index * span, span), span), :]


def first_kernel(sections, src, dst, count, tiles, field, bias, dense, bias_out, own, *rest):
    others, (total, sems) = rest[:-2], rest[-2:]
    size = tiles.shape[-1]
    block_rows = field.shape[0]
    _, s = place_of(sections)
    live = count[0, 0]
    dense[...] = jnp.zeros_like(dense)

    def tile_copy(e):
        row = pl.multiple_of(dst[0, 0, e] * size, size)
        col = pl.multiple_of(src[0, 0, e] * size, size)
        target = dense.at[pl.ds(row, size), pl.ds(col, size)]
        return pltpu.make_async_copy(tiles.at[0, 0, e], target, sems.at[e])

    lax.fori_loop(0, live, lambda e, carry: (tile_copy(e).start(), carry)[1], 0)
    bias_out[...] = bias[...]
    lax.fori_loop(0, live, lambda e, carry: (tile_copy(e).wait(), carry)[1], 0)
    for t in range(dense.shape[1] // size):
        cols = pl.ds(t * size, size)
        total[cols, :] = contract(dense[:, cols], field[...], 0, 0)
    own[...] = piece_of(total, s, block_rows)
    for k, out in enumerate(others, 1):
        out[...] = piece_of(total, s ^ k, block_rows).astype(BF16)


def block_kernel(sections, *refs):
    parts, own, others, total = refs[:sections], refs[sections], refs[sections + 1 : -1], refs[-1]
    share = own.shape[0]
    tile = tile_of(sections)
    value = parts[0][...]
    for ref in parts[1:]:
        value = value + ref[...].astype(F32)
    total[...] = value
    own[...] = piece_of(total, tile, share)
    for k, out in enumerate(others, 1):
        out[...] = piece_of(total, tile ^ k, share).astype(BF16)


def middle_kernel(norm, sections, replicas, parts, *refs):
    tiles, (pair, w_self, w_neigh, bias, act) = refs[:replicas], refs[replicas : replicas + 5]
    letters, (turned_f, turned_a) = refs[replicas + 5 : -2], refs[-2:]
    share, width = act.shape
    rows = width // parts
    q, _ = place_of(sections)
    total = tiles[0][...]
    for ref in tiles[1:]:
        total = total + ref[...].astype(F32)
    aggregate = (total * norm).astype(BF16)
    field = pair[pl.ds(0, share), :]
    pre = contract(field, w_self[...], 1, 0) + contract(aggregate, w_neigh[...], 1, 0)
    pre = pre + bias[...]
    slope = jnp.exp(jnp.minimum(pre, 0.0))
    act[...] = jnp.where(pre > 0.0, pre, slope - 1.0).astype(BF16)
    grad = (pair[pl.ds(share, share), :].astype(F32) * slope).astype(BF16)
    turned_f[...] = field.T
    turned_a[...] = aggregate.T
    span = sections * rows
    for k, letter in enumerate(letters):
        slot = (q ^ k) % (parts // sections)
        letter[pl.ds(0, share), :] = grad
        letter[pl.ds(share, span), pl.ds(0, share)] = piece_of(turned_f, slot, span)
        letter[pl.ds(share, span), pl.ds(128, share)] = piece_of(turned_a, slot, span)


def pack_kernel(sections, share, rows, *refs):
    letters, packs = refs[:-sections], refs[-sections:]
    _, s = place_of(sections)
    tile = tile_of(sections)
    block_rows = len(letters) * share
    for k, letter in enumerate(letters):
        here = pl.ds(pl.multiple_of((tile ^ k) * share, share), share)
        turned = pl.ds(pl.multiple_of(block_rows + (tile ^ k) * rows, rows), rows)
        for m, pack in enumerate(packs):
            first = pl.multiple_of(share + (s ^ m) * rows, 16)
            pack[here, :] = letter[pl.ds(0, share), :]
            pack[turned, :] = letter[pl.ds(first, rows), :]


def terms_kernel(share, rows, *refs):
    packs, out = refs[:-1], refs[-1]
    width = out.shape[1]
    replicas = packs[0].shape[0] // (share + rows)
    ones = jnp.ones((16, share), BF16)
    sums = []
    for pack in packs:
        total = jnp.zeros((2 * rows + 16, width), F32)
        for i in range(replicas):
            turned = pl.ds(replicas * share + i * rows, rows)
            field, aggregate = pack[turned, pl.ds(0, share)], pack[turned, pl.ds(128, share)]
            left = jnp.concatenate([field, aggregate, ones])
            total += contract(left, pack[pl.ds(i * share, share), :], 1, 0)
        sums.append(total)
    total = tree_sum(sums)
    tail = total[2 * rows :]
    high = tail.astype(BF16).astype(F32)
    line = lax.broadcasted_iota(jnp.int32, tail.shape, 0)
    out[pl.ds(0, 2 * rows), :] = total[: 2 * rows].astype(BF16)
    out[pl.ds(2 * rows, 16), :] = jnp.where(line == 0, high, tail - high).astype(BF16)


def back_kernel(norm, sections, replicas, *refs):
    packs, (dense, w_self, w_neigh, act) = refs[:sections], refs[sections : sections + 4]
    own, outs, (message, total) = refs[sections + 4], refs[sections + 5 : -2], refs[-2:]
    me_rep = lax.axis_index("rep")
    q, s = place_of(sections)
    block_rows = dense.shape[0]
    share = block_rows // replicas
    for k, pack in enumerate(packs):
        here = pl.ds(pl.multiple_of((s ^ k) * block_rows, block_rows), block_rows)
        grad = pack[pl.ds(0, block_rows), :]
        message[here, :] = contract(grad, w_neigh[...], 1, 1).astype(BF16)
    total[...] = contract(dense[...], message[...], 1, 0) * norm

    @pl.when(me_rep == q)
    def _():
        total[...] += contract(packs[0][pl.ds(0, block_rows), :], w_self[...], 1, 1)

    own[...] = piece_of(total, me_rep, share).astype(BF16)
    for j, out in enumerate(outs):
        out[pl.ds(0, share), :] = piece_of(total, me_rep ^ mask_of(q, j), share).astype(BF16)
    outs[0][pl.ds(share, share), :] = act[...]


def level_kernel(rows, factor, *refs):
    parts, (bias, summed) = refs[:-2], refs[-2:]
    terms = tree_sum([ref[...].astype(F32) for ref in parts])
    tail = terms[2 * rows : 2 * rows + 8]
    bias[...] = (tail[0:1] + tail[1:2]) * factor
    summed[...] = terms[: 2 * rows].astype(BF16)


def pick_kernel(sections, act, came, out):
    q, _ = place_of(sections)
    share = act.shape[0]
    arrived = came[pl.ds(share, share), :].astype(F32)
    out[...] = jnp.where(q == 0, act[...].astype(F32), arrived).astype(BF16)


def last_kernel(*refs):
    parts, (act, grad_features, activations) = refs[:-3], refs[-3:]
    here = pl.ds(0, grad_features.shape[0])
    grad_features[...] = tree_sum([ref[here, :].astype(F32) for ref in parts]).astype(BF16)
    activations[...] = act[...]


def join_kernel(sections, *refs):
    pieces, out = refs[:-1], refs[-1]
    span = pieces[0].shape[0]
    q, _ = place_of(sections)
    for k, piece in enumerate(pieces):
        slot = (q % len(pieces)) ^ k
        out[pl.ds(pl.multiple_of(slot * span, 16), span), :] = piece[...]


def collect_kernel(rows, factor, *refs):
    joined, (grad_self, grad_neigh) = refs[:-2], refs[-2:]
    sections = len(joined)
    _, s = place_of(sections)
    for k, ref in enumerate(joined):
        for j in range(ref.shape[0] // (2 * rows)):
            place = pl.ds(pl.multiple_of((j * sections + (s ^ k)) * rows, rows), rows)
            base = j * 2 * rows
            grad_self[place, :] = ref[pl.ds(base, rows), :].astype(F32) * factor
            grad_neigh[place, :] = ref[pl.ds(base + rows, rows), :].astype(F32) * factor


def shards(
    features, w_self, w_neigh, bias_vector, cotangent, adj_values, src_slots, dst_slots, slot_counts
):
    block_rows, width = features.shape
    blocks, replicas = lax.axis_size("row"), lax.axis_size("rep")
    sections = blocks // replicas
    share = block_rows // replicas
    slot_total, size = adj_values.shape[2], adj_values.shape[-1]
    norm = 1.0 / math.sqrt(slot_total * replicas / (block_rows // size))
    factor = 1.0 / math.sqrt(block_rows * blocks)
    parts = min(blocks, width // 16)
    rows = width // parts

    def flat(q, s, c):
        return (q * sections + s) * replicas + c

    places = [
        (q, s, c) for q in range(replicas) for s in range(sections) for c in range(replicas)
    ]
    here = [flat(q, s, c) for q, s, c in places]
    source = [flat(c, s, q ^ turn(c, replicas)) for q, s, c in places]
    inside = [flat(q ^ c, s, c) for q, s, c in places]

    def swap_level(value, j):
        level = [flat(q, s, c ^ masks(q, replicas)[j]) for q, s, c in places]
        return lax.ppermute(value, ("row", "rep"), list(zip(here, level)))

    plane_rows = sections * block_rows
    chip, plane = place_of(sections)[0], lax.axis_index("rep")
    offset = (plane ^ turn(chip, replicas) ^ chip) * share
    pair = jnp.concatenate(
        [
            lax.dynamic_slice_in_dim(features, offset, share, 0),
            lax.dynamic_slice_in_dim(cotangent, offset, share, 0),
        ]
    )
    features, pair = lax.optimization_barrier((features, pair))
    dense, bias, own, *sent = call(
        functools.partial(first_kernel, sections),
        [
            shape((block_rows, plane_rows), BF16),
            shape((1, width), F32),
            shape((block_rows, width), F32),
        ]
        + [shape((block_rows, width), BF16)] * (sections - 1),
        [SMEM] * 3 + [HBM, VMEM, VMEM],
        [
            pltpu.VMEM((plane_rows, width), F32),
            pltpu.SemaphoreType.DMA((slot_total,)),
        ],
        flops=2 * plane_rows * block_rows * width,
        limit=51 * 1024 * 1024,
    )(src_slots, dst_slots, slot_counts, adj_values, features, bias_vector[None, :])
    pair, *sent = lax.optimization_barrier((pair, *sent))
    pair = lax.ppermute(pair, ("row", "rep"), list(zip(source, here)))
    received = [swap(value, k) for k, value in enumerate(sent, 1)]

    own, *sent = call(
        functools.partial(block_kernel, sections),
        [shape((share, width), F32)] + [shape((share, width), BF16)] * (replicas - 1),
        [VMEM] * sections,
        [pltpu.VMEM((block_rows, width), F32)],
    )(own, *received)
    received = [swap(value, k * sections) for k, value in enumerate(sent, 1)]

    act, *letters = call(
        functools.partial(middle_kernel, norm, sections, replicas, parts),
        [shape((share, width), BF16)]
        + [shape((share + sections * rows, width), BF16)] * replicas,
        [VMEM] * (replicas + 4),
        [pltpu.VMEM((width, share), BF16)] * 2,
    )(own, *received, pair, w_self, w_neigh, bias)
    letters = letters[:1] + [swap(v, k * sections) for k, v in enumerate(letters[1:], 1)]

    packs = call(
        functools.partial(pack_kernel, sections, share, rows),
        [shape((replicas * (share + rows), width), BF16)] * sections,
        [VMEM] * replicas,
    )(*letters)
    packs = packs[:1] + [swap(value, k) for k, value in enumerate(packs[1:], 1)]

    (terms,) = call(
        functools.partial(terms_kernel, share, rows),
        [shape((2 * rows + 16, width), BF16)],
        [VMEM] * sections,
        flops=2 * plane_rows * width * (2 * rows + 16),
    )(*packs)
    terms = [terms] + [swap_rep(terms, k) for k in range(1, replicas)]

    sent = call(
        functools.partial(back_kernel, norm, sections, replicas),
        [shape((share, width), BF16), shape((2 * share, width), BF16)]
        + [shape((share, width), BF16)] * (replicas - 2),
        [VMEM] * (sections + 4),
        [pltpu.VMEM((plane_rows, width), BF16), pltpu.VMEM((block_rows, width), F32)],
        flops=2 * plane_rows * width * (block_rows + width),
    )(*packs, dense, w_self, w_neigh, act)
    _, *terms = lax.optimization_barrier((sent[0], *terms))
    grad_bias, summed = call(
        functools.partial(level_kernel, rows, factor),
        [shape((1, width), F32), shape((2 * rows, width), BF16)],
        [VMEM] * replicas,
    )(*terms)
    summed, *sent = lax.optimization_barrier((summed, *sent))
    received = [sent[0]] + [swap_level(value, j) for j, value in enumerate(sent[1:])]
    (act,) = call(
        functools.partial(pick_kernel, sections),
        [shape((share, width), BF16)],
        [VMEM] * 2,
    )(act, received[1])
    act = lax.ppermute(act, ("row", "rep"), list(zip(here, inside)))

    spread = parts // sections
    pieces = [summed] + [swap(summed, k * sections) for k in range(1, spread)]
    received[2], *pieces = lax.optimization_barrier((received[2], *pieces))
    (joined,) = call(
        functools.partial(join_kernel, sections),
        [shape((spread * 2 * rows, width), BF16)],
        [VMEM] * spread,
    )(*pieces)
    joined = [joined] + [swap(joined, k) for k in range(1, sections)]
    grad_self, grad_neigh = call(
        functools.partial(collect_kernel, rows, factor),
        [shape((width, width), F32)] * 2,
        [VMEM] * sections,
    )(*joined)
    grad_features, activations = call(
        last_kernel, [shape((share, width), BF16)] * 2, [VMEM] * (replicas + 1)
    )(*received, act)
    return activations, grad_features, grad_self, grad_neigh, grad_bias[0]


def solution(mesh):
    placed = (
        P("row", None),
        P(),
        P(),
        P(),
        P("row", None),
        P("row", "rep", None, None, None),
        P("row", "rep", None),
        P("row", "rep", None),
        P("row", "rep"),
    )
    return jax.shard_map(
        shards,
        mesh=mesh,
        in_specs=placed,
        out_specs=(P(("row", "rep"), None), P(("row", "rep"), None), P(), P(), P()),
        check_vma=False,
    )
```

```python
import functools
import math

import jax
import jax.numpy as jnp
from jax import lax
from jax.experimental import pallas as pl
from jax.experimental.pallas import tpu as pltpu
from jax.sharding import PartitionSpec as P

F32 = jnp.float32
BF16 = jnp.bfloat16
VMEM = pl.BlockSpec(memory_space=pltpu.VMEM)
HBM = pl.BlockSpec(memory_space=pltpu.HBM)
SMEM = pl.BlockSpec(memory_space=pltpu.SMEM)
LIMIT = 16 * 1024 * 1024


def call(body, outs, ins, scratch=(), flops=0, limit=LIMIT):
    size = sum(math.prod(out.shape) * out.dtype.itemsize for out in outs)
    kernel = pl.pallas_call(
        body,
        out_shape=outs,
        in_specs=ins,
        out_specs=[VMEM] * len(outs),
        scratch_shapes=list(scratch),
        compiler_params=pltpu.CompilerParams(vmem_limit_bytes=limit),
        cost_estimate=pl.CostEstimate(flops=flops, bytes_accessed=2 * size, transcendentals=0),
    )
    return lambda *operands: list(kernel(*operands))


def shape(dims, kind):
    return jax.ShapeDtypeStruct(tuple(dims), kind)


def swap(value, step):
    return lax.ppermute(value, "row", [(i, i ^ step) for i in range(lax.axis_size("row"))])


def swap_rep(value, step):
    return lax.ppermute(value, "rep", [(i, i ^ step) for i in range(lax.axis_size("rep"))])


def contract(left, right, left_dim, right_dim):
    return lax.dot_general(
        left, right, (((left_dim,), (right_dim,)), ((), ())), preferred_element_type=F32
    )


def tree_sum(parts):
    while len(parts) > 1:
        parts = [parts[i] + parts[i + 1] for i in range(0, len(parts), 2)]
    return parts[0]


def place_of(sections):
    me = lax.axis_index("row")
    return me // sections, me % sections


def turn(c, replicas):
    out, bits = 0, replicas.bit_length() - 1
    for i in range(bits):
        out = out | ((c >> i) & 1) << (bits - 1 - i)
    return out


def tile_of(sections):
    return place_of(sections)[0] ^ lax.axis_index("rep")


def masks(first, count):
    first = first or 1
    return [first] + [m for m in range(1, count) if m != first]


def mask_of(first, j):
    first = jnp.where(first == 0, 1, first)
    return first if j == 0 else jnp.where(j >= first, j + 1, j)


def piece_of(ref, index, span):
    return ref[pl.ds(pl.multiple_of(index * span, span), span), :]


def first_kernel(sections, src, dst, count, tiles, field, bias, dense, bias_out, own, *rest):
    others, (total, sems) = rest[:-2], rest[-2:]
    size = tiles.shape[-1]
    block_rows = field.shape[0]
    _, s = place_of(sections)
    live = count[0, 0]
    dense[...] = jnp.zeros_like(dense)

    def tile_copy(e):
        row = pl.multiple_of(dst[0, 0, e] * size, size)
        col = pl.multiple_of(src[0, 0, e] * size, size)
        target = dense.at[pl.ds(row, size), pl.ds(col, size)]
        return pltpu.make_async_copy(tiles.at[0, 0, e], target, sems.at[e])

    lax.fori_loop(0, live, lambda e, carry: (tile_copy(e).start(), carry)[1], 0)
    bias_out[...] = bias[...]
    lax.fori_loop(0, live, lambda e, carry: (tile_copy(e).wait(), carry)[1], 0)
    for t in range(dense.shape[1] // size):
        cols = pl.ds(t * size, size)
        total[cols, :] = contract(dense[:, cols], field[...], 0, 0)
    own[...] = piece_of(total, s, block_rows)
    for k, out in enumerate(others, 1):
        out[...] = piece_of(total, s ^ k, block_rows).astype(BF16)


def block_kernel(sections, *refs):
    parts, own, others, total = refs[:sections], refs[sections], refs[sections + 1 : -1], refs[-1]
    share = own.shape[0]
    tile = tile_of(sections)
    value = parts[0][...]
    for ref in parts[1:]:
        value = value + ref[...].astype(F32)
    total[...] = value
    own[...] = piece_of(total, tile, share)
    for k, out in enumerate(others, 1):
        out[...] = piece_of(total, tile ^ k, share).astype(BF16)


def middle_kernel(norm, sections, replicas, parts, *refs):
    tiles, (pair, w_self, w_neigh, bias, act) = refs[:replicas], refs[replicas : replicas + 5]
    letters, (turned_f, turned_a) = refs[replicas + 5 : -2], refs[-2:]
    share, width = act.shape
    rows = width // parts
    q, _ = place_of(sections)
    total = tiles[0][...]
    for ref in tiles[1:]:
        total = total + ref[...].astype(F32)
    aggregate = (total * norm).astype(BF16)
    field = pair[pl.ds(0, share), :]
    pre = contract(field, w_self[...], 1, 0) + contract(aggregate, w_neigh[...], 1, 0)
    pre = pre + bias[...]
    slope = jnp.exp(jnp.minimum(pre, 0.0))
    act[...] = jnp.where(pre > 0.0, pre, slope - 1.0).astype(BF16)
    grad = (pair[pl.ds(share, share), :].astype(F32) * slope).astype(BF16)
    turned_f[...] = field.T
    turned_a[...] = aggregate.T
    span = sections * rows
    for k, letter in enumerate(letters):
        slot = (q ^ k) % (parts // sections)
        letter[pl.ds(0, share), :] = grad
        letter[pl.ds(share, span), pl.ds(0, share)] = piece_of(turned_f, slot, span)
        letter[pl.ds(share, span), pl.ds(128, share)] = piece_of(turned_a, slot, span)


def pack_kernel(sections, share, rows, *refs):
    letters, packs = refs[:-sections], refs[-sections:]
    _, s = place_of(sections)
    tile = tile_of(sections)
    block_rows = len(letters) * share
    for k, letter in enumerate(letters):
        here = pl.ds(pl.multiple_of((tile ^ k) * share, share), share)
        turned = pl.ds(pl.multiple_of(block_rows + (tile ^ k) * rows, rows), rows)
        for m, pack in enumerate(packs):
            first = pl.multiple_of(share + (s ^ m) * rows, 16)
            pack[here, :] = letter[pl.ds(0, share), :]
            pack[turned, :] = letter[pl.ds(first, rows), :]


def terms_kernel(share, rows, *refs):
    packs, out = refs[:-1], refs[-1]
    width = out.shape[1]
    replicas = packs[0].shape[0] // (share + rows)
    ones = jnp.ones((16, share), BF16)
    sums = []
    for pack in packs:
        total = jnp.zeros((2 * rows + 16, width), F32)
        for i in range(replicas):
            turned = pl.ds(replicas * share + i * rows, rows)
            field, aggregate = pack[turned, pl.ds(0, share)], pack[turned, pl.ds(128, share)]
            left = jnp.concatenate([field, aggregate, ones])
            total += contract(left, pack[pl.ds(i * share, share), :], 1, 0)
        sums.append(total)
    total = tree_sum(sums)
    tail = total[2 * rows :]
    high = tail.astype(BF16).astype(F32)
    line = lax.broadcasted_iota(jnp.int32, tail.shape, 0)
    out[pl.ds(0, 2 * rows), :] = total[: 2 * rows].astype(BF16)
    out[pl.ds(2 * rows, 16), :] = jnp.where(line == 0, high, tail - high).astype(BF16)


def back_kernel(norm, sections, replicas, *refs):
    packs, (dense, w_self, w_neigh, act) = refs[:sections], refs[sections : sections + 4]
    own, outs, (message, total) = refs[sections + 4], refs[sections + 5 : -2], refs[-2:]
    me_rep = lax.axis_index("rep")
    q, s = place_of(sections)
    block_rows = dense.shape[0]
    share = block_rows // replicas
    for k, pack in enumerate(packs):
        here = pl.ds(pl.multiple_of((s ^ k) * block_rows, block_rows), block_rows)
        grad = pack[pl.ds(0, block_rows), :]
        message[here, :] = contract(grad, w_neigh[...], 1, 1).astype(BF16)
    total[...] = contract(dense[...], message[...], 1, 0) * norm

    @pl.when(me_rep == q)
    def _():
        total[...] += contract(packs[0][pl.ds(0, block_rows), :], w_self[...], 1, 1)

    own[...] = piece_of(total, me_rep, share).astype(BF16)
    for j, out in enumerate(outs):
        out[pl.ds(0, share), :] = piece_of(total, me_rep ^ mask_of(q, j), share).astype(BF16)
    outs[0][pl.ds(share, share), :] = act[...]


def level_kernel(rows, factor, *refs):
    parts, (bias, summed) = refs[:-2], refs[-2:]
    terms = tree_sum([ref[...].astype(F32) for ref in parts])
    tail = terms[2 * rows : 2 * rows + 8]
    bias[...] = (tail[0:1] + tail[1:2]) * factor
    summed[...] = terms[: 2 * rows].astype(BF16)


def pick_kernel(sections, act, came, out):
    q, _ = place_of(sections)
    share = act.shape[0]
    arrived = came[pl.ds(share, share), :].astype(F32)
    out[...] = jnp.where(q == 0, act[...].astype(F32), arrived).astype(BF16)


def last_kernel(*refs):
    parts, (act, grad_features, activations) = refs[:-3], refs[-3:]
    here = pl.ds(0, grad_features.shape[0])
    grad_features[...] = tree_sum([ref[here, :].astype(F32) for ref in parts]).astype(BF16)
    activations[...] = act[...]


def join_kernel(sections, *refs):
    pieces, out = refs[:-1], refs[-1]
    span = pieces[0].shape[0]
    q, _ = place_of(sections)
    for k, piece in enumerate(pieces):
        slot = (q % len(pieces)) ^ k
        out[pl.ds(pl.multiple_of(slot * span, 16), span), :] = piece[...]


def collect_kernel(rows, factor, *refs):
    joined, (grad_self, grad_neigh) = refs[:-2], refs[-2:]
    sections = len(joined)
    _, s = place_of(sections)
    for k, ref in enumerate(joined):
        for j in range(ref.shape[0] // (2 * rows)):
            place = pl.ds(pl.multiple_of((j * sections + (s ^ k)) * rows, rows), rows)
            base = j * 2 * rows
            grad_self[place, :] = ref[pl.ds(base, rows), :].astype(F32) * factor
            grad_neigh[place, :] = ref[pl.ds(base + rows, rows), :].astype(F32) * factor


def shards(
    features, w_self, w_neigh, bias_vector, cotangent, adj_values, src_slots, dst_slots, slot_counts
):
    block_rows, width = features.shape
    blocks, replicas = lax.axis_size("row"), lax.axis_size("rep")
    sections = blocks // replicas
    share = block_rows // replicas
    slot_total, size = adj_values.shape[2], adj_values.shape[-1]
    norm = 1.0 / math.sqrt(slot_total * replicas / (block_rows // size))
    factor = 1.0 / math.sqrt(block_rows * blocks)
    parts = min(blocks, width // 16)
    rows = width // parts

    def flat(q, s, c):
        return (q * sections + s) * replicas + c

    places = [
        (q, s, c) for q in range(replicas) for s in range(sections) for c in range(replicas)
    ]
    here = [flat(q, s, c) for q, s, c in places]
    source = [flat(c, s, q ^ turn(c, replicas)) for q, s, c in places]
    inside = [flat(q ^ c, s, c) for q, s, c in places]

    def swap_level(value, j):
        level = [flat(q, s, c ^ masks(q, replicas)[j]) for q, s, c in places]
        return lax.ppermute(value, ("row", "rep"), list(zip(here, level)))

    plane_rows = sections * block_rows
    chip, plane = place_of(sections)[0], lax.axis_index("rep")
    offset = (plane ^ turn(chip, replicas) ^ chip) * share
    pair = jnp.concatenate(
        [
            lax.dynamic_slice_in_dim(features, offset, share, 0),
            lax.dynamic_slice_in_dim(cotangent, offset, share, 0),
        ]
    )
    features, pair = lax.optimization_barrier((features, pair))
    dense, bias, own, *sent = call(
        functools.partial(first_kernel, sections),
        [
            shape((block_rows, plane_rows), BF16),
            shape((1, width), F32),
            shape((block_rows, width), F32),
        ]
        + [shape((block_rows, width), BF16)] * (sections - 1),
        [SMEM] * 3 + [HBM, VMEM, VMEM],
        [
            pltpu.VMEM((plane_rows, width), F32),
            pltpu.SemaphoreType.DMA((slot_total,)),
        ],
        flops=2 * plane_rows * block_rows * width,
        limit=51 * 1024 * 1024,
    )(src_slots, dst_slots, slot_counts, adj_values, features, bias_vector[None, :])
    pair, *sent = lax.optimization_barrier((pair, *sent))
    pair = lax.ppermute(pair, ("row", "rep"), list(zip(source, here)))
    received = [swap(value, k) for k, value in enumerate(sent, 1)]

    own, *sent = call(
        functools.partial(block_kernel, sections),
        [shape((share, width), F32)] + [shape((share, width), BF16)] * (replicas - 1),
        [VMEM] * sections,
        [pltpu.VMEM((block_rows, width), F32)],
    )(own, *received)
    received = [swap(value, k * sections) for k, value in enumerate(sent, 1)]

    act, *letters = call(
        functools.partial(middle_kernel, norm, sections, replicas, parts),
        [shape((share, width), BF16)]
        + [shape((share + sections * rows, width), BF16)] * replicas,
        [VMEM] * (replicas + 4),
        [pltpu.VMEM((width, share), BF16)] * 2,
    )(own, *received, pair, w_self, w_neigh, bias)
    letters = letters[:1] + [swap(v, k * sections) for k, v in enumerate(letters[1:], 1)]

    packs = call(
        functools.partial(pack_kernel, sections, share, rows),
        [shape((replicas * (share + rows), width), BF16)] * sections,
        [VMEM] * replicas,
    )(*letters)
    packs = packs[:1] + [swap(value, k) for k, value in enumerate(packs[1:], 1)]

    (terms,) = call(
        functools.partial(terms_kernel, share, rows),
        [shape((2 * rows + 16, width), BF16)],
        [VMEM] * sections,
        flops=2 * plane_rows * width * (2 * rows + 16),
    )(*packs)
    terms, *packs = lax.optimization_barrier((terms, *packs))
    terms = [terms] + [swap_rep(terms, k) for k in range(1, replicas)]

    sent = call(
        functools.partial(back_kernel, norm, sections, replicas),
        [shape((share, width), BF16), shape((2 * share, width), BF16)]
        + [shape((share, width), BF16)] * (replicas - 2),
        [VMEM] * (sections + 4),
        [pltpu.VMEM((plane_rows, width), BF16), pltpu.VMEM((block_rows, width), F32)],
        flops=2 * plane_rows * width * (block_rows + width),
    )(*packs, dense, w_self, w_neigh, act)
    received = [swap_level(value, j) for j, value in enumerate(sent[2:], 1)]
    _, *terms = lax.optimization_barrier((sent[0], *terms))
    grad_bias, summed = call(
        functools.partial(level_kernel, rows, factor),
        [shape((1, width), F32), shape((2 * rows, width), BF16)],
        [VMEM] * replicas,
    )(*terms)
    summed, loaded = lax.optimization_barrier((summed, sent[1]))
    loaded = swap_level(loaded, 0)
    (act,) = call(
        functools.partial(pick_kernel, sections),
        [shape((share, width), BF16)],
        [VMEM] * 2,
    )(act, loaded)
    act = lax.ppermute(act, ("row", "rep"), list(zip(here, inside)))
    spread = parts // sections
    pieces = [summed] + [swap(summed, k * sections) for k in range(1, spread)]
    pieces[-1], *received = lax.optimization_barrier((pieces[-1], *received))
    (joined,) = call(
        functools.partial(join_kernel, sections),
        [shape((spread * 2 * rows, width), BF16)],
        [VMEM] * spread,
    )(*pieces)
    joined = [joined] + [swap(joined, k) for k in range(1, sections)]
    grad_self, grad_neigh = call(
        functools.partial(collect_kernel, rows, factor),
        [shape((width, width), F32)] * 2,
        [VMEM] * sections,
    )(*joined)
    grad_features, activations = call(
        last_kernel, [shape((share, width), BF16)] * 2, [VMEM] * (replicas + 1)
    )(sent[0], loaded, *received, act)
    return activations, grad_features, grad_self, grad_neigh, grad_bias[0]


def solution(mesh):
    placed = (
        P("row", None),
        P(),
        P(),
        P(),
        P("row", None),
        P("row", "rep", None, None, None),
        P("row", "rep", None),
        P("row", "rep", None),
        P("row", "rep"),
    )
    return jax.shard_map(
        shards,
        mesh=mesh,
        in_specs=placed,
        out_specs=(P(("row", "rep"), None), P(("row", "rep"), None), P(), P(), P()),
        check_vma=False,
    )
```

```python
import functools
import math

import jax
import jax.numpy as jnp
from jax import lax
from jax.experimental import pallas as pl
from jax.experimental.pallas import tpu as pltpu
from jax.sharding import PartitionSpec as P

F32 = jnp.float32
BF16 = jnp.bfloat16
VMEM = pl.BlockSpec(memory_space=pltpu.VMEM)
HBM = pl.BlockSpec(memory_space=pltpu.HBM)
SMEM = pl.BlockSpec(memory_space=pltpu.SMEM)
LIMIT = 16 * 1024 * 1024


def call(body, outs, ins, scratch=(), flops=0, limit=LIMIT):
    size = sum(math.prod(out.shape) * out.dtype.itemsize for out in outs)
    kernel = pl.pallas_call(
        body,
        out_shape=outs,
        in_specs=ins,
        out_specs=[VMEM] * len(outs),
        scratch_shapes=list(scratch),
        compiler_params=pltpu.CompilerParams(vmem_limit_bytes=limit),
        cost_estimate=pl.CostEstimate(flops=flops, bytes_accessed=2 * size, transcendentals=0),
    )
    return lambda *operands: list(kernel(*operands))


def shape(dims, kind):
    return jax.ShapeDtypeStruct(tuple(dims), kind)


def swap(value, step):
    return lax.ppermute(value, "row", [(i, i ^ step) for i in range(lax.axis_size("row"))])


def swap_rep(value, step):
    return lax.ppermute(value, "rep", [(i, i ^ step) for i in range(lax.axis_size("rep"))])


def contract(left, right, left_dim, right_dim):
    return lax.dot_general(
        left, right, (((left_dim,), (right_dim,)), ((), ())), preferred_element_type=F32
    )


def tree_sum(parts):
    while len(parts) > 1:
        parts = [parts[i] + parts[i + 1] for i in range(0, len(parts), 2)]
    return parts[0]


def place_of(sections):
    me = lax.axis_index("row")
    return me // sections, me % sections


def turn(c, replicas):
    out, bits = 0, replicas.bit_length() - 1
    for i in range(bits):
        out = out | ((c >> i) & 1) << (bits - 1 - i)
    return out


def tile_of(sections):
    return place_of(sections)[0] ^ lax.axis_index("rep")


def piece_of(ref, index, span):
    return ref[pl.ds(pl.multiple_of(index * span, span), span), :]


def first_kernel(sections, src, dst, count, tiles, field, bias, dense, bias_out, own, *rest):
    others, (total, sems) = rest[:-2], rest[-2:]
    size = tiles.shape[-1]
    block_rows = field.shape[0]
    _, s = place_of(sections)
    live = count[0, 0]
    dense[...] = jnp.zeros_like(dense)

    def tile_copy(e):
        row = pl.multiple_of(dst[0, 0, e] * size, size)
        col = pl.multiple_of(src[0, 0, e] * size, size)
        target = dense.at[pl.ds(row, size), pl.ds(col, size)]
        return pltpu.make_async_copy(tiles.at[0, 0, e], target, sems.at[e])

    lax.fori_loop(0, live, lambda e, carry: (tile_copy(e).start(), carry)[1], 0)
    bias_out[...] = bias[...]
    lax.fori_loop(0, live, lambda e, carry: (tile_copy(e).wait(), carry)[1], 0)
    for t in range(dense.shape[1] // size):
        cols = pl.ds(t * size, size)
        total[cols, :] = contract(dense[:, cols], field[...], 0, 0)
    own[...] = piece_of(total, s, block_rows)
    for k, out in enumerate(others, 1):
        out[...] = piece_of(total, s ^ k, block_rows).astype(BF16)


def block_kernel(sections, *refs):
    parts, own, others, total = refs[:sections], refs[sections], refs[sections + 1 : -1], refs[-1]
    share = own.shape[0]
    tile = tile_of(sections)
    value = parts[0][...]
    for ref in parts[1:]:
        value = value + ref[...].astype(F32)
    total[...] = value
    own[...] = piece_of(total, tile, share)
    for k, out in enumerate(others, 1):
        out[...] = piece_of(total, tile ^ k, share).astype(BF16)


def middle_kernel(norm, sections, replicas, parts, *refs):
    tiles, (pair, w_self, w_neigh, bias, act) = refs[:replicas], refs[replicas : replicas + 5]
    letters, (turned_f, turned_a) = refs[replicas + 5 : -2], refs[-2:]
    share, width = act.shape
    rows = width // parts
    q, _ = place_of(sections)
    total = tiles[0][...]
    for ref in tiles[1:]:
        total = total + ref[...].astype(F32)
    aggregate = (total * norm).astype(BF16)
    field = pair[pl.ds(0, share), :]
    pre = contract(field, w_self[...], 1, 0) + contract(aggregate, w_neigh[...], 1, 0)
    pre = pre + bias[...]
    slope = jnp.exp(jnp.minimum(pre, 0.0))
    act[...] = jnp.where(pre > 0.0, pre, slope - 1.0).astype(BF16)
    grad = (pair[pl.ds(share, share), :].astype(F32) * slope).astype(BF16)
    turned_f[...] = field.T
    turned_a[...] = aggregate.T
    span = sections * rows
    for k, letter in enumerate(letters):
        slot = (q ^ k) % (parts // sections)
        letter[pl.ds(0, share), :] = grad
        letter[pl.ds(share, span), pl.ds(0, share)] = piece_of(turned_f, slot, span)
        letter[pl.ds(share, span), pl.ds(128, share)] = piece_of(turned_a, slot, span)


def pack_kernel(sections, share, rows, *refs):
    letters, packs = refs[:-sections], refs[-sections:]
    _, s = place_of(sections)
    tile = tile_of(sections)
    block_rows = len(letters) * share
    for k, letter in enumerate(letters):
        here = pl.ds(pl.multiple_of((tile ^ k) * share, share), share)
        turned = pl.ds(pl.multiple_of(block_rows + (tile ^ k) * rows, rows), rows)
        for m, pack in enumerate(packs):
            first = pl.multiple_of(share + (s ^ m) * rows, 16)
            pack[here, :] = letter[pl.ds(0, share), :]
            pack[turned, :] = letter[pl.ds(first, rows), :]


def terms_kernel(share, rows, *refs):
    packs, out = refs[:-1], refs[-1]
    width = out.shape[1]
    replicas = packs[0].shape[0] // (share + rows)
    ones = jnp.ones((16, share), BF16)
    sums = []
    for pack in packs:
        total = jnp.zeros((2 * rows + 16, width), F32)
        for i in range(replicas):
            turned = pl.ds(replicas * share + i * rows, rows)
            field, aggregate = pack[turned, pl.ds(0, share)], pack[turned, pl.ds(128, share)]
            left = jnp.concatenate([field, aggregate, ones])
            total += contract(left, pack[pl.ds(i * share, share), :], 1, 0)
        sums.append(total)
    total = tree_sum(sums)
    out[pl.ds(0, 2 * rows), :] = total[: 2 * rows].astype(BF16)
    write_bias(rows, total[2 * rows :], out)


def back_kernel(norm, sections, replicas, *refs):
    packs, (dense, w_self, w_neigh) = refs[:sections], refs[sections : sections + 3]
    keep, send, message, total = refs[sections + 3 :]
    me_rep = lax.axis_index("rep")
    q, s = place_of(sections)
    block_rows = dense.shape[0]
    for k, pack in enumerate(packs):
        here = pl.ds(pl.multiple_of((s ^ k) * block_rows, block_rows), block_rows)
        grad = pack[pl.ds(0, block_rows), :]
        message[here, :] = contract(grad, w_neigh[...], 1, 1).astype(BF16)
    total[...] = contract(dense[...], message[...], 1, 0) * norm

    @pl.when(me_rep == q)
    def _():
        total[...] += contract(packs[0][pl.ds(0, block_rows), :], w_self[...], 1, 1)

    halves(0, block_rows // replicas, total, keep, send)


def halves(bit, share, total, keep, send):
    mine = (lax.axis_index("rep") >> bit) & 1
    for i in range(keep.shape[0] // share):
        to = pl.ds(i * share, share)
        keep[to, :] = piece_of(total, 2 * i + mine, share)
        send[to, :] = piece_of(total, 2 * i + 1 - mine, share).astype(BF16)


def split_kernel(bit, share, held, came, keep, send, total):
    total[...] = held[...] + came[...].astype(F32)
    halves(bit, share, total, keep, send)


def add_terms(rows, here, came):
    summed = here[pl.ds(0, 2 * rows), :].astype(F32) + came[pl.ds(0, 2 * rows), :].astype(F32)
    tails = [ref[pl.ds(2 * rows, 16), :].astype(F32) for ref in (here, came)]
    bias = (tails[0][0:1] + tails[0][1:2]) + (tails[1][0:1] + tails[1][1:2])
    return summed, bias


def halfway_kernel(rows, here, came, out):
    summed, bias = add_terms(rows, here, came)
    out[pl.ds(0, 2 * rows), :] = summed.astype(BF16)
    write_bias(rows, jnp.broadcast_to(bias, (16, bias.shape[1])), out)


def write_bias(rows, tail, out):
    high = tail.astype(BF16).astype(F32)
    line = lax.broadcasted_iota(jnp.int32, tail.shape, 0)
    out[pl.ds(2 * rows, 16), :] = jnp.where(line == 0, high, tail - high).astype(BF16)


def level_kernel(rows, factor, here, came, bias, summed):
    total, tail = add_terms(rows, here, came)
    bias[...] = tail * factor
    summed[...] = total.astype(BF16)


def last_kernel(held, came, act, grad_features, activations):
    grad_features[...] = (held[...] + came[...].astype(F32)).astype(BF16)
    activations[...] = act[...]


def join_kernel(sections, bit, here, came, out):
    span = here.shape[0]
    mine = (place_of(sections)[0] >> bit) & 1
    out[pl.ds(pl.multiple_of(mine * span, 16), span), :] = here[...]
    out[pl.ds(pl.multiple_of((1 - mine) * span, 16), span), :] = came[...]


def collect_kernel(rows, factor, *refs):
    joined, (grad_self, grad_neigh) = refs[:-2], refs[-2:]
    sections = len(joined)
    _, s = place_of(sections)
    for k, ref in enumerate(joined):
        for j in range(ref.shape[0] // (2 * rows)):
            place = pl.ds(pl.multiple_of((j * sections + (s ^ k)) * rows, rows), rows)
            base = j * 2 * rows
            grad_self[place, :] = ref[pl.ds(base, rows), :].astype(F32) * factor
            grad_neigh[place, :] = ref[pl.ds(base + rows, rows), :].astype(F32) * factor


def shards(
    features, w_self, w_neigh, bias_vector, cotangent, adj_values, src_slots, dst_slots, slot_counts
):
    block_rows, width = features.shape
    blocks, replicas = lax.axis_size("row"), lax.axis_size("rep")
    sections = blocks // replicas
    share = block_rows // replicas
    slot_total, size = adj_values.shape[2], adj_values.shape[-1]
    norm = 1.0 / math.sqrt(slot_total * replicas / (block_rows // size))
    factor = 1.0 / math.sqrt(block_rows * blocks)
    parts = min(blocks, width // 16)
    rows = width // parts

    def flat(q, s, c):
        return (q * sections + s) * replicas + c

    places = [
        (q, s, c) for q in range(replicas) for s in range(sections) for c in range(replicas)
    ]
    here = [flat(q, s, c) for q, s, c in places]
    source = [flat(c, s, q ^ turn(c, replicas)) for q, s, c in places]
    level = [flat(q, s, q ^ c) for q, s, c in places]
    inside = [flat(q ^ c, s, c) for q, s, c in places]

    plane_rows = sections * block_rows
    chip, plane = place_of(sections)[0], lax.axis_index("rep")
    offset = (plane ^ turn(chip, replicas) ^ chip) * share
    pair = jnp.concatenate(
        [
            lax.dynamic_slice_in_dim(features, offset, share, 0),
            lax.dynamic_slice_in_dim(cotangent, offset, share, 0),
        ]
    )
    features, pair = lax.optimization_barrier((features, pair))
    dense, bias, own, *sent = call(
        functools.partial(first_kernel, sections),
        [
            shape((block_rows, plane_rows), BF16),
            shape((1, width), F32),
            shape((block_rows, width), F32),
        ]
        + [shape((block_rows, width), BF16)] * (sections - 1),
        [SMEM] * 3 + [HBM, VMEM, VMEM],
        [
            pltpu.VMEM((plane_rows, width), F32),
            pltpu.SemaphoreType.DMA((slot_total,)),
        ],
        flops=2 * plane_rows * block_rows * width,
        limit=51 * 1024 * 1024,
    )(src_slots, dst_slots, slot_counts, adj_values, features, bias_vector[None, :])
    pair, *sent = lax.optimization_barrier((pair, *sent))
    pair = lax.ppermute(pair, ("row", "rep"), list(zip(source, here)))
    received = [swap(value, k) for k, value in enumerate(sent, 1)]

    own, *sent = call(
        functools.partial(block_kernel, sections),
        [shape((share, width), F32)] + [shape((share, width), BF16)] * (replicas - 1),
        [VMEM] * sections,
        [pltpu.VMEM((block_rows, width), F32)],
    )(own, *received)
    received = [swap(value, k * sections) for k, value in enumerate(sent, 1)]

    act, *letters = call(
        functools.partial(middle_kernel, norm, sections, replicas, parts),
        [shape((share, width), BF16)]
        + [shape((share + sections * rows, width), BF16)] * replicas,
        [VMEM] * (replicas + 4),
        [pltpu.VMEM((width, share), BF16)] * 2,
    )(own, *received, pair, w_self, w_neigh, bias)
    letters = letters[:1] + [swap(v, k * sections) for k, v in enumerate(letters[1:], 1)]

    packs = call(
        functools.partial(pack_kernel, sections, share, rows),
        [shape((replicas * (share + rows), width), BF16)] * sections,
        [VMEM] * replicas,
    )(*letters)
    packs = packs[:1] + [swap(value, k) for k, value in enumerate(packs[1:], 1)]

    (terms,) = call(
        functools.partial(terms_kernel, share, rows),
        [shape((2 * rows + 16, width), BF16)],
        [VMEM] * sections,
        flops=2 * plane_rows * width * (2 * rows + 16),
    )(*packs)
    terms, act = lax.optimization_barrier((terms, act))
    act = lax.ppermute(act, ("row", "rep"), list(zip(here, level)))
    half = replicas // 2
    keep, send = call(
        functools.partial(back_kernel, norm, sections, replicas),
        [shape((half * share, width), F32), shape((half * share, width), BF16)],
        [VMEM] * (sections + 3),
        [pltpu.VMEM((plane_rows, width), BF16), pltpu.VMEM((block_rows, width), F32)],
        flops=2 * plane_rows * width * (block_rows + width),
    )(*packs, dense, w_self, w_neigh)

    bits = half.bit_length()
    for bit in range(bits - 1):
        came = swap_rep(terms, 1 << bit)
        came, keep = lax.optimization_barrier((came, keep))
        (terms,) = call(
            functools.partial(halfway_kernel, rows),
            [shape((2 * rows + 16, width), BF16)],
            [VMEM] * 2,
        )(terms, came)
    came = swap_rep(terms, half)
    terms, send = lax.optimization_barrier((terms, send))
    for bit in range(1, bits):
        arrived = swap_rep(send, 1 << (bit - 1))
        half //= 2
        keep, send = call(
            functools.partial(split_kernel, bit, share),
            [shape((half * share, width), F32), shape((half * share, width), BF16)],
            [VMEM] * 2,
            [pltpu.VMEM((2 * half * share, width), F32)],
        )(keep, arrived)
    arrived = swap_rep(send, replicas // 2)

    came, act, keep = lax.optimization_barrier((came, act, keep))
    act = lax.ppermute(act, ("row", "rep"), list(zip(here, inside)))
    grad_bias, joined = call(
        functools.partial(level_kernel, rows, factor),
        [shape((1, width), F32), shape((2 * rows, width), BF16)],
        [VMEM] * 2,
    )(terms, came)
    for bit in range((parts // sections).bit_length() - 1):
        (joined,) = call(
            functools.partial(join_kernel, sections, bit),
            [shape((2 * joined.shape[0], width), BF16)],
            [VMEM] * 2,
        )(joined, swap(joined, sections << bit))
    joined, act, arrived = lax.optimization_barrier((joined, act, arrived))
    joined = [joined] + [swap(joined, k) for k in range(1, sections)]
    grad_self, grad_neigh = call(
        functools.partial(collect_kernel, rows, factor),
        [shape((width, width), F32)] * 2,
        [VMEM] * sections,
    )(*joined)
    grad_features, activations = call(
        last_kernel, [shape((share, width), BF16)] * 2, [VMEM] * 3
    )(keep, arrived, act)
    return activations, grad_features, grad_self, grad_neigh, grad_bias[0]


def solution(mesh):
    placed = (
        P("row", None),
        P(),
        P(),
        P(),
        P("row", None),
        P("row", "rep", None, None, None),
        P("row", "rep", None),
        P("row", "rep", None),
        P("row", "rep"),
    )
    return jax.shard_map(
        shards,
        mesh=mesh,
        in_specs=placed,
        out_specs=(P(("row", "rep"), None), P(("row", "rep"), None), P(), P(), P()),
        check_vma=False,
    )
```

```python
import functools
import math

import jax
import jax.numpy as jnp
from jax import lax
from jax.experimental import pallas as pl
from jax.experimental.pallas import tpu as pltpu
from jax.sharding import PartitionSpec as P

F32 = jnp.float32
BF16 = jnp.bfloat16
VMEM = pl.BlockSpec(memory_space=pltpu.VMEM)
HBM = pl.BlockSpec(memory_space=pltpu.HBM)
SMEM = pl.BlockSpec(memory_space=pltpu.SMEM)
LIMIT = 16 * 1024 * 1024


def call(body, outs, ins, scratch=(), flops=0, limit=LIMIT):
    size = sum(math.prod(out.shape) * out.dtype.itemsize for out in outs)
    kernel = pl.pallas_call(
        body,
        out_shape=outs,
        in_specs=ins,
        out_specs=[VMEM] * len(outs),
        scratch_shapes=list(scratch),
        compiler_params=pltpu.CompilerParams(vmem_limit_bytes=limit),
        cost_estimate=pl.CostEstimate(flops=flops, bytes_accessed=2 * size, transcendentals=0),
    )
    return lambda *operands: list(kernel(*operands))


def shape(dims, kind):
    return jax.ShapeDtypeStruct(tuple(dims), kind)


def swap(value, step):
    return lax.ppermute(value, "row", [(i, i ^ step) for i in range(lax.axis_size("row"))])


def swap_rep(value, step):
    return lax.ppermute(value, "rep", [(i, i ^ step) for i in range(lax.axis_size("rep"))])


def contract(left, right, left_dim, right_dim):
    return lax.dot_general(
        left, right, (((left_dim,), (right_dim,)), ((), ())), preferred_element_type=F32
    )


def tree_sum(parts):
    while len(parts) > 1:
        parts = [parts[i] + parts[i + 1] for i in range(0, len(parts), 2)]
    return parts[0]


def place_of(sections):
    me = lax.axis_index("row")
    return me // sections, me % sections


def turn(c, replicas):
    out, bits = 0, replicas.bit_length() - 1
    for i in range(bits):
        out = out | ((c >> i) & 1) << (bits - 1 - i)
    return out


def tile_of(sections):
    return place_of(sections)[0] ^ lax.axis_index("rep")


def masks(first, count):
    first = first or 1
    return [first] + [m for m in range(1, count) if m != first]


def mask_of(first, j):
    first = jnp.where(first == 0, 1, first)
    return first if j == 0 else jnp.where(j >= first, j + 1, j)


def piece_of(ref, index, span):
    return ref[pl.ds(pl.multiple_of(index * span, span), span), :]


def first_kernel(sections, src, dst, count, tiles, field, bias, dense, bias_out, own, *rest):
    others, (total, sems) = rest[:-2], rest[-2:]
    size = tiles.shape[-1]
    block_rows = field.shape[0]
    _, s = place_of(sections)
    live = count[0, 0]
    dense[...] = jnp.zeros_like(dense)

    def tile_copy(e):
        row = pl.multiple_of(dst[0, 0, e] * size, size)
        col = pl.multiple_of(src[0, 0, e] * size, size)
        target = dense.at[pl.ds(row, size), pl.ds(col, size)]
        return pltpu.make_async_copy(tiles.at[0, 0, e], target, sems.at[e])

    lax.fori_loop(0, live, lambda e, carry: (tile_copy(e).start(), carry)[1], 0)
    bias_out[...] = bias[...]
    lax.fori_loop(0, live, lambda e, carry: (tile_copy(e).wait(), carry)[1], 0)
    for t in range(dense.shape[1] // size):
        cols = pl.ds(t * size, size)
        total[cols, :] = contract(dense[:, cols], field[...], 0, 0)
    own[...] = piece_of(total, s, block_rows)
    for k, out in enumerate(others, 1):
        out[...] = piece_of(total, s ^ k, block_rows).astype(BF16)


def block_kernel(sections, *refs):
    parts, own, others, total = refs[:sections], refs[sections], refs[sections + 1 : -1], refs[-1]
    share = own.shape[0]
    tile = tile_of(sections)
    value = parts[0][...]
    for ref in parts[1:]:
        value = value + ref[...].astype(F32)
    total[...] = value
    own[...] = piece_of(total, tile, share)
    for k, out in enumerate(others, 1):
        out[...] = piece_of(total, tile ^ k, share).astype(BF16)


def middle_kernel(norm, sections, replicas, parts, *refs):
    tiles, (pair, w_self, w_neigh, bias, act) = refs[:replicas], refs[replicas : replicas + 5]
    letters, (turned_f, turned_a) = refs[replicas + 5 : -2], refs[-2:]
    share, width = act.shape
    rows = width // parts
    q, _ = place_of(sections)
    total = tiles[0][...]
    for ref in tiles[1:]:
        total = total + ref[...].astype(F32)
    aggregate = (total * norm).astype(BF16)
    field = pair[pl.ds(0, share), :]
    pre = contract(field, w_self[...], 1, 0) + contract(aggregate, w_neigh[...], 1, 0)
    pre = pre + bias[...]
    slope = jnp.exp(jnp.minimum(pre, 0.0))
    act[...] = jnp.where(pre > 0.0, pre, slope - 1.0).astype(BF16)
    grad = (pair[pl.ds(share, share), :].astype(F32) * slope).astype(BF16)
    turned_f[...] = field.T
    turned_a[...] = aggregate.T
    span = sections * rows
    for k, letter in enumerate(letters):
        slot = (q ^ k) % (parts // sections)
        letter[pl.ds(0, share), :] = grad
        letter[pl.ds(share, span), pl.ds(0, share)] = piece_of(turned_f, slot, span)
        letter[pl.ds(share, span), pl.ds(128, share)] = piece_of(turned_a, slot, span)


def terms_kernel(share, *refs):
    letters, (grads, terms, turned) = refs[:-3], refs[-3:]
    tile = tile_of(lax.axis_size("row") // len(letters))
    width = grads.shape[1]
    span = letters[0].shape[0] - share
    for k, letter in enumerate(letters):
        here = pl.ds(pl.multiple_of((tile ^ k) * share, share), share)
        grads[here, :] = letter[pl.ds(0, share), :]
        turned[tile ^ k] = letter[pl.ds(share, span), :]
    ones = jnp.ones((16, share), BF16)
    total = jnp.zeros((2 * span + 16, width), F32)
    for i in range(len(letters)):
        field, aggregate = turned[i, :, pl.ds(0, share)], turned[i, :, pl.ds(128, share)]
        left = jnp.concatenate([field, aggregate, ones])
        total += contract(left, grads[pl.ds(i * share, share), :], 1, 0)
    write_terms(total[: 2 * span], total[2 * span :], terms)


def write_terms(weights, tail, out):
    span = weights.shape[0]
    out[pl.ds(0, span), :] = weights.astype(BF16)
    high = tail.astype(BF16).astype(F32)
    line = lax.broadcasted_iota(jnp.int32, tail.shape, 0)
    out[pl.ds(span, 16), :] = jnp.where(line == 0, high, tail - high).astype(BF16)


def add_terms(refs):
    span = refs[0].shape[0] - 16
    weights = tree_sum([ref[pl.ds(0, span), :].astype(F32) for ref in refs])
    tails = [ref[pl.ds(span, 16), :].astype(F32) for ref in refs]
    return weights, tree_sum([tail[0:1] + tail[1:2] for tail in tails])


def level_kernel(*refs):
    weights, bias = add_terms(refs[:-1])
    write_terms(weights, jnp.broadcast_to(bias, (16, bias.shape[1])), refs[-1])


def chip_kernel(factor, *refs):
    weights, bias = add_terms(refs[:-2])
    refs[-2][...] = weights.astype(BF16)
    refs[-1][...] = bias * factor


def back_kernel(norm, sections, replicas, *refs):
    packs, (dense, w_self, w_neigh, act) = refs[:sections], refs[sections : sections + 4]
    own, outs, (message, total) = refs[sections + 4], refs[sections + 5 : -2], refs[-2:]
    me_rep = lax.axis_index("rep")
    q, s = place_of(sections)
    block_rows = dense.shape[0]
    share = block_rows // replicas
    for k, pack in enumerate(packs):
        here = pl.ds(pl.multiple_of((s ^ k) * block_rows, block_rows), block_rows)
        message[here, :] = contract(pack[...], w_neigh[...], 1, 1).astype(BF16)
    total[...] = contract(dense[...], message[...], 1, 0) * norm

    @pl.when(me_rep == q)
    def _():
        total[...] += contract(packs[0][...], w_self[...], 1, 1)

    own[...] = piece_of(total, me_rep, share).astype(BF16)
    for j, out in enumerate(outs):
        out[pl.ds(0, share), :] = piece_of(total, me_rep ^ mask_of(q, j), share).astype(BF16)
    outs[0][pl.ds(share, share), :] = act[...]


def pick_kernel(sections, act, came, out):
    q, _ = place_of(sections)
    share = act.shape[0]
    arrived = came[pl.ds(share, share), :].astype(F32)
    out[...] = jnp.where(q == 0, act[...].astype(F32), arrived).astype(BF16)


def last_kernel(*refs):
    parts, (act, grad_features, activations) = refs[:-3], refs[-3:]
    here = pl.ds(0, grad_features.shape[0])
    grad_features[...] = tree_sum([ref[here, :].astype(F32) for ref in parts]).astype(BF16)
    activations[...] = act[...]


def collect_kernel(sections, factor, *refs):
    pieces, (grad_self, grad_neigh) = refs[:-2], refs[-2:]
    q, _ = place_of(sections)
    span = pieces[0].shape[0] // 2
    for k, piece in enumerate(pieces):
        slot = (q % len(pieces)) ^ k
        place = pl.ds(pl.multiple_of(slot * span, span), span)
        grad_self[place, :] = piece[pl.ds(0, span), :].astype(F32) * factor
        grad_neigh[place, :] = piece[pl.ds(span, span), :].astype(F32) * factor


def shards(
    features, w_self, w_neigh, bias_vector, cotangent, adj_values, src_slots, dst_slots, slot_counts
):
    block_rows, width = features.shape
    blocks, replicas = lax.axis_size("row"), lax.axis_size("rep")
    sections = blocks // replicas
    share = block_rows // replicas
    slot_total, size = adj_values.shape[2], adj_values.shape[-1]
    norm = 1.0 / math.sqrt(slot_total * replicas / (block_rows // size))
    factor = 1.0 / math.sqrt(block_rows * blocks)
    parts = min(blocks, width // 16)
    rows = width // parts

    def flat(q, s, c):
        return (q * sections + s) * replicas + c

    places = [
        (q, s, c) for q in range(replicas) for s in range(sections) for c in range(replicas)
    ]
    here = [flat(q, s, c) for q, s, c in places]
    source = [flat(c, s, q ^ turn(c, replicas)) for q, s, c in places]
    inside = [flat(q ^ c, s, c) for q, s, c in places]

    def swap_level(value, j):
        level = [flat(q, s, c ^ masks(q, replicas)[j]) for q, s, c in places]
        return lax.ppermute(value, ("row", "rep"), list(zip(here, level)))

    plane_rows = sections * block_rows
    chip, plane = place_of(sections)[0], lax.axis_index("rep")
    offset = (plane ^ turn(chip, replicas) ^ chip) * share
    pair = jnp.concatenate(
        [
            lax.dynamic_slice_in_dim(features, offset, share, 0),
            lax.dynamic_slice_in_dim(cotangent, offset, share, 0),
        ]
    )
    features, pair = lax.optimization_barrier((features, pair))
    dense, bias, own, *sent = call(
        functools.partial(first_kernel, sections),
        [
            shape((block_rows, plane_rows), BF16),
            shape((1, width), F32),
            shape((block_rows, width), F32),
        ]
        + [shape((block_rows, width), BF16)] * (sections - 1),
        [SMEM] * 3 + [HBM, VMEM, VMEM],
        [
            pltpu.VMEM((plane_rows, width), F32),
            pltpu.SemaphoreType.DMA((slot_total,)),
        ],
        flops=2 * plane_rows * block_rows * width,
        limit=51 * 1024 * 1024,
    )(src_slots, dst_slots, slot_counts, adj_values, features, bias_vector[None, :])
    pair, *sent = lax.optimization_barrier((pair, *sent))
    pair = lax.ppermute(pair, ("row", "rep"), list(zip(source, here)))
    received = [swap(value, k) for k, value in enumerate(sent, 1)]

    own, *sent = call(
        functools.partial(block_kernel, sections),
        [shape((share, width), F32)] + [shape((share, width), BF16)] * (replicas - 1),
        [VMEM] * sections,
        [pltpu.VMEM((block_rows, width), F32)],
    )(own, *received)
    received = [swap(value, k * sections) for k, value in enumerate(sent, 1)]

    act, *letters = call(
        functools.partial(middle_kernel, norm, sections, replicas, parts),
        [shape((share, width), BF16)]
        + [shape((share + sections * rows, width), BF16)] * replicas,
        [VMEM] * (replicas + 4),
        [pltpu.VMEM((width, share), BF16)] * 2,
    )(own, *received, pair, w_self, w_neigh, bias)
    letters = letters[:1] + [swap(v, k * sections) for k, v in enumerate(letters[1:], 1)]

    span = sections * rows
    grads, terms = call(
        functools.partial(terms_kernel, share),
        [shape((block_rows, width), BF16), shape((2 * span + 16, width), BF16)],
        [VMEM] * replicas,
        [pltpu.VMEM((replicas, span, width), BF16)],
        flops=2 * block_rows * width * (2 * span + 16),
    )(*letters)
    packs = [grads] + [swap(grads, k) for k in range(1, sections)]
    terms = [terms] + [swap_rep(terms, k) for k in range(1, replicas)]

    sent = call(
        functools.partial(back_kernel, norm, sections, replicas),
        [shape((share, width), BF16), shape((2 * share, width), BF16)]
        + [shape((share, width), BF16)] * (replicas - 2),
        [VMEM] * (sections + 4),
        [pltpu.VMEM((plane_rows, width), BF16), pltpu.VMEM((block_rows, width), F32)],
        flops=2 * plane_rows * width * (block_rows + width),
    )(*packs, dense, w_self, w_neigh, act)
    _, *terms = lax.optimization_barrier((sent[0], *terms))
    received = [swap_level(value, j) for j, value in enumerate(sent[1:])]
    (act,) = call(
        functools.partial(pick_kernel, sections),
        [shape((share, width), BF16)],
        [VMEM] * 2,
    )(act, received[0])
    act = lax.ppermute(act, ("row", "rep"), list(zip(here, inside)))

    (terms,) = call(
        level_kernel, [shape((2 * span + 16, width), BF16)], [VMEM] * replicas
    )(*terms)
    summed, grad_bias = call(
        functools.partial(chip_kernel, factor),
        [shape((2 * span, width), BF16), shape((1, width), F32)],
        [VMEM] * sections,
    )(terms, *[swap(terms, k) for k in range(1, sections)])
    pieces = [summed] + [swap(summed, k * sections) for k in range(1, parts // sections)]
    grad_features, activations = call(
        last_kernel, [shape((share, width), BF16)] * 2, [VMEM] * (replicas + 1)
    )(sent[0], *received, act)
    grad_self, grad_neigh = call(
        functools.partial(collect_kernel, sections, factor),
        [shape((width, width), F32)] * 2,
        [VMEM] * len(pieces),
    )(*pieces)
    return activations, grad_features, grad_self, grad_neigh, grad_bias[0]


def solution(mesh):
    placed = (
        P("row", None),
        P(),
        P(),
        P(),
        P("row", None),
        P("row", "rep", None, None, None),
        P("row", "rep", None),
        P("row", "rep", None),
        P("row", "rep"),
    )
    return jax.shard_map(
        shards,
        mesh=mesh,
        in_specs=placed,
        out_specs=(P(("row", "rep"), None), P(("row", "rep"), None), P(), P(), P()),
        check_vma=False,
    )
```

```python
import functools
import math

import jax
import jax.numpy as jnp
from jax import lax
from jax.experimental import pallas as pl
from jax.experimental.pallas import tpu as pltpu
from jax.sharding import PartitionSpec as P

F32 = jnp.float32
BF16 = jnp.bfloat16
VMEM = pl.BlockSpec(memory_space=pltpu.VMEM)
HBM = pl.BlockSpec(memory_space=pltpu.HBM)
SMEM = pl.BlockSpec(memory_space=pltpu.SMEM)
LIMIT = 16 * 1024 * 1024


def call(body, outs, ins, scratch=(), flops=0, limit=LIMIT):
    size = sum(math.prod(out.shape) * out.dtype.itemsize for out in outs)
    kernel = pl.pallas_call(
        body,
        out_shape=outs,
        in_specs=ins,
        out_specs=[VMEM] * len(outs),
        scratch_shapes=list(scratch),
        compiler_params=pltpu.CompilerParams(vmem_limit_bytes=limit),
        cost_estimate=pl.CostEstimate(flops=flops, bytes_accessed=2 * size, transcendentals=0),
    )
    return lambda *operands: list(kernel(*operands))


def shape(dims, kind):
    return jax.ShapeDtypeStruct(tuple(dims), kind)


def swap(value, step):
    return lax.ppermute(value, "row", [(i, i ^ step) for i in range(lax.axis_size("row"))])


def swap_rep(value, step):
    return lax.ppermute(value, "rep", [(i, i ^ step) for i in range(lax.axis_size("rep"))])


def contract(left, right, left_dim, right_dim):
    return lax.dot_general(
        left, right, (((left_dim,), (right_dim,)), ((), ())), preferred_element_type=F32
    )


def tree_sum(parts):
    while len(parts) > 1:
        parts = [parts[i] + parts[i + 1] for i in range(0, len(parts), 2)]
    return parts[0]


def place_of(sections):
    me = lax.axis_index("row")
    return me // sections, me % sections


def turn(c, replicas):
    out, bits = 0, replicas.bit_length() - 1
    for i in range(bits):
        out = out | ((c >> i) & 1) << (bits - 1 - i)
    return out


def tile_of(sections):
    return place_of(sections)[0] ^ lax.axis_index("rep")


def masks(first, count):
    first = first or 1
    return [first] + [m for m in range(1, count) if m != first]


def mask_of(first, j):
    first = jnp.where(first == 0, 1, first)
    return first if j == 0 else jnp.where(j >= first, j + 1, j)


def piece_of(ref, index, span):
    return ref[pl.ds(pl.multiple_of(index * span, span), span), :]


def first_kernel(sections, src, dst, count, tiles, field, bias, dense, bias_out, own, *rest):
    others, (total, sems) = rest[:-2], rest[-2:]
    size = tiles.shape[-1]
    block_rows = field.shape[0]
    _, s = place_of(sections)
    live = count[0, 0]
    dense[...] = jnp.zeros_like(dense)

    def tile_copy(e):
        row = pl.multiple_of(dst[0, 0, e] * size, size)
        col = pl.multiple_of(src[0, 0, e] * size, size)
        target = dense.at[pl.ds(row, size), pl.ds(col, size)]
        return pltpu.make_async_copy(tiles.at[0, 0, e], target, sems.at[e])

    lax.fori_loop(0, live, lambda e, carry: (tile_copy(e).start(), carry)[1], 0)
    bias_out[...] = bias[...]
    lax.fori_loop(0, live, lambda e, carry: (tile_copy(e).wait(), carry)[1], 0)
    for t in range(dense.shape[1] // size):
        cols = pl.ds(t * size, size)
        total[cols, :] = contract(dense[:, cols], field[...], 0, 0)
    own[...] = piece_of(total, s, block_rows)
    for k, out in enumerate(others, 1):
        out[...] = piece_of(total, s ^ k, block_rows).astype(BF16)


def block_kernel(sections, *refs):
    parts, own, others, total = refs[:sections], refs[sections], refs[sections + 1 : -1], refs[-1]
    share = own.shape[0]
    tile = tile_of(sections)
    value = parts[0][...]
    for ref in parts[1:]:
        value = value + ref[...].astype(F32)
    total[...] = value
    own[...] = piece_of(total, tile, share)
    for k, out in enumerate(others, 1):
        out[...] = piece_of(total, tile ^ k, share).astype(BF16)


def middle_kernel(norm, sections, replicas, parts, *refs):
    tiles, (pair, w_self, w_neigh, bias, act) = refs[:replicas], refs[replicas : replicas + 5]
    letters, (turned_f, turned_a) = refs[replicas + 5 : -2], refs[-2:]
    share, width = act.shape
    rows = width // parts
    q, _ = place_of(sections)
    total = tiles[0][...]
    for ref in tiles[1:]:
        total = total + ref[...].astype(F32)
    aggregate = (total * norm).astype(BF16)
    field = pair[pl.ds(0, share), :]
    pre = contract(field, w_self[...], 1, 0) + contract(aggregate, w_neigh[...], 1, 0)
    pre = pre + bias[...]
    slope = jnp.exp(jnp.minimum(pre, 0.0))
    act[...] = jnp.where(pre > 0.0, pre, slope - 1.0).astype(BF16)
    grad = (pair[pl.ds(share, share), :].astype(F32) * slope).astype(BF16)
    turned_f[...] = field.T
    turned_a[...] = aggregate.T
    span = sections * rows
    for k, letter in enumerate(letters):
        slot = (q ^ k) % (parts // sections)
        letter[pl.ds(0, share), :] = grad
        letter[pl.ds(share, span), pl.ds(0, share)] = piece_of(turned_f, slot, span)
        letter[pl.ds(share, span), pl.ds(128, share)] = piece_of(turned_a, slot, span)


def terms_kernel(share, *refs):
    letters, (grads, terms, turned) = refs[:-3], refs[-3:]
    tile = tile_of(lax.axis_size("row") // len(letters))
    width = grads.shape[1]
    span = letters[0].shape[0] - share
    for k, letter in enumerate(letters):
        here = pl.ds(pl.multiple_of((tile ^ k) * share, share), share)
        grads[here, :] = letter[pl.ds(0, share), :]
        turned[tile ^ k] = letter[pl.ds(share, span), :]
    ones = jnp.ones((16, share), BF16)
    total = jnp.zeros((2 * span + 16, width), F32)
    for i in range(len(letters)):
        field, aggregate = turned[i, :, pl.ds(0, share)], turned[i, :, pl.ds(128, share)]
        left = jnp.concatenate([field, aggregate, ones])
        total += contract(left, grads[pl.ds(i * share, share), :], 1, 0)
    write_terms(total[: 2 * span], total[2 * span :], terms)


def write_terms(weights, tail, out):
    span = weights.shape[0]
    out[pl.ds(0, span), :] = weights.astype(BF16)
    high = tail.astype(BF16).astype(F32)
    line = lax.broadcasted_iota(jnp.int32, tail.shape, 0)
    out[pl.ds(span, 16), :] = jnp.where(line == 0, high, tail - high).astype(BF16)


def add_terms(refs):
    span = refs[0].shape[0] - 16
    weights = tree_sum([ref[pl.ds(0, span), :].astype(F32) for ref in refs])
    tails = [ref[pl.ds(span, 16), :].astype(F32) for ref in refs]
    return weights, tree_sum([tail[0:1] + tail[1:2] for tail in tails])


def level_kernel(*refs):
    weights, bias = add_terms(refs[:-1])
    write_terms(weights, jnp.broadcast_to(bias, (16, bias.shape[1])), refs[-1])


def chip_kernel(factor, *refs):
    weights, bias = add_terms(refs[:-2])
    refs[-2][...] = weights.astype(BF16)
    refs[-1][...] = bias * factor


def back_kernel(norm, sections, replicas, *refs):
    packs, (dense, w_self, w_neigh, act) = refs[:sections], refs[sections : sections + 4]
    own, outs, (message, total) = refs[sections + 4], refs[sections + 5 : -2], refs[-2:]
    me_rep = lax.axis_index("rep")
    q, s = place_of(sections)
    block_rows = dense.shape[0]
    share = block_rows // replicas
    for k, pack in enumerate(packs):
        here = pl.ds(pl.multiple_of((s ^ k) * block_rows, block_rows), block_rows)
        message[here, :] = contract(pack[...], w_neigh[...], 1, 1).astype(BF16)
    total[...] = contract(dense[...], message[...], 1, 0) * norm

    @pl.when(me_rep == q)
    def _():
        total[...] += contract(packs[0][...], w_self[...], 1, 1)

    own[...] = piece_of(total, me_rep, share).astype(BF16)
    for j, out in enumerate(outs):
        out[pl.ds(0, share), :] = piece_of(total, me_rep ^ mask_of(q, j), share).astype(BF16)
    outs[0][pl.ds(share, share), :] = act[...]


def pick_kernel(sections, act, came, out):
    q, _ = place_of(sections)
    share = act.shape[0]
    arrived = came[pl.ds(share, share), :].astype(F32)
    out[...] = jnp.where(q == 0, act[...].astype(F32), arrived).astype(BF16)


def last_kernel(*refs):
    parts, (act, grad_features, activations) = refs[:-3], refs[-3:]
    here = pl.ds(0, grad_features.shape[0])
    grad_features[...] = tree_sum([ref[here, :].astype(F32) for ref in parts]).astype(BF16)
    activations[...] = act[...]


def collect_kernel(sections, factor, *refs):
    pieces, (grad_self, grad_neigh) = refs[:-2], refs[-2:]
    q, _ = place_of(sections)
    span = pieces[0].shape[0] // 2
    for k, piece in enumerate(pieces):
        slot = (q % len(pieces)) ^ k
        place = pl.ds(pl.multiple_of(slot * span, span), span)
        grad_self[place, :] = piece[pl.ds(0, span), :].astype(F32) * factor
        grad_neigh[place, :] = piece[pl.ds(span, span), :].astype(F32) * factor


def shards(
    features, w_self, w_neigh, bias_vector, cotangent, adj_values, src_slots, dst_slots, slot_counts
):
    block_rows, width = features.shape
    blocks, replicas = lax.axis_size("row"), lax.axis_size("rep")
    sections = blocks // replicas
    share = block_rows // replicas
    slot_total, size = adj_values.shape[2], adj_values.shape[-1]
    norm = 1.0 / math.sqrt(slot_total * replicas / (block_rows // size))
    factor = 1.0 / math.sqrt(block_rows * blocks)
    parts = min(blocks, width // 16)
    rows = width // parts

    def flat(q, s, c):
        return (q * sections + s) * replicas + c

    places = [
        (q, s, c) for q in range(replicas) for s in range(sections) for c in range(replicas)
    ]
    here = [flat(q, s, c) for q, s, c in places]
    source = [flat(c, s, q ^ turn(c, replicas)) for q, s, c in places]
    inside = [flat(q ^ c, s, c) for q, s, c in places]

    def swap_level(value, j):
        level = [flat(q, s, c ^ masks(q, replicas)[j]) for q, s, c in places]
        return lax.ppermute(value, ("row", "rep"), list(zip(here, level)))

    plane_rows = sections * block_rows
    chip, plane = place_of(sections)[0], lax.axis_index("rep")
    offset = (plane ^ turn(chip, replicas) ^ chip) * share
    pair = jnp.concatenate(
        [
            lax.dynamic_slice_in_dim(features, offset, share, 0),
            lax.dynamic_slice_in_dim(cotangent, offset, share, 0),
        ]
    )
    features, pair = lax.optimization_barrier((features, pair))
    dense, bias, own, *sent = call(
        functools.partial(first_kernel, sections),
        [
            shape((block_rows, plane_rows), BF16),
            shape((1, width), F32),
            shape((block_rows, width), F32),
        ]
        + [shape((block_rows, width), BF16)] * (sections - 1),
        [SMEM] * 3 + [HBM, VMEM, VMEM],
        [
            pltpu.VMEM((plane_rows, width), F32),
            pltpu.SemaphoreType.DMA((slot_total,)),
        ],
        flops=2 * plane_rows * block_rows * width,
        limit=51 * 1024 * 1024,
    )(src_slots, dst_slots, slot_counts, adj_values, features, bias_vector[None, :])
    pair, *sent = lax.optimization_barrier((pair, *sent))
    pair = lax.ppermute(pair, ("row", "rep"), list(zip(source, here)))
    received = [swap(value, k) for k, value in enumerate(sent, 1)]

    own, *sent = call(
        functools.partial(block_kernel, sections),
        [shape((share, width), F32)] + [shape((share, width), BF16)] * (replicas - 1),
        [VMEM] * sections,
        [pltpu.VMEM((block_rows, width), F32)],
    )(own, *received)
    received = [swap(value, k * sections) for k, value in enumerate(sent, 1)]

    act, *letters = call(
        functools.partial(middle_kernel, norm, sections, replicas, parts),
        [shape((share, width), BF16)]
        + [shape((share + sections * rows, width), BF16)] * replicas,
        [VMEM] * (replicas + 4),
        [pltpu.VMEM((width, share), BF16)] * 2,
    )(own, *received, pair, w_self, w_neigh, bias)
    letters = letters[:1] + [swap(v, k * sections) for k, v in enumerate(letters[1:], 1)]

    span = sections * rows
    grads, terms = call(
        functools.partial(terms_kernel, share),
        [shape((block_rows, width), BF16), shape((2 * span + 16, width), BF16)],
        [VMEM] * replicas,
        [pltpu.VMEM((replicas, span, width), BF16)],
        flops=2 * block_rows * width * (2 * span + 16),
    )(*letters)
    packs = [grads] + [swap(grads, k) for k in range(1, sections)]
    terms = [terms] + [swap_rep(terms, k) for k in range(1, replicas)]

    sent = call(
        functools.partial(back_kernel, norm, sections, replicas),
        [shape((share, width), BF16), shape((2 * share, width), BF16)]
        + [shape((share, width), BF16)] * (replicas - 2),
        [VMEM] * (sections + 4),
        [pltpu.VMEM((plane_rows, width), BF16), pltpu.VMEM((block_rows, width), F32)],
        flops=2 * plane_rows * width * (block_rows + width),
    )(*packs, dense, w_self, w_neigh, act)
    _, *terms = lax.optimization_barrier((sent[0], *terms))
    received = [swap_level(value, j) for j, value in enumerate(sent[1:])]
    (terms,) = call(
        level_kernel, [shape((2 * span + 16, width), BF16)], [VMEM] * replicas
    )(*terms)
    summed, grad_bias = call(
        functools.partial(chip_kernel, factor),
        [shape((2 * span, width), BF16), shape((1, width), F32)],
        [VMEM] * sections,
    )(terms, *[swap(terms, k) for k in range(1, sections)])
    summed, received[0] = lax.optimization_barrier((summed, received[0]))
    (act,) = call(
        functools.partial(pick_kernel, sections),
        [shape((share, width), BF16)],
        [VMEM] * 2,
    )(act, received[0])
    act = lax.ppermute(act, ("row", "rep"), list(zip(here, inside)))
    pieces = [summed] + [swap(summed, k * sections) for k in range(1, parts // sections)]
    grad_features, activations = call(
        last_kernel, [shape((share, width), BF16)] * 2, [VMEM] * (replicas + 1)
    )(sent[0], *received, act)
    grad_self, grad_neigh = call(
        functools.partial(collect_kernel, sections, factor),
        [shape((width, width), F32)] * 2,
        [VMEM] * len(pieces),
    )(*pieces)
    return activations, grad_features, grad_self, grad_neigh, grad_bias[0]


def solution(mesh):
    placed = (
        P("row", None),
        P(),
        P(),
        P(),
        P("row", None),
        P("row", "rep", None, None, None),
        P("row", "rep", None),
        P("row", "rep", None),
        P("row", "rep"),
    )
    return jax.shard_map(
        shards,
        mesh=mesh,
        in_specs=placed,
        out_specs=(P(("row", "rep"), None), P(("row", "rep"), None), P(), P(), P()),
        check_vma=False,
    )
```

```python
import functools
import math

import jax
import jax.numpy as jnp
from jax import lax
from jax.experimental import pallas as pl
from jax.experimental.pallas import tpu as pltpu
from jax.sharding import PartitionSpec as P

F32 = jnp.float32
BF16 = jnp.bfloat16
VMEM = pl.BlockSpec(memory_space=pltpu.VMEM)
HBM = pl.BlockSpec(memory_space=pltpu.HBM)
SMEM = pl.BlockSpec(memory_space=pltpu.SMEM)
LIMIT = 16 * 1024 * 1024


def call(body, outs, ins, scratch=(), flops=0, limit=LIMIT):
    size = sum(math.prod(out.shape) * out.dtype.itemsize for out in outs)
    kernel = pl.pallas_call(
        body,
        out_shape=outs,
        in_specs=ins,
        out_specs=[VMEM] * len(outs),
        scratch_shapes=list(scratch),
        compiler_params=pltpu.CompilerParams(vmem_limit_bytes=limit),
        cost_estimate=pl.CostEstimate(flops=flops, bytes_accessed=2 * size, transcendentals=0),
    )
    return lambda *operands: list(kernel(*operands))


def shape(dims, kind):
    return jax.ShapeDtypeStruct(tuple(dims), kind)


def swap(value, step):
    return lax.ppermute(value, "row", [(i, i ^ step) for i in range(lax.axis_size("row"))])


def swap_rep(value, step):
    return lax.ppermute(value, "rep", [(i, i ^ step) for i in range(lax.axis_size("rep"))])


def contract(left, right, left_dim, right_dim):
    return lax.dot_general(
        left, right, (((left_dim,), (right_dim,)), ((), ())), preferred_element_type=F32
    )


def tree_sum(parts):
    while len(parts) > 1:
        parts = [parts[i] + parts[i + 1] for i in range(0, len(parts), 2)]
    return parts[0]


def place_of(sections):
    me = lax.axis_index("row")
    return me // sections, me % sections


def turn(c, replicas):
    out, bits = 0, replicas.bit_length() - 1
    for i in range(bits):
        out = out | ((c >> i) & 1) << (bits - 1 - i)
    return out


def tile_of(sections):
    return place_of(sections)[0] ^ lax.axis_index("rep")


def piece_of(ref, index, span):
    return ref[pl.ds(pl.multiple_of(index * span, span), span), :]


def first_kernel(sections, src, dst, count, tiles, field, bias, dense, bias_out, own, *rest):
    others, (total, sems) = rest[:-2], rest[-2:]
    size = tiles.shape[-1]
    block_rows = field.shape[0]
    _, s = place_of(sections)
    live = count[0, 0]
    dense[...] = jnp.zeros_like(dense)

    def tile_copy(e):
        row = pl.multiple_of(dst[0, 0, e] * size, size)
        col = pl.multiple_of(src[0, 0, e] * size, size)
        target = dense.at[pl.ds(row, size), pl.ds(col, size)]
        return pltpu.make_async_copy(tiles.at[0, 0, e], target, sems.at[e])

    lax.fori_loop(0, live, lambda e, carry: (tile_copy(e).start(), carry)[1], 0)
    bias_out[...] = bias[...]
    lax.fori_loop(0, live, lambda e, carry: (tile_copy(e).wait(), carry)[1], 0)
    for t in range(dense.shape[1] // size):
        cols = pl.ds(t * size, size)
        total[cols, :] = contract(dense[:, cols], field[...], 0, 0)
    own[...] = piece_of(total, s, block_rows)
    for k, out in enumerate(others, 1):
        out[...] = piece_of(total, s ^ k, block_rows).astype(BF16)


def block_kernel(sections, *refs):
    parts, own, others, total = refs[:sections], refs[sections], refs[sections + 1 : -1], refs[-1]
    share = own.shape[0]
    tile = tile_of(sections)
    value = parts[0][...]
    for ref in parts[1:]:
        value = value + ref[...].astype(F32)
    total[...] = value
    own[...] = piece_of(total, tile, share)
    for k, out in enumerate(others, 1):
        out[...] = piece_of(total, tile ^ k, share).astype(BF16)


def middle_kernel(norm, sections, replicas, parts, *refs):
    tiles, (pair, w_self, w_neigh, bias, act) = refs[:replicas], refs[replicas : replicas + 5]
    letters, (turned_f, turned_a) = refs[replicas + 5 : -2], refs[-2:]
    share, width = act.shape
    rows = width // parts
    q, _ = place_of(sections)
    total = tiles[0][...]
    for ref in tiles[1:]:
        total = total + ref[...].astype(F32)
    aggregate = (total * norm).astype(BF16)
    field = pair[pl.ds(0, share), :]
    pre = contract(field, w_self[...], 1, 0) + contract(aggregate, w_neigh[...], 1, 0)
    pre = pre + bias[...]
    slope = jnp.exp(jnp.minimum(pre, 0.0))
    act[...] = jnp.where(pre > 0.0, pre, slope - 1.0).astype(BF16)
    grad = (pair[pl.ds(share, share), :].astype(F32) * slope).astype(BF16)
    turned_f[...] = field.T
    turned_a[...] = aggregate.T
    span = sections * rows
    for k, letter in enumerate(letters):
        slot = (q ^ k) % (parts // sections)
        letter[pl.ds(0, share), :] = grad
        letter[pl.ds(share, span), pl.ds(0, share)] = piece_of(turned_f, slot, span)
        letter[pl.ds(share, span), pl.ds(128, share)] = piece_of(turned_a, slot, span)


def terms_kernel(share, *refs):
    letters, (grads, terms, turned) = refs[:-3], refs[-3:]
    tile = tile_of(lax.axis_size("row") // len(letters))
    width = grads.shape[1]
    span = letters[0].shape[0] - share
    for k, letter in enumerate(letters):
        here = pl.ds(pl.multiple_of((tile ^ k) * share, share), share)
        grads[here, :] = letter[pl.ds(0, share), :]
        turned[tile ^ k] = letter[pl.ds(share, span), :]
    ones = jnp.ones((16, share), BF16)
    total = jnp.zeros((2 * span + 16, width), F32)
    for i in range(len(letters)):
        field, aggregate = turned[i, :, pl.ds(0, share)], turned[i, :, pl.ds(128, share)]
        left = jnp.concatenate([field, aggregate, ones])
        total += contract(left, grads[pl.ds(i * share, share), :], 1, 0)
    write_terms(total[: 2 * span], total[2 * span :], terms)


def write_terms(weights, tail, out):
    span = weights.shape[0]
    out[pl.ds(0, span), :] = weights.astype(BF16)
    high = tail.astype(BF16).astype(F32)
    line = lax.broadcasted_iota(jnp.int32, tail.shape, 0)
    out[pl.ds(span, 16), :] = jnp.where(line == 0, high, tail - high).astype(BF16)


def add_terms(refs):
    span = refs[0].shape[0] - 16
    weights = tree_sum([ref[pl.ds(0, span), :].astype(F32) for ref in refs])
    tails = [ref[pl.ds(span, 16), :].astype(F32) for ref in refs]
    return weights, tree_sum([tail[0:1] + tail[1:2] for tail in tails])


def level_kernel(*refs):
    weights, bias = add_terms(refs[:-1])
    write_terms(weights, jnp.broadcast_to(bias, (16, bias.shape[1])), refs[-1])


def chip_kernel(factor, *refs):
    weights, bias = add_terms(refs[:-2])
    refs[-2][...] = weights.astype(BF16)
    refs[-1][...] = bias * factor


def back_kernel(norm, sections, replicas, *refs):
    packs, (dense, w_self, w_neigh) = refs[:sections], refs[sections : sections + 3]
    outs, (message, total) = refs[sections + 3 : -2], refs[-2:]
    me_rep = lax.axis_index("rep")
    q, s = place_of(sections)
    block_rows = dense.shape[0]
    share = block_rows // replicas
    for k, pack in enumerate(packs):
        here = pl.ds(pl.multiple_of((s ^ k) * block_rows, block_rows), block_rows)
        message[here, :] = contract(pack[...], w_neigh[...], 1, 1).astype(BF16)
    total[...] = contract(dense[...], message[...], 1, 0) * norm

    @pl.when(me_rep == q)
    def _():
        total[...] += contract(packs[0][...], w_self[...], 1, 1)

    for k, out in enumerate(outs):
        out[...] = piece_of(total, me_rep ^ k, share).astype(BF16)


def last_kernel(*refs):
    parts, (act, grad_features, activations) = refs[:-3], refs[-3:]
    grad_features[...] = tree_sum([ref[...].astype(F32) for ref in parts]).astype(BF16)
    activations[...] = act[...]


def collect_kernel(sections, factor, *refs):
    pieces, (grad_self, grad_neigh) = refs[:-2], refs[-2:]
    q, _ = place_of(sections)
    span = pieces[0].shape[0] // 2
    for k, piece in enumerate(pieces):
        slot = (q % len(pieces)) ^ k
        place = pl.ds(pl.multiple_of(slot * span, span), span)
        grad_self[place, :] = piece[pl.ds(0, span), :].astype(F32) * factor
        grad_neigh[place, :] = piece[pl.ds(span, span), :].astype(F32) * factor


def shards(
    features, w_self, w_neigh, bias_vector, cotangent, adj_values, src_slots, dst_slots, slot_counts
):
    block_rows, width = features.shape
    blocks, replicas = lax.axis_size("row"), lax.axis_size("rep")
    sections = blocks // replicas
    share = block_rows // replicas
    slot_total, size = adj_values.shape[2], adj_values.shape[-1]
    norm = 1.0 / math.sqrt(slot_total * replicas / (block_rows // size))
    factor = 1.0 / math.sqrt(block_rows * blocks)
    parts = min(blocks, width // 16)
    rows = width // parts

    def flat(q, s, c):
        return (q * sections + s) * replicas + c

    places = [
        (q, s, c) for q in range(replicas) for s in range(sections) for c in range(replicas)
    ]
    here = [flat(q, s, c) for q, s, c in places]
    source = [flat(c, s, q ^ turn(c, replicas)) for q, s, c in places]
    level = [flat(q, s, q ^ c) for q, s, c in places]
    inside = [flat(q ^ c, s, c) for q, s, c in places]

    plane_rows = sections * block_rows
    chip, plane = place_of(sections)[0], lax.axis_index("rep")
    offset = (plane ^ turn(chip, replicas) ^ chip) * share
    pair = jnp.concatenate(
        [
            lax.dynamic_slice_in_dim(features, offset, share, 0),
            lax.dynamic_slice_in_dim(cotangent, offset, share, 0),
        ]
    )
    features, pair = lax.optimization_barrier((features, pair))
    dense, bias, own, *sent = call(
        functools.partial(first_kernel, sections),
        [
            shape((block_rows, plane_rows), BF16),
            shape((1, width), F32),
            shape((block_rows, width), F32),
        ]
        + [shape((block_rows, width), BF16)] * (sections - 1),
        [SMEM] * 3 + [HBM, VMEM, VMEM],
        [
            pltpu.VMEM((plane_rows, width), F32),
            pltpu.SemaphoreType.DMA((slot_total,)),
        ],
        flops=2 * plane_rows * block_rows * width,
        limit=51 * 1024 * 1024,
    )(src_slots, dst_slots, slot_counts, adj_values, features, bias_vector[None, :])
    pair, *sent = lax.optimization_barrier((pair, *sent))
    pair = lax.ppermute(pair, ("row", "rep"), list(zip(source, here)))
    received = [swap(value, k) for k, value in enumerate(sent, 1)]

    own, *sent = call(
        functools.partial(block_kernel, sections),
        [shape((share, width), F32)] + [shape((share, width), BF16)] * (replicas - 1),
        [VMEM] * sections,
        [pltpu.VMEM((block_rows, width), F32)],
    )(own, *received)
    received = [swap(value, k * sections) for k, value in enumerate(sent, 1)]

    act, *letters = call(
        functools.partial(middle_kernel, norm, sections, replicas, parts),
        [shape((share, width), BF16)]
        + [shape((share + sections * rows, width), BF16)] * replicas,
        [VMEM] * (replicas + 4),
        [pltpu.VMEM((width, share), BF16)] * 2,
    )(own, *received, pair, w_self, w_neigh, bias)
    letters = letters[:1] + [swap(v, k * sections) for k, v in enumerate(letters[1:], 1)]

    act = lax.ppermute(act, ("row", "rep"), list(zip(here, level)))
    act, *letters = lax.optimization_barrier((act, *letters))
    span = sections * rows
    grads, terms = call(
        functools.partial(terms_kernel, share),
        [shape((block_rows, width), BF16), shape((2 * span + 16, width), BF16)],
        [VMEM] * replicas,
        [pltpu.VMEM((replicas, span, width), BF16)],
        flops=2 * block_rows * width * (2 * span + 16),
    )(*letters)
    packs = [grads] + [swap(grads, k) for k in range(1, sections)]
    terms, act = lax.optimization_barrier((terms, act))
    act = lax.ppermute(act, ("row", "rep"), list(zip(here, inside)))
    terms = [terms] + [swap_rep(terms, k) for k in range(1, replicas)]

    sent = call(
        functools.partial(back_kernel, norm, sections, replicas),
        [shape((share, width), BF16)] * replicas,
        [VMEM] * (sections + 3),
        [pltpu.VMEM((plane_rows, width), BF16), pltpu.VMEM((block_rows, width), F32)],
        flops=2 * plane_rows * width * (block_rows + width),
    )(*packs, dense, w_self, w_neigh)
    received = [swap_rep(value, k) for k, value in enumerate(sent[1:], 1)]
    act, received[0], *terms = lax.optimization_barrier((act, received[0], *terms))
    (terms,) = call(
        level_kernel, [shape((2 * span + 16, width), BF16)], [VMEM] * replicas
    )(*terms)
    summed, grad_bias = call(
        functools.partial(chip_kernel, factor),
        [shape((2 * span, width), BF16), shape((1, width), F32)],
        [VMEM] * sections,
    )(terms, *[swap(terms, k) for k in range(1, sections)])
    pieces = [summed] + [swap(summed, k * sections) for k in range(1, parts // sections)]
    grad_features, activations = call(
        last_kernel, [shape((share, width), BF16)] * 2, [VMEM] * (replicas + 1)
    )(sent[0], *received, act)
    grad_self, grad_neigh = call(
        functools.partial(collect_kernel, sections, factor),
        [shape((width, width), F32)] * 2,
        [VMEM] * len(pieces),
    )(*pieces)
    return activations, grad_features, grad_self, grad_neigh, grad_bias[0]


def solution(mesh):
    placed = (
        P("row", None),
        P(),
        P(),
        P(),
        P("row", None),
        P("row", "rep", None, None, None),
        P("row", "rep", None),
        P("row", "rep", None),
        P("row", "rep"),
    )
    return jax.shard_map(
        shards,
        mesh=mesh,
        in_specs=placed,
        out_specs=(P(("row", "rep"), None), P(("row", "rep"), None), P(), P(), P()),
        check_vma=False,
    )
```

```python
import functools
import math

import jax
import jax.numpy as jnp
from jax import lax
from jax.experimental import pallas as pl
from jax.experimental.pallas import tpu as pltpu
from jax.sharding import PartitionSpec as P

F32 = jnp.float32
BF16 = jnp.bfloat16
VMEM = pl.BlockSpec(memory_space=pltpu.VMEM)
HBM = pl.BlockSpec(memory_space=pltpu.HBM)
SMEM = pl.BlockSpec(memory_space=pltpu.SMEM)
LIMIT = 16 * 1024 * 1024


def call(body, outs, ins, scratch=(), flops=0, limit=LIMIT):
    size = sum(math.prod(out.shape) * out.dtype.itemsize for out in outs)
    kernel = pl.pallas_call(
        body,
        out_shape=outs,
        in_specs=ins,
        out_specs=[VMEM] * len(outs),
        scratch_shapes=list(scratch),
        compiler_params=pltpu.CompilerParams(vmem_limit_bytes=limit),
        cost_estimate=pl.CostEstimate(flops=flops, bytes_accessed=2 * size, transcendentals=0),
    )
    return lambda *operands: list(kernel(*operands))


def shape(dims, kind):
    return jax.ShapeDtypeStruct(tuple(dims), kind)


def swap(value, step):
    return lax.ppermute(value, "row", [(i, i ^ step) for i in range(lax.axis_size("row"))])


def swap_all(values, sections):
    order = sorted(range(1, len(values) + 1), key=lambda k: (-bin(k).count("1"), k))
    came = {k: swap(values[k - 1], k * sections) for k in order}
    return [came[k] for k in range(1, len(values) + 1)]


def swap_rep(value, step):
    return lax.ppermute(value, "rep", [(i, i ^ step) for i in range(lax.axis_size("rep"))])


def contract(left, right, left_dim, right_dim):
    return lax.dot_general(
        left, right, (((left_dim,), (right_dim,)), ((), ())), preferred_element_type=F32
    )


def tree_sum(parts):
    while len(parts) > 1:
        parts = [parts[i] + parts[i + 1] for i in range(0, len(parts), 2)]
    return parts[0]


def place_of(sections):
    me = lax.axis_index("row")
    return me // sections, me % sections


def turn(c, replicas):
    out, bits = 0, replicas.bit_length() - 1
    for i in range(bits):
        out = out | ((c >> i) & 1) << (bits - 1 - i)
    return out


def tile_of(sections):
    return place_of(sections)[0] ^ lax.axis_index("rep")


def masks(first, count):
    first = first or 1
    return [first] + [m for m in range(1, count) if m != first]


def mask_of(first, j):
    first = jnp.where(first == 0, 1, first)
    return first if j == 0 else jnp.where(j >= first, j + 1, j)


def piece_of(ref, index, span):
    return ref[pl.ds(pl.multiple_of(index * span, span), span), :]


def first_kernel(sections, src, dst, count, tiles, field, bias, dense, bias_out, own, *rest):
    others, (total, sems) = rest[:-2], rest[-2:]
    size = tiles.shape[-1]
    block_rows = field.shape[0]
    _, s = place_of(sections)
    live = count[0, 0]
    dense[...] = jnp.zeros_like(dense)

    def tile_copy(e):
        row = pl.multiple_of(dst[0, 0, e] * size, size)
        col = pl.multiple_of(src[0, 0, e] * size, size)
        target = dense.at[pl.ds(row, size), pl.ds(col, size)]
        return pltpu.make_async_copy(tiles.at[0, 0, e], target, sems.at[e])

    lax.fori_loop(0, live, lambda e, carry: (tile_copy(e).start(), carry)[1], 0)
    bias_out[...] = bias[...]
    lax.fori_loop(0, live, lambda e, carry: (tile_copy(e).wait(), carry)[1], 0)
    for t in range(dense.shape[1] // size):
        cols = pl.ds(t * size, size)
        total[cols, :] = contract(dense[:, cols], field[...], 0, 0)
    own[...] = piece_of(total, s, block_rows)
    for k, out in enumerate(others, 1):
        out[...] = piece_of(total, s ^ k, block_rows).astype(BF16)


def block_kernel(sections, *refs):
    parts, own, others, total = refs[:sections], refs[sections], refs[sections + 1 : -1], refs[-1]
    share = own.shape[0]
    tile = tile_of(sections)
    value = parts[0][...]
    for ref in parts[1:]:
        value = value + ref[...].astype(F32)
    total[...] = value
    own[...] = piece_of(total, tile, share)
    for k, out in enumerate(others, 1):
        out[...] = piece_of(total, tile ^ k, share).astype(BF16)


def middle_kernel(norm, sections, replicas, parts, *refs):
    tiles, (pair, w_self, w_neigh, bias, act) = refs[:replicas], refs[replicas : replicas + 5]
    letters, (turned_f, turned_a) = refs[replicas + 5 : -2], refs[-2:]
    share, width = act.shape
    rows = width // parts
    q, _ = place_of(sections)
    total = tiles[0][...]
    for ref in tiles[1:]:
        total = total + ref[...].astype(F32)
    aggregate = (total * norm).astype(BF16)
    field = pair[pl.ds(0, share), :]
    pre = contract(field, w_self[...], 1, 0) + contract(aggregate, w_neigh[...], 1, 0)
    pre = pre + bias[...]
    slope = jnp.exp(jnp.minimum(pre, 0.0))
    act[...] = jnp.where(pre > 0.0, pre, slope - 1.0).astype(BF16)
    grad = (pair[pl.ds(share, share), :].astype(F32) * slope).astype(BF16)
    turned_f[...] = field.T
    turned_a[...] = aggregate.T
    span = sections * rows
    for k, letter in enumerate(letters):
        slot = (q ^ k) % (parts // sections)
        letter[pl.ds(0, share), :] = grad
        letter[pl.ds(share, span), pl.ds(0, share)] = piece_of(turned_f, slot, span)
        letter[pl.ds(share, span), pl.ds(128, share)] = piece_of(turned_a, slot, span)


def pack_kernel(sections, share, rows, *refs):
    letters, packs = refs[:-sections], refs[-sections:]
    _, s = place_of(sections)
    tile = tile_of(sections)
    block_rows = len(letters) * share
    for k, letter in enumerate(letters):
        here = pl.ds(pl.multiple_of((tile ^ k) * share, share), share)
        turned = pl.ds(pl.multiple_of(block_rows + (tile ^ k) * rows, rows), rows)
        for m, pack in enumerate(packs):
            first = pl.multiple_of(share + (s ^ m) * rows, 16)
            pack[here, :] = letter[pl.ds(0, share), :]
            pack[turned, :] = letter[pl.ds(first, rows), :]


def terms_kernel(share, rows, *refs):
    packs, out = refs[:-1], refs[-1]
    width = out.shape[1]
    replicas = packs[0].shape[0] // (share + rows)
    ones = jnp.ones((16, share), BF16)
    sums = []
    for pack in packs:
        total = jnp.zeros((2 * rows + 16, width), F32)
        for i in range(replicas):
            turned = pl.ds(replicas * share + i * rows, rows)
            field, aggregate = pack[turned, pl.ds(0, share)], pack[turned, pl.ds(128, share)]
            left = jnp.concatenate([field, aggregate, ones])
            total += contract(left, pack[pl.ds(i * share, share), :], 1, 0)
        sums.append(total)
    total = tree_sum(sums)
    tail = total[2 * rows :]
    high = tail.astype(BF16).astype(F32)
    line = lax.broadcasted_iota(jnp.int32, tail.shape, 0)
    out[pl.ds(0, 2 * rows), :] = total[: 2 * rows].astype(BF16)
    out[pl.ds(2 * rows, 16), :] = jnp.where(line == 0, high, tail - high).astype(BF16)


def back_kernel(norm, sections, replicas, *refs):
    packs, (dense, w_self, w_neigh, act) = refs[:sections], refs[sections : sections + 4]
    own, outs, (message, total) = refs[sections + 4], refs[sections + 5 : -2], refs[-2:]
    me_rep = lax.axis_index("rep")
    q, s = place_of(sections)
    block_rows = dense.shape[0]
    share = block_rows // replicas
    for k, pack in enumerate(packs):
        here = pl.ds(pl.multiple_of((s ^ k) * block_rows, block_rows), block_rows)
        grad = pack[pl.ds(0, block_rows), :]
        message[here, :] = contract(grad, w_neigh[...], 1, 1).astype(BF16)
    total[...] = contract(dense[...], message[...], 1, 0) * norm

    @pl.when(me_rep == q)
    def _():
        total[...] += contract(packs[0][pl.ds(0, block_rows), :], w_self[...], 1, 1)

    own[...] = piece_of(total, me_rep, share).astype(BF16)
    for j, out in enumerate(outs):
        out[pl.ds(0, share), :] = piece_of(total, me_rep ^ mask_of(q, j), share).astype(BF16)
    outs[0][pl.ds(share, share), :] = act[...]


def level_kernel(rows, factor, *refs):
    parts, (bias, summed) = refs[:-2], refs[-2:]
    terms = tree_sum([ref[...].astype(F32) for ref in parts])
    tail = terms[2 * rows : 2 * rows + 8]
    bias[...] = (tail[0:1] + tail[1:2]) * factor
    summed[...] = terms[: 2 * rows].astype(BF16)


def pick_kernel(sections, act, came, out):
    q, _ = place_of(sections)
    share = act.shape[0]
    arrived = came[pl.ds(share, share), :].astype(F32)
    out[...] = jnp.where(q == 0, act[...].astype(F32), arrived).astype(BF16)


def last_kernel(*refs):
    parts, (act, grad_features, activations) = refs[:-3], refs[-3:]
    here = pl.ds(0, grad_features.shape[0])
    grad_features[...] = tree_sum([ref[here, :].astype(F32) for ref in parts]).astype(BF16)
    activations[...] = act[...]


def join_kernel(sections, *refs):
    pieces, out = refs[:-1], refs[-1]
    span = pieces[0].shape[0]
    q, _ = place_of(sections)
    for k, piece in enumerate(pieces):
        slot = (q % len(pieces)) ^ k
        out[pl.ds(pl.multiple_of(slot * span, 16), span), :] = piece[...]


def collect_kernel(rows, factor, *refs):
    joined, (grad_self, grad_neigh) = refs[:-2], refs[-2:]
    sections = len(joined)
    _, s = place_of(sections)
    for k, ref in enumerate(joined):
        for j in range(ref.shape[0] // (2 * rows)):
            place = pl.ds(pl.multiple_of((j * sections + (s ^ k)) * rows, rows), rows)
            base = j * 2 * rows
            grad_self[place, :] = ref[pl.ds(base, rows), :].astype(F32) * factor
            grad_neigh[place, :] = ref[pl.ds(base + rows, rows), :].astype(F32) * factor


def shards(
    features, w_self, w_neigh, bias_vector, cotangent, adj_values, src_slots, dst_slots, slot_counts
):
    block_rows, width = features.shape
    blocks, replicas = lax.axis_size("row"), lax.axis_size("rep")
    sections = blocks // replicas
    share = block_rows // replicas
    slot_total, size = adj_values.shape[2], adj_values.shape[-1]
    norm = 1.0 / math.sqrt(slot_total * replicas / (block_rows // size))
    factor = 1.0 / math.sqrt(block_rows * blocks)
    parts = min(blocks, width // 16)
    rows = width // parts

    def flat(q, s, c):
        return (q * sections + s) * replicas + c

    places = [
        (q, s, c) for q in range(replicas) for s in range(sections) for c in range(replicas)
    ]
    here = [flat(q, s, c) for q, s, c in places]
    source = [flat(c, s, q ^ turn(c, replicas)) for q, s, c in places]
    inside = [flat(q ^ c, s, c) for q, s, c in places]

    def swap_level(value, j):
        level = [flat(q, s, c ^ masks(q, replicas)[j]) for q, s, c in places]
        return lax.ppermute(value, ("row", "rep"), list(zip(here, level)))

    plane_rows = sections * block_rows
    chip, plane = place_of(sections)[0], lax.axis_index("rep")
    offset = (plane ^ turn(chip, replicas) ^ chip) * share
    pair = jnp.concatenate(
        [
            lax.dynamic_slice_in_dim(features, offset, share, 0),
            lax.dynamic_slice_in_dim(cotangent, offset, share, 0),
        ]
    )
    dense, bias, own, *sent = call(
        functools.partial(first_kernel, sections),
        [
            shape((block_rows, plane_rows), BF16),
            shape((1, width), F32),
            shape((block_rows, width), F32),
        ]
        + [shape((block_rows, width), BF16)] * (sections - 1),
        [SMEM] * 3 + [HBM, VMEM, VMEM],
        [
            pltpu.VMEM((plane_rows, width), F32),
            pltpu.SemaphoreType.DMA((slot_total,)),
        ],
        flops=2 * plane_rows * block_rows * width,
        limit=51 * 1024 * 1024,
    )(src_slots, dst_slots, slot_counts, adj_values, features, bias_vector[None, :])
    pair, *sent = lax.optimization_barrier((pair, *sent))
    pair = lax.ppermute(pair, ("row", "rep"), list(zip(source, here)))
    received = [swap(value, k) for k, value in enumerate(sent, 1)]

    own, *sent = call(
        functools.partial(block_kernel, sections),
        [shape((share, width), F32)] + [shape((share, width), BF16)] * (replicas - 1),
        [VMEM] * sections,
        [pltpu.VMEM((block_rows, width), F32)],
    )(own, *received)
    received = swap_all(sent, sections)

    act, *letters = call(
        functools.partial(middle_kernel, norm, sections, replicas, parts),
        [shape((share, width), BF16)]
        + [shape((share + sections * rows, width), BF16)] * replicas,
        [VMEM] * (replicas + 4),
        [pltpu.VMEM((width, share), BF16)] * 2,
    )(own, *received, pair, w_self, w_neigh, bias)
    letters = letters[:1] + swap_all(letters[1:], sections)

    packs = call(
        functools.partial(pack_kernel, sections, share, rows),
        [shape((replicas * (share + rows), width), BF16)] * sections,
        [VMEM] * replicas,
    )(*letters)
    packs = packs[:1] + [swap(value, k) for k, value in enumerate(packs[1:], 1)]

    (terms,) = call(
        functools.partial(terms_kernel, share, rows),
        [shape((2 * rows + 16, width), BF16)],
        [VMEM] * sections,
        flops=2 * plane_rows * width * (2 * rows + 16),
    )(*packs)
    terms, *packs = lax.optimization_barrier((terms, *packs))
    terms = [terms] + [swap_rep(terms, k) for k in range(1, replicas)]

    sent = call(
        functools.partial(back_kernel, norm, sections, replicas),
        [shape((share, width), BF16), shape((2 * share, width), BF16)]
        + [shape((share, width), BF16)] * (replicas - 2),
        [VMEM] * (sections + 4),
        [pltpu.VMEM((plane_rows, width), BF16), pltpu.VMEM((block_rows, width), F32)],
        flops=2 * plane_rows * width * (block_rows + width),
    )(*packs, dense, w_self, w_neigh, act)
    received = [swap_level(value, j) for j, value in enumerate(sent[2:], 1)]
    _, *terms = lax.optimization_barrier((sent[0], *terms))
    grad_bias, summed = call(
        functools.partial(level_kernel, rows, factor),
        [shape((1, width), F32), shape((2 * rows, width), BF16)],
        [VMEM] * replicas,
    )(*terms)
    summed, loaded = lax.optimization_barrier((summed, sent[1]))
    loaded = swap_level(loaded, 0)
    (act,) = call(
        functools.partial(pick_kernel, sections),
        [shape((share, width), BF16)],
        [VMEM] * 2,
    )(act, loaded)
    act = lax.ppermute(act, ("row", "rep"), list(zip(here, inside)))
    spread = parts // sections
    pieces = [summed] + swap_all([summed] * (spread - 1), sections)
    pieces[-1], *received = lax.optimization_barrier((pieces[-1], *received))
    (joined,) = call(
        functools.partial(join_kernel, sections),
        [shape((spread * 2 * rows, width), BF16)],
        [VMEM] * spread,
    )(*pieces)
    joined = [joined] + [swap(joined, k) for k in range(1, sections)]
    grad_self, grad_neigh = call(
        functools.partial(collect_kernel, rows, factor),
        [shape((width, width), F32)] * 2,
        [VMEM] * sections,
    )(*joined)
    grad_features, activations = call(
        last_kernel, [shape((share, width), BF16)] * 2, [VMEM] * (replicas + 1)
    )(sent[0], loaded, *received, act)
    return activations, grad_features, grad_self, grad_neigh, grad_bias[0]


def solution(mesh):
    placed = (
        P("row", None),
        P(),
        P(),
        P(),
        P("row", None),
        P("row", "rep", None, None, None),
        P("row", "rep", None),
        P("row", "rep", None),
        P("row", "rep"),
    )
    return jax.shard_map(
        shards,
        mesh=mesh,
        in_specs=placed,
        out_specs=(P(("row", "rep"), None), P(("row", "rep"), None), P(), P(), P()),
        check_vma=False,
    )
```

```python
import functools
import math

import jax
import jax.numpy as jnp
from jax import lax
from jax.experimental import pallas as pl
from jax.experimental.pallas import tpu as pltpu
from jax.sharding import PartitionSpec as P

F32 = jnp.float32
BF16 = jnp.bfloat16
VMEM = pl.BlockSpec(memory_space=pltpu.VMEM)
HBM = pl.BlockSpec(memory_space=pltpu.HBM)
SMEM = pl.BlockSpec(memory_space=pltpu.SMEM)
LIMIT = 16 * 1024 * 1024


def call(body, outs, ins, scratch=(), flops=0, limit=LIMIT):
    size = sum(math.prod(out.shape) * out.dtype.itemsize for out in outs)
    kernel = pl.pallas_call(
        body,
        out_shape=outs,
        in_specs=ins,
        out_specs=[VMEM] * len(outs),
        scratch_shapes=list(scratch),
        compiler_params=pltpu.CompilerParams(vmem_limit_bytes=limit),
        cost_estimate=pl.CostEstimate(flops=flops, bytes_accessed=2 * size, transcendentals=0),
    )
    return lambda *operands: list(kernel(*operands))


def shape(dims, kind):
    return jax.ShapeDtypeStruct(tuple(dims), kind)


def swap(value, step):
    return lax.ppermute(value, "row", [(i, i ^ step) for i in range(lax.axis_size("row"))])


def swap_rep(value, step):
    return lax.ppermute(value, "rep", [(i, i ^ step) for i in range(lax.axis_size("rep"))])


def contract(left, right, left_dim, right_dim):
    return lax.dot_general(
        left, right, (((left_dim,), (right_dim,)), ((), ())), preferred_element_type=F32
    )


def tree_sum(parts):
    while len(parts) > 1:
        parts = [parts[i] + parts[i + 1] for i in range(0, len(parts), 2)]
    return parts[0]


def place_of(sections):
    me = lax.axis_index("row")
    return me // sections, me % sections


def turn(c, replicas):
    out, bits = 0, replicas.bit_length() - 1
    for i in range(bits):
        out = out | ((c >> i) & 1) << (bits - 1 - i)
    return out


def tile_of(sections):
    return place_of(sections)[0] ^ lax.axis_index("rep")


def piece_of(ref, index, span):
    return ref[pl.ds(pl.multiple_of(index * span, span), span), :]


def first_kernel(sections, src, dst, count, tiles, field, bias, dense, bias_out, own, *rest):
    others, (total, sems) = rest[:-2], rest[-2:]
    size = tiles.shape[-1]
    block_rows = field.shape[0]
    _, s = place_of(sections)
    live = count[0, 0]
    dense[...] = jnp.zeros_like(dense)

    def tile_copy(e):
        row = pl.multiple_of(dst[0, 0, e] * size, size)
        col = pl.multiple_of(src[0, 0, e] * size, size)
        target = dense.at[pl.ds(row, size), pl.ds(col, size)]
        return pltpu.make_async_copy(tiles.at[0, 0, e], target, sems.at[e])

    lax.fori_loop(0, live, lambda e, carry: (tile_copy(e).start(), carry)[1], 0)
    bias_out[...] = bias[...]
    lax.fori_loop(0, live, lambda e, carry: (tile_copy(e).wait(), carry)[1], 0)
    for t in range(dense.shape[1] // size):
        cols = pl.ds(t * size, size)
        total[cols, :] = contract(dense[:, cols], field[...], 0, 0)
    own[...] = piece_of(total, s, block_rows)
    for k, out in enumerate(others, 1):
        out[...] = piece_of(total, s ^ k, block_rows).astype(BF16)


def block_kernel(sections, *refs):
    parts, own, others, total = refs[:sections], refs[sections], refs[sections + 1 : -1], refs[-1]
    share = own.shape[0]
    tile = tile_of(sections)
    value = parts[0][...]
    for ref in parts[1:]:
        value = value + ref[...].astype(F32)
    total[...] = value
    own[...] = piece_of(total, tile, share)
    for k, out in enumerate(others, 1):
        out[...] = piece_of(total, tile ^ k, share).astype(BF16)


def middle_kernel(norm, sections, replicas, parts, *refs):
    tiles, (pair, w_self, w_neigh, bias, act) = refs[:replicas], refs[replicas : replicas + 5]
    letters, (turned_f, turned_a) = refs[replicas + 5 : -2], refs[-2:]
    share, width = act.shape
    rows = width // parts
    q, _ = place_of(sections)
    total = tiles[0][...]
    for ref in tiles[1:]:
        total = total + ref[...].astype(F32)
    aggregate = (total * norm).astype(BF16)
    field = pair[pl.ds(0, share), :]
    pre = contract(field, w_self[...], 1, 0) + contract(aggregate, w_neigh[...], 1, 0)
    pre = pre + bias[...]
    slope = jnp.exp(jnp.minimum(pre, 0.0))
    act[...] = jnp.where(pre > 0.0, pre, slope - 1.0).astype(BF16)
    grad = (pair[pl.ds(share, share), :].astype(F32) * slope).astype(BF16)
    turned_f[...] = field.T
    turned_a[...] = aggregate.T
    span = sections * rows
    for k, letter in enumerate(letters):
        slot = (q ^ k) % (parts // sections)
        letter[pl.ds(0, share), :] = grad
        letter[pl.ds(share, span), pl.ds(0, share)] = piece_of(turned_f, slot, span)
        letter[pl.ds(share, span), pl.ds(128, share)] = piece_of(turned_a, slot, span)


def pack_kernel(sections, share, rows, *refs):
    letters, packs = refs[:1] + refs[1:-sections][::-1], refs[-sections:]
    _, s = place_of(sections)
    tile = tile_of(sections)
    block_rows = len(letters) * share
    for k, letter in enumerate(letters):
        here = pl.ds(pl.multiple_of((tile ^ k) * share, share), share)
        turned = pl.ds(pl.multiple_of(block_rows + (tile ^ k) * rows, rows), rows)
        for m, pack in enumerate(packs):
            first = pl.multiple_of(share + (s ^ m) * rows, 16)
            pack[here, :] = letter[pl.ds(0, share), :]
            pack[turned, :] = letter[pl.ds(first, rows), :]


def terms_kernel(share, rows, *refs):
    packs, out = refs[:-1], refs[-1]
    width = out.shape[1]
    replicas = packs[0].shape[0] // (share + rows)
    ones = jnp.ones((16, share), BF16)
    sums = []
    for pack in packs:
        total = jnp.zeros((2 * rows + 16, width), F32)
        for i in range(replicas):
            turned = pl.ds(replicas * share + i * rows, rows)
            field, aggregate = pack[turned, pl.ds(0, share)], pack[turned, pl.ds(128, share)]
            left = jnp.concatenate([field, aggregate, ones])
            total += contract(left, pack[pl.ds(i * share, share), :], 1, 0)
        sums.append(total)
    total = tree_sum(sums)
    tail = total[2 * rows :]
    high = tail.astype(BF16).astype(F32)
    line = lax.broadcasted_iota(jnp.int32, tail.shape, 0)
    out[pl.ds(0, 2 * rows), :] = total[: 2 * rows].astype(BF16)
    out[pl.ds(2 * rows, 16), :] = jnp.where(line == 0, high, tail - high).astype(BF16)


def back_kernel(norm, sections, replicas, *refs):
    packs, (dense, w_self, w_neigh) = refs[:sections], refs[sections : sections + 3]
    outs, (message, total) = refs[sections + 3 : -2], refs[-2:]
    me_rep = lax.axis_index("rep")
    q, s = place_of(sections)
    block_rows = dense.shape[0]
    share = block_rows // replicas
    for k, pack in enumerate(packs):
        here = pl.ds(pl.multiple_of((s ^ k) * block_rows, block_rows), block_rows)
        grad = pack[pl.ds(0, block_rows), :]
        message[here, :] = contract(grad, w_neigh[...], 1, 1).astype(BF16)
    total[...] = contract(dense[...], message[...], 1, 0) * norm

    @pl.when(me_rep == q)
    def _():
        total[...] += contract(packs[0][pl.ds(0, block_rows), :], w_self[...], 1, 1)

    for k, out in enumerate(outs):
        out[...] = piece_of(total, me_rep ^ k, share).astype(BF16)


def level_kernel(rows, factor, *refs):
    parts, (bias, summed) = refs[:-2], refs[-2:]
    terms = tree_sum([ref[...].astype(F32) for ref in parts])
    tail = terms[2 * rows : 2 * rows + 8]
    bias[...] = (tail[0:1] + tail[1:2]) * factor
    summed[...] = terms[: 2 * rows].astype(BF16)


def last_kernel(*refs):
    parts, (act, grad_features, activations) = refs[:-3], refs[-3:]
    grad_features[...] = tree_sum([ref[...].astype(F32) for ref in parts]).astype(BF16)
    activations[...] = act[...]


def join_kernel(sections, *refs):
    pieces, out = refs[:-1], refs[-1]
    span = pieces[0].shape[0]
    q, _ = place_of(sections)
    for k, piece in enumerate(pieces):
        slot = (q % len(pieces)) ^ k
        out[pl.ds(pl.multiple_of(slot * span, 16), span), :] = piece[...]


def collect_kernel(rows, factor, *refs):
    joined, (grad_self, grad_neigh) = refs[:-2], refs[-2:]
    sections = len(joined)
    _, s = place_of(sections)
    for k, ref in enumerate(joined):
        for j in range(ref.shape[0] // (2 * rows)):
            place = pl.ds(pl.multiple_of((j * sections + (s ^ k)) * rows, rows), rows)
            base = j * 2 * rows
            grad_self[place, :] = ref[pl.ds(base, rows), :].astype(F32) * factor
            grad_neigh[place, :] = ref[pl.ds(base + rows, rows), :].astype(F32) * factor


def shards(
    features, w_self, w_neigh, bias_vector, cotangent, adj_values, src_slots, dst_slots, slot_counts
):
    block_rows, width = features.shape
    blocks, replicas = lax.axis_size("row"), lax.axis_size("rep")
    sections = blocks // replicas
    share = block_rows // replicas
    slot_total, size = adj_values.shape[2], adj_values.shape[-1]
    norm = 1.0 / math.sqrt(slot_total * replicas / (block_rows // size))
    factor = 1.0 / math.sqrt(block_rows * blocks)
    parts = min(blocks, width // 16)
    rows = width // parts

    def flat(q, s, c):
        return (q * sections + s) * replicas + c

    places = [
        (q, s, c) for q in range(replicas) for s in range(sections) for c in range(replicas)
    ]
    here = [flat(q, s, c) for q, s, c in places]
    source = [flat(c, s, q ^ turn(c, replicas)) for q, s, c in places]
    level = [flat(q, s, q ^ c) for q, s, c in places]
    inside = [flat(q ^ c, s, c) for q, s, c in places]

    plane_rows = sections * block_rows
    chip, plane = place_of(sections)[0], lax.axis_index("rep")
    offset = (plane ^ turn(chip, replicas) ^ chip) * share
    pair = jnp.concatenate(
        [
            lax.dynamic_slice_in_dim(features, offset, share, 0),
            lax.dynamic_slice_in_dim(cotangent, offset, share, 0),
        ]
    )
    features, pair = lax.optimization_barrier((features, pair))
    dense, bias, own, *sent = call(
        functools.partial(first_kernel, sections),
        [
            shape((block_rows, plane_rows), BF16),
            shape((1, width), F32),
            shape((block_rows, width), F32),
        ]
        + [shape((block_rows, width), BF16)] * (sections - 1),
        [SMEM] * 3 + [HBM, VMEM, VMEM],
        [
            pltpu.VMEM((plane_rows, width), F32),
            pltpu.SemaphoreType.DMA((slot_total,)),
        ],
        flops=2 * plane_rows * block_rows * width,
        limit=51 * 1024 * 1024,
    )(src_slots, dst_slots, slot_counts, adj_values, features, bias_vector[None, :])
    pair, *sent = lax.optimization_barrier((pair, *sent))
    pair = lax.ppermute(pair, ("row", "rep"), list(zip(source, here)))
    received = [swap(value, k) for k, value in enumerate(sent, 1)]

    own, *sent = call(
        functools.partial(block_kernel, sections),
        [shape((share, width), F32)] + [shape((share, width), BF16)] * (replicas - 1),
        [VMEM] * sections,
        [pltpu.VMEM((block_rows, width), F32)],
    )(own, *received)
    received = [swap(value, k * sections) for k, value in enumerate(sent, 1)]

    act, *letters = call(
        functools.partial(middle_kernel, norm, sections, replicas, parts),
        [shape((share, width), BF16)]
        + [shape((share + sections * rows, width), BF16)] * replicas,
        [VMEM] * (replicas + 4),
        [pltpu.VMEM((width, share), BF16)] * 2,
    )(own, *received[::-1], pair, w_self, w_neigh, bias)
    letters = letters[:1] + [swap(v, k * sections) for k, v in enumerate(letters[1:], 1)]

    packs = call(
        functools.partial(pack_kernel, sections, share, rows),
        [shape((replicas * (share + rows), width), BF16)] * sections,
        [VMEM] * replicas,
    )(letters[0], *letters[:0:-1])
    packs = packs[:1] + [swap(value, k) for k, value in enumerate(packs[1:], 1)]

    (terms,) = call(
        functools.partial(terms_kernel, share, rows),
        [shape((2 * rows + 16, width), BF16)],
        [VMEM] * sections,
        flops=2 * plane_rows * width * (2 * rows + 16),
    )(*packs)
    terms, *packs = lax.optimization_barrier((terms, *packs))
    terms, act = lax.optimization_barrier((terms, act))
    act = lax.ppermute(act, ("row", "rep"), list(zip(here, level)))
    terms = [terms] + [swap_rep(terms, k) for k in range(1, replicas)]

    sent = call(
        functools.partial(back_kernel, norm, sections, replicas),
        [shape((share, width), BF16)] * replicas,
        [VMEM] * (sections + 3),
        [pltpu.VMEM((plane_rows, width), BF16), pltpu.VMEM((block_rows, width), F32)],
        flops=2 * plane_rows * width * (block_rows + width),
    )(*packs, dense, w_self, w_neigh)
    received = [swap_rep(value, k) for k, value in enumerate(sent[2:], 2)]
    _, *terms = lax.optimization_barrier((sent[0], *terms))
    grad_bias, summed = call(
        functools.partial(level_kernel, rows, factor),
        [shape((1, width), F32), shape((2 * rows, width), BF16)],
        [VMEM] * replicas,
    )(*terms)
    summed, act, near = lax.optimization_barrier((summed, act, sent[1]))
    near = swap_rep(near, 1)
    act = lax.ppermute(act, ("row", "rep"), list(zip(here, inside)))
    spread = parts // sections
    pieces = [summed] + [swap(summed, k * sections) for k in range(1, spread)]
    pieces[-1], act, near, *received = lax.optimization_barrier(
        (pieces[-1], act, near, *received)
    )
    (joined,) = call(
        functools.partial(join_kernel, sections),
        [shape((spread * 2 * rows, width), BF16)],
        [VMEM] * spread,
    )(*pieces)
    joined = [joined] + [swap(joined, k) for k in range(1, sections)]
    grad_self, grad_neigh = call(
        functools.partial(collect_kernel, rows, factor),
        [shape((width, width), F32)] * 2,
        [VMEM] * sections,
    )(*joined)
    grad_features, activations = call(
        last_kernel, [shape((share, width), BF16)] * 2, [VMEM] * (replicas + 1)
    )(sent[0], near, *received, act)
    return activations, grad_features, grad_self, grad_neigh, grad_bias[0]


def solution(mesh):
    placed = (
        P("row", None),
        P(),
        P(),
        P(),
        P("row", None),
        P("row", "rep", None, None, None),
        P("row", "rep", None),
        P("row", "rep", None),
        P("row", "rep"),
    )
    return jax.shard_map(
        shards,
        mesh=mesh,
        in_specs=placed,
        out_specs=(P(("row", "rep"), None), P(("row", "rep"), None), P(), P(), P()),
        check_vma=False,
    )
```

```python
import functools
import math

import jax
import jax.numpy as jnp
from jax import lax
from jax.experimental import pallas as pl
from jax.experimental.pallas import tpu as pltpu
from jax.sharding import PartitionSpec as P

F32 = jnp.float32
BF16 = jnp.bfloat16
VMEM = pl.BlockSpec(memory_space=pltpu.VMEM)
HBM = pl.BlockSpec(memory_space=pltpu.HBM)
SMEM = pl.BlockSpec(memory_space=pltpu.SMEM)
LIMIT = 16 * 1024 * 1024


def call(body, outs, ins, scratch=(), flops=0, limit=LIMIT):
    size = sum(math.prod(out.shape) * out.dtype.itemsize for out in outs)
    kernel = pl.pallas_call(
        body,
        out_shape=outs,
        in_specs=ins,
        out_specs=[VMEM] * len(outs),
        scratch_shapes=list(scratch),
        compiler_params=pltpu.CompilerParams(vmem_limit_bytes=limit),
        cost_estimate=pl.CostEstimate(flops=flops, bytes_accessed=2 * size, transcendentals=0),
    )
    return lambda *operands: list(kernel(*operands))


def shape(dims, kind):
    return jax.ShapeDtypeStruct(tuple(dims), kind)


def swap(value, step):
    return lax.ppermute(value, "row", [(i, i ^ step) for i in range(lax.axis_size("row"))])


def swap_rep(value, step):
    return lax.ppermute(value, "rep", [(i, i ^ step) for i in range(lax.axis_size("rep"))])


def contract(left, right, left_dim, right_dim):
    return lax.dot_general(
        left, right, (((left_dim,), (right_dim,)), ((), ())), preferred_element_type=F32
    )


def tree_sum(parts):
    while len(parts) > 1:
        parts = [parts[i] + parts[i + 1] for i in range(0, len(parts), 2)]
    return parts[0]


def place_of(sections):
    me = lax.axis_index("row")
    return me // sections, me % sections


def turn(c, replicas):
    out, bits = 0, replicas.bit_length() - 1
    for i in range(bits):
        out = out | ((c >> i) & 1) << (bits - 1 - i)
    return out


def tile_of(sections):
    return place_of(sections)[0] ^ lax.axis_index("rep")


def masks(first, count):
    first = first or 1
    return [first] + [m for m in range(1, count) if m != first]


def mask_of(first, j):
    first = jnp.where(first == 0, 1, first)
    return first if j == 0 else jnp.where(j >= first, j + 1, j)


def piece_of(ref, index, span):
    return ref[pl.ds(pl.multiple_of(index * span, span), span), :]


def first_kernel(sections, src, dst, count, tiles, field, bias, dense, bias_out, own, *rest):
    others, (total, sems) = rest[:-2], rest[-2:]
    size = tiles.shape[-1]
    block_rows = field.shape[0]
    _, s = place_of(sections)
    live = count[0, 0]
    dense[...] = jnp.zeros_like(dense)

    def tile_copy(e):
        row = pl.multiple_of(dst[0, 0, e] * size, size)
        col = pl.multiple_of(src[0, 0, e] * size, size)
        target = dense.at[pl.ds(row, size), pl.ds(col, size)]
        return pltpu.make_async_copy(tiles.at[0, 0, e], target, sems.at[e])

    lax.fori_loop(0, live, lambda e, carry: (tile_copy(e).start(), carry)[1], 0)
    bias_out[...] = bias[...]
    lax.fori_loop(0, live, lambda e, carry: (tile_copy(e).wait(), carry)[1], 0)
    for t in range(dense.shape[1] // size):
        cols = pl.ds(t * size, size)
        total[cols, :] = contract(dense[:, cols], field[...], 0, 0)
    own[...] = piece_of(total, s, block_rows)
    for k, out in enumerate(others, 1):
        out[...] = piece_of(total, s ^ k, block_rows).astype(BF16)


def block_kernel(sections, *refs):
    parts, own, others, total = refs[:sections], refs[sections], refs[sections + 1 : -1], refs[-1]
    share = own.shape[0]
    tile = tile_of(sections)
    value = parts[0][...]
    for ref in parts[1:]:
        value = value + ref[...].astype(F32)
    total[...] = value
    own[...] = piece_of(total, tile, share)
    for k, out in enumerate(others, 1):
        out[...] = piece_of(total, tile ^ k, share).astype(BF16)


def middle_kernel(norm, sections, replicas, parts, *refs):
    tiles, (pair, w_self, w_neigh, bias, act) = refs[:replicas], refs[replicas : replicas + 5]
    letters, (turned_f, turned_a) = refs[replicas + 5 : -2], refs[-2:]
    share, width = act.shape
    rows = width // parts
    q, _ = place_of(sections)
    total = tiles[0][...]
    for ref in tiles[1:]:
        total = total + ref[...].astype(F32)
    aggregate = (total * norm).astype(BF16)
    field = pair[pl.ds(0, share), :]
    pre = contract(field, w_self[...], 1, 0) + contract(aggregate, w_neigh[...], 1, 0)
    pre = pre + bias[...]
    slope = jnp.exp(jnp.minimum(pre, 0.0))
    act[...] = jnp.where(pre > 0.0, pre, slope - 1.0).astype(BF16)
    grad = (pair[pl.ds(share, share), :].astype(F32) * slope).astype(BF16)
    turned_f[...] = field.T
    turned_a[...] = aggregate.T
    span = sections * rows
    for k, letter in enumerate(letters):
        slot = (q ^ k) % (parts // sections)
        letter[pl.ds(0, share), :] = grad
        letter[pl.ds(share, span), pl.ds(0, share)] = piece_of(turned_f, slot, span)
        letter[pl.ds(share, span), pl.ds(128, share)] = piece_of(turned_a, slot, span)


def pack_kernel(sections, share, rows, *refs):
    letters, packs = refs[:-sections], refs[-sections:]
    _, s = place_of(sections)
    tile = tile_of(sections)
    block_rows = len(letters) * share
    for k, letter in enumerate(letters):
        here = pl.ds(pl.multiple_of((tile ^ k) * share, share), share)
        turned = pl.ds(pl.multiple_of(block_rows + (tile ^ k) * rows, rows), rows)
        for m, pack in enumerate(packs):
            first = pl.multiple_of(share + (s ^ m) * rows, 16)
            pack[here, :] = letter[pl.ds(0, share), :]
            pack[turned, :] = letter[pl.ds(first, rows), :]


def terms_kernel(share, rows, *refs):
    packs, (act, out, loaded) = refs[:-3], refs[-3:]
    width = out.shape[1]
    replicas = packs[0].shape[0] // (share + rows)
    ones = jnp.ones((16, share), BF16)
    sums = []
    for pack in packs:
        total = jnp.zeros((2 * rows + 16, width), F32)
        for i in range(replicas):
            turned = pl.ds(replicas * share + i * rows, rows)
            field, aggregate = pack[turned, pl.ds(0, share)], pack[turned, pl.ds(128, share)]
            left = jnp.concatenate([field, aggregate, ones])
            total += contract(left, pack[pl.ds(i * share, share), :], 1, 0)
        sums.append(total)
    total = tree_sum(sums)
    tail = total[2 * rows :]
    high = tail.astype(BF16).astype(F32)
    line = lax.broadcasted_iota(jnp.int32, tail.shape, 0)
    out[pl.ds(0, 2 * rows), :] = total[: 2 * rows].astype(BF16)
    out[pl.ds(2 * rows, 16), :] = jnp.where(line == 0, high, tail - high).astype(BF16)
    loaded[pl.ds(0, 2 * rows + 16), :] = out[...]
    loaded[pl.ds(2 * rows + 16, share), :] = act[...]


def back_kernel(norm, sections, replicas, *refs):
    packs, (dense, w_self, w_neigh) = refs[:sections], refs[sections : sections + 3]
    outs, (message, total) = refs[sections + 3 : -2], refs[-2:]
    me_rep = lax.axis_index("rep")
    q, s = place_of(sections)
    block_rows = dense.shape[0]
    share = block_rows // replicas
    for k, pack in enumerate(packs):
        here = pl.ds(pl.multiple_of((s ^ k) * block_rows, block_rows), block_rows)
        grad = pack[pl.ds(0, block_rows), :]
        message[here, :] = contract(grad, w_neigh[...], 1, 1).astype(BF16)
    total[...] = contract(dense[...], message[...], 1, 0) * norm

    @pl.when(me_rep == q)
    def _():
        total[...] += contract(packs[0][pl.ds(0, block_rows), :], w_self[...], 1, 1)

    for k, out in enumerate(outs):
        out[...] = piece_of(total, me_rep ^ k, share).astype(BF16)


def level_kernel(sections, rows, factor, *refs):
    parts, (act, bias, summed, act_out, sorted_parts) = refs[:-5], refs[-5:]
    q, _ = place_of(sections)
    me = lax.axis_index("rep")
    span = 2 * rows + 16
    sorted_parts[me] = parts[0][...]
    for j, part in enumerate(parts[1:]):
        sorted_parts[me ^ mask_of(q, j)] = part[pl.ds(0, span), :]
    terms = tree_sum([sorted_parts[c].astype(F32) for c in range(len(parts))])
    tail = terms[2 * rows : 2 * rows + 8]
    bias[...] = (tail[0:1] + tail[1:2]) * factor
    summed[...] = terms[: 2 * rows].astype(BF16)
    came = parts[1][pl.ds(span, act.shape[0]), :]
    act_out[...] = jnp.where(q == 0, act[...].astype(F32), came.astype(F32)).astype(BF16)


def last_kernel(*refs):
    parts, (act, grad_features, activations) = refs[:-3], refs[-3:]
    grad_features[...] = tree_sum([ref[...].astype(F32) for ref in parts]).astype(BF16)
    activations[...] = act[...]


def join_kernel(sections, *refs):
    pieces, out = refs[:-1], refs[-1]
    span = pieces[0].shape[0]
    q, _ = place_of(sections)
    for k, piece in enumerate(pieces):
        slot = (q % len(pieces)) ^ k
        out[pl.ds(pl.multiple_of(slot * span, 16), span), :] = piece[...]


def collect_kernel(rows, factor, *refs):
    joined, (grad_self, grad_neigh) = refs[:-2], refs[-2:]
    sections = len(joined)
    _, s = place_of(sections)
    for k, ref in enumerate(joined):
        for j in range(ref.shape[0] // (2 * rows)):
            place = pl.ds(pl.multiple_of((j * sections + (s ^ k)) * rows, rows), rows)
            base = j * 2 * rows
            grad_self[place, :] = ref[pl.ds(base, rows), :].astype(F32) * factor
            grad_neigh[place, :] = ref[pl.ds(base + rows, rows), :].astype(F32) * factor


def shards(
    features, w_self, w_neigh, bias_vector, cotangent, adj_values, src_slots, dst_slots, slot_counts
):
    block_rows, width = features.shape
    blocks, replicas = lax.axis_size("row"), lax.axis_size("rep")
    sections = blocks // replicas
    share = block_rows // replicas
    slot_total, size = adj_values.shape[2], adj_values.shape[-1]
    norm = 1.0 / math.sqrt(slot_total * replicas / (block_rows // size))
    factor = 1.0 / math.sqrt(block_rows * blocks)
    parts = min(blocks, width // 16)
    rows = width // parts

    def flat(q, s, c):
        return (q * sections + s) * replicas + c

    places = [
        (q, s, c) for q in range(replicas) for s in range(sections) for c in range(replicas)
    ]
    here = [flat(q, s, c) for q, s, c in places]
    source = [flat(c, s, q ^ turn(c, replicas)) for q, s, c in places]
    inside = [flat(q ^ c, s, c) for q, s, c in places]

    def swap_level(value, j):
        level = [flat(q, s, c ^ masks(q, replicas)[j]) for q, s, c in places]
        return lax.ppermute(value, ("row", "rep"), list(zip(here, level)))

    plane_rows = sections * block_rows
    chip, plane = place_of(sections)[0], lax.axis_index("rep")
    offset = (plane ^ turn(chip, replicas) ^ chip) * share
    pair = jnp.concatenate(
        [
            lax.dynamic_slice_in_dim(features, offset, share, 0),
            lax.dynamic_slice_in_dim(cotangent, offset, share, 0),
        ]
    )
    features, pair = lax.optimization_barrier((features, pair))
    dense, bias, own, *sent = call(
        functools.partial(first_kernel, sections),
        [
            shape((block_rows, plane_rows), BF16),
            shape((1, width), F32),
            shape((block_rows, width), F32),
        ]
        + [shape((block_rows, width), BF16)] * (sections - 1),
        [SMEM] * 3 + [HBM, VMEM, VMEM],
        [
            pltpu.VMEM((plane_rows, width), F32),
            pltpu.SemaphoreType.DMA((slot_total,)),
        ],
        flops=2 * plane_rows * block_rows * width,
        limit=51 * 1024 * 1024,
    )(src_slots, dst_slots, slot_counts, adj_values, features, bias_vector[None, :])
    pair, *sent = lax.optimization_barrier((pair, *sent))
    pair = lax.ppermute(pair, ("row", "rep"), list(zip(source, here)))
    received = [swap(value, k) for k, value in enumerate(sent, 1)]

    own, *sent = call(
        functools.partial(block_kernel, sections),
        [shape((share, width), F32)] + [shape((share, width), BF16)] * (replicas - 1),
        [VMEM] * sections,
        [pltpu.VMEM((block_rows, width), F32)],
    )(own, *received)
    received = [swap(value, k * sections) for k, value in enumerate(sent, 1)]

    act, *letters = call(
        functools.partial(middle_kernel, norm, sections, replicas, parts),
        [shape((share, width), BF16)]
        + [shape((share + sections * rows, width), BF16)] * replicas,
        [VMEM] * (replicas + 4),
        [pltpu.VMEM((width, share), BF16)] * 2,
    )(own, *received, pair, w_self, w_neigh, bias)
    letters = letters[:1] + [swap(v, k * sections) for k, v in enumerate(letters[1:], 1)]

    packs = call(
        functools.partial(pack_kernel, sections, share, rows),
        [shape((replicas * (share + rows), width), BF16)] * sections,
        [VMEM] * replicas,
    )(*letters)
    packs = packs[:1] + [swap(value, k) for k, value in enumerate(packs[1:], 1)]

    span = 2 * rows + 16
    terms, loaded = call(
        functools.partial(terms_kernel, share, rows),
        [shape((span, width), BF16), shape((span + share, width), BF16)],
        [VMEM] * (sections + 1),
        flops=2 * plane_rows * width * span,
    )(*packs, act)
    parts_here = [terms, swap_level(loaded, 0)]
    parts_here += [swap_level(terms, j) for j in range(1, replicas - 1)]

    sent = call(
        functools.partial(back_kernel, norm, sections, replicas),
        [shape((share, width), BF16)] * replicas,
        [VMEM] * (sections + 3),
        [pltpu.VMEM((plane_rows, width), BF16), pltpu.VMEM((block_rows, width), F32)],
        flops=2 * plane_rows * width * (block_rows + width),
    )(*packs, dense, w_self, w_neigh)
    received = [swap_rep(value, k) for k, value in enumerate(sent[2:], 2)]
    _, *parts_here = lax.optimization_barrier((sent[0], *parts_here))

    grad_bias, summed, act = call(
        functools.partial(level_kernel, sections, rows, factor),
        [
            shape((1, width), F32),
            shape((2 * rows, width), BF16),
            shape((share, width), BF16),
        ],
        [VMEM] * (replicas + 1),
        [pltpu.VMEM((replicas, span, width), BF16)],
    )(*parts_here, act)
    act = lax.ppermute(act, ("row", "rep"), list(zip(here, inside)))
    summed, near = lax.optimization_barrier((summed, sent[1]))
    near = swap_rep(near, 1)
    spread = parts // sections
    pieces = [summed] + [swap(summed, k * sections) for k in range(1, spread)]
    pieces[-1], act, near, *received = lax.optimization_barrier(
        (pieces[-1], act, near, *received)
    )
    (joined,) = call(
        functools.partial(join_kernel, sections),
        [shape((spread * 2 * rows, width), BF16)],
        [VMEM] * spread,
    )(*pieces)
    joined = [joined] + [swap(joined, k) for k in range(1, sections)]
    grad_self, grad_neigh = call(
        functools.partial(collect_kernel, rows, factor),
        [shape((width, width), F32)] * 2,
        [VMEM] * sections,
    )(*joined)
    grad_features, activations = call(
        last_kernel, [shape((share, width), BF16)] * 2, [VMEM] * (replicas + 1)
    )(sent[0], near, *received, act)
    return activations, grad_features, grad_self, grad_neigh, grad_bias[0]


def solution(mesh):
    placed = (
        P("row", None),
        P(),
        P(),
        P(),
        P("row", None),
        P("row", "rep", None, None, None),
        P("row", "rep", None),
        P("row", "rep", None),
        P("row", "rep"),
    )
    return jax.shard_map(
        shards,
        mesh=mesh,
        in_specs=placed,
        out_specs=(P(("row", "rep"), None), P(("row", "rep"), None), P(), P(), P()),
        check_vma=False,
    )
```

```python
import functools
import math

import jax
import jax.numpy as jnp
from jax import lax
from jax.experimental import pallas as pl
from jax.experimental.pallas import tpu as pltpu
from jax.sharding import PartitionSpec as P

F32 = jnp.float32
BF16 = jnp.bfloat16
VMEM = pl.BlockSpec(memory_space=pltpu.VMEM)
HBM = pl.BlockSpec(memory_space=pltpu.HBM)
SMEM = pl.BlockSpec(memory_space=pltpu.SMEM)
LIMIT = 16 * 1024 * 1024


def call(body, outs, ins, scratch=(), flops=0, limit=LIMIT):
    size = sum(math.prod(out.shape) * out.dtype.itemsize for out in outs)
    kernel = pl.pallas_call(
        body,
        out_shape=outs,
        in_specs=ins,
        out_specs=[VMEM] * len(outs),
        scratch_shapes=list(scratch),
        compiler_params=pltpu.CompilerParams(vmem_limit_bytes=limit),
        cost_estimate=pl.CostEstimate(flops=flops, bytes_accessed=2 * size, transcendentals=0),
    )
    return lambda *operands: list(kernel(*operands))


def shape(dims, kind):
    return jax.ShapeDtypeStruct(tuple(dims), kind)


def swap(value, step):
    return lax.ppermute(value, "row", [(i, i ^ step) for i in range(lax.axis_size("row"))])


def swap_rep(value, step):
    return lax.ppermute(value, "rep", [(i, i ^ step) for i in range(lax.axis_size("rep"))])


def contract(left, right, left_dim, right_dim):
    return lax.dot_general(
        left, right, (((left_dim,), (right_dim,)), ((), ())), preferred_element_type=F32
    )


def tree_sum(parts):
    while len(parts) > 1:
        parts = [parts[i] + parts[i + 1] for i in range(0, len(parts), 2)]
    return parts[0]


def place_of(sections):
    me = lax.axis_index("row")
    return me // sections, me % sections


def turn(c, replicas):
    out, bits = 0, replicas.bit_length() - 1
    for i in range(bits):
        out = out | ((c >> i) & 1) << (bits - 1 - i)
    return out


def tile_of(sections):
    return place_of(sections)[0] ^ lax.axis_index("rep")


def masks(first, count):
    first = first or 1
    return [first] + [m for m in range(1, count) if m != first]


def mask_of(first, j):
    first = jnp.where(first == 0, 1, first)
    return first if j == 0 else jnp.where(j >= first, j + 1, j)


def piece_of(ref, index, span):
    return ref[pl.ds(pl.multiple_of(index * span, span), span), :]


def first_kernel(sections, src, dst, count, tiles, field, bias, dense, bias_out, own, *rest):
    others, (total, sems) = rest[:-2], rest[-2:]
    size = tiles.shape[-1]
    block_rows = field.shape[0]
    _, s = place_of(sections)
    live = count[0, 0]
    dense[...] = jnp.zeros_like(dense)

    def tile_copy(e):
        row = pl.multiple_of(dst[0, 0, e] * size, size)
        col = pl.multiple_of(src[0, 0, e] * size, size)
        target = dense.at[pl.ds(row, size), pl.ds(col, size)]
        return pltpu.make_async_copy(tiles.at[0, 0, e], target, sems.at[e])

    lax.fori_loop(0, live, lambda e, carry: (tile_copy(e).start(), carry)[1], 0)
    bias_out[...] = bias[...]
    lax.fori_loop(0, live, lambda e, carry: (tile_copy(e).wait(), carry)[1], 0)
    for t in range(dense.shape[1] // size):
        cols = pl.ds(t * size, size)
        total[cols, :] = contract(dense[:, cols], field[...], 0, 0)
    own[...] = piece_of(total, s, block_rows)
    for k, out in enumerate(others, 1):
        out[...] = piece_of(total, s ^ k, block_rows).astype(BF16)


def block_kernel(sections, *refs):
    parts, own, others, total = refs[:sections], refs[sections], refs[sections + 1 : -1], refs[-1]
    share = own.shape[0]
    tile = tile_of(sections)
    value = parts[0][...]
    for ref in parts[1:]:
        value = value + ref[...].astype(F32)
    total[...] = value
    own[...] = piece_of(total, tile, share)
    for k, out in enumerate(others, 1):
        out[...] = piece_of(total, tile ^ k, share).astype(BF16)


def middle_kernel(norm, sections, replicas, parts, *refs):
    tiles, (pair, w_self, w_neigh, bias, act) = refs[:replicas], refs[replicas : replicas + 5]
    letters, (turned_f, turned_a) = refs[replicas + 5 : -2], refs[-2:]
    share, width = act.shape
    rows = width // parts
    q, _ = place_of(sections)
    total = tiles[0][...]
    for ref in tiles[1:]:
        total = total + ref[...].astype(F32)
    aggregate = (total * norm).astype(BF16)
    field = pair[pl.ds(0, share), :]
    pre = contract(field, w_self[...], 1, 0) + contract(aggregate, w_neigh[...], 1, 0)
    pre = pre + bias[...]
    slope = jnp.exp(jnp.minimum(pre, 0.0))
    act[...] = jnp.where(pre > 0.0, pre, slope - 1.0).astype(BF16)
    grad = (pair[pl.ds(share, share), :].astype(F32) * slope).astype(BF16)
    turned_f[...] = field.T
    turned_a[...] = aggregate.T
    span = sections * rows
    for k, letter in enumerate(letters):
        slot = (q ^ k) % (parts // sections)
        letter[pl.ds(0, share), :] = grad
        letter[pl.ds(share, span), pl.ds(0, share)] = piece_of(turned_f, slot, span)
        letter[pl.ds(share, span), pl.ds(128, share)] = piece_of(turned_a, slot, span)


def pack_kernel(sections, share, rows, *refs):
    letters, packs = refs[:-sections], refs[-sections:]
    _, s = place_of(sections)
    tile = tile_of(sections)
    block_rows = len(letters) * share
    for k, letter in enumerate(letters):
        here = pl.ds(pl.multiple_of((tile ^ k) * share, share), share)
        turned = pl.ds(pl.multiple_of(block_rows + (tile ^ k) * rows, rows), rows)
        for m, pack in enumerate(packs):
            first = pl.multiple_of(share + (s ^ m) * rows, 16)
            pack[here, :] = letter[pl.ds(0, share), :]
            pack[turned, :] = letter[pl.ds(first, rows), :]


def terms_kernel(share, rows, *refs):
    packs, out = refs[:-1], refs[-1]
    width = out.shape[1]
    replicas = packs[0].shape[0] // (share + rows)
    ones = jnp.ones((16, share), BF16)
    sums = []
    for pack in packs:
        total = jnp.zeros((2 * rows + 16, width), F32)
        for i in range(replicas):
            turned = pl.ds(replicas * share + i * rows, rows)
            field, aggregate = pack[turned, pl.ds(0, share)], pack[turned, pl.ds(128, share)]
            left = jnp.concatenate([field, aggregate, ones])
            total += contract(left, pack[pl.ds(i * share, share), :], 1, 0)
        sums.append(total)
    total = tree_sum(sums)
    tail = total[2 * rows :]
    high = tail.astype(BF16).astype(F32)
    line = lax.broadcasted_iota(jnp.int32, tail.shape, 0)
    out[pl.ds(0, 2 * rows), :] = total[: 2 * rows].astype(BF16)
    out[pl.ds(2 * rows, 16), :] = jnp.where(line == 0, high, tail - high).astype(BF16)


def back_kernel(norm, sections, replicas, *refs):
    packs, (dense, w_self, w_neigh, act) = refs[:sections], refs[sections : sections + 4]
    own, outs, (message, total) = refs[sections + 4], refs[sections + 5 : -2], refs[-2:]
    me_rep = lax.axis_index("rep")
    q, s = place_of(sections)
    block_rows = dense.shape[0]
    share = block_rows // replicas
    for k, pack in enumerate(packs):
        here = pl.ds(pl.multiple_of((s ^ k) * block_rows, block_rows), block_rows)
        grad = pack[pl.ds(0, block_rows), :]
        message[here, :] = contract(grad, w_neigh[...], 1, 1).astype(BF16)
    total[...] = contract(dense[...], message[...], 1, 0) * norm

    @pl.when(me_rep == q)
    def _():
        total[...] += contract(packs[0][pl.ds(0, block_rows), :], w_self[...], 1, 1)

    own[...] = piece_of(total, me_rep, share).astype(BF16)
    for j, out in enumerate(outs):
        out[pl.ds(0, share), :] = piece_of(total, me_rep ^ mask_of(q, j), share).astype(BF16)
    outs[0][pl.ds(share, share), :] = act[...]


def level_kernel(rows, factor, *refs):
    parts, (bias, summed) = refs[:-2], refs[-2:]
    terms = tree_sum([ref[...].astype(F32) for ref in parts])
    tail = terms[2 * rows : 2 * rows + 8]
    bias[...] = (tail[0:1] + tail[1:2]) * factor
    summed[...] = terms[: 2 * rows].astype(BF16)


def pick_kernel(sections, act, came, out):
    q, _ = place_of(sections)
    share = act.shape[0]
    arrived = came[pl.ds(share, share), :].astype(F32)
    out[...] = jnp.where(q == 0, act[...].astype(F32), arrived).astype(BF16)


def last_kernel(*refs):
    parts, (act, grad_features, activations) = refs[:-3], refs[-3:]
    here = pl.ds(0, grad_features.shape[0])
    grad_features[...] = tree_sum([ref[here, :].astype(F32) for ref in parts]).astype(BF16)
    activations[...] = act[...]


def join_kernel(sections, *refs):
    pieces, out = refs[:-1], refs[-1]
    span = pieces[0].shape[0]
    q, _ = place_of(sections)
    for k, piece in enumerate(pieces):
        slot = (q % len(pieces)) ^ k
        out[pl.ds(pl.multiple_of(slot * span, 16), span), :] = piece[...]


def collect_kernel(rows, factor, *refs):
    joined, (grad_self, grad_neigh) = refs[:-2], refs[-2:]
    sections = len(joined)
    _, s = place_of(sections)
    for k, ref in enumerate(joined):
        for j in range(ref.shape[0] // (2 * rows)):
            place = pl.ds(pl.multiple_of((j * sections + (s ^ k)) * rows, rows), rows)
            base = j * 2 * rows
            grad_self[place, :] = ref[pl.ds(base, rows), :].astype(F32) * factor
            grad_neigh[place, :] = ref[pl.ds(base + rows, rows), :].astype(F32) * factor


def shards(
    features, w_self, w_neigh, bias_vector, cotangent, adj_values, src_slots, dst_slots, slot_counts
):
    block_rows, width = features.shape
    blocks, replicas = lax.axis_size("row"), lax.axis_size("rep")
    sections = blocks // replicas
    share = block_rows // replicas
    slot_total, size = adj_values.shape[2], adj_values.shape[-1]
    norm = 1.0 / math.sqrt(slot_total * replicas / (block_rows // size))
    factor = 1.0 / math.sqrt(block_rows * blocks)
    parts = min(blocks, width // 16)
    rows = width // parts

    def flat(q, s, c):
        return (q * sections + s) * replicas + c

    places = [
        (q, s, c) for q in range(replicas) for s in range(sections) for c in range(replicas)
    ]
    here = [flat(q, s, c) for q, s, c in places]
    source = [flat(c, s, q ^ turn(c, replicas)) for q, s, c in places]
    inside = [flat(q ^ c, s, c) for q, s, c in places]

    def swap_level(value, j):
        level = [flat(q, s, c ^ masks(q, replicas)[j]) for q, s, c in places]
        return lax.ppermute(value, ("row", "rep"), list(zip(here, level)))

    plane_rows = sections * block_rows
    chip, plane = place_of(sections)[0], lax.axis_index("rep")
    offset = (plane ^ turn(chip, replicas) ^ chip) * share
    pair = jnp.concatenate(
        [
            lax.dynamic_slice_in_dim(features, offset, share, 0),
            lax.dynamic_slice_in_dim(cotangent, offset, share, 0),
        ]
    )
    features, pair = lax.optimization_barrier((features, pair))
    dense, bias, own, *sent = call(
        functools.partial(first_kernel, sections),
        [
            shape((block_rows, plane_rows), BF16),
            shape((1, width), F32),
            shape((block_rows, width), F32),
        ]
        + [shape((block_rows, width), BF16)] * (sections - 1),
        [SMEM] * 3 + [HBM, VMEM, VMEM],
        [
            pltpu.VMEM((plane_rows, width), F32),
            pltpu.SemaphoreType.DMA((slot_total,)),
        ],
        flops=2 * plane_rows * block_rows * width,
        limit=51 * 1024 * 1024,
    )(src_slots, dst_slots, slot_counts, adj_values, features, bias_vector[None, :])
    pair, *sent = lax.optimization_barrier((pair, *sent))
    pair = lax.ppermute(pair, ("row", "rep"), list(zip(source, here)))
    received = [swap(value, k) for k, value in enumerate(sent, 1)]

    own, *sent = call(
        functools.partial(block_kernel, sections),
        [shape((share, width), F32)] + [shape((share, width), BF16)] * (replicas - 1),
        [VMEM] * sections,
        [pltpu.VMEM((block_rows, width), F32)],
    )(own, *received)
    received = [swap(value, k * sections) for k, value in enumerate(sent, 1)]

    act, *letters = call(
        functools.partial(middle_kernel, norm, sections, replicas, parts),
        [shape((share, width), BF16)]
        + [shape((share + sections * rows, width), BF16)] * replicas,
        [VMEM] * (replicas + 4),
        [pltpu.VMEM((width, share), BF16)] * 2,
    )(own, *received, pair, w_self, w_neigh, bias)
    letters = letters[:1] + [swap(v, k * sections) for k, v in enumerate(letters[1:], 1)]

    packs = call(
        functools.partial(pack_kernel, sections, share, rows),
        [shape((replicas * (share + rows), width), BF16)] * sections,
        [VMEM] * replicas,
    )(*letters)
    packs = packs[:1] + [swap(value, k) for k, value in enumerate(packs[1:], 1)]

    (terms,) = call(
        functools.partial(terms_kernel, share, rows),
        [shape((2 * rows + 16, width), BF16)],
        [VMEM] * sections,
        flops=2 * plane_rows * width * (2 * rows + 16),
    )(*packs)
    terms = [terms] + [swap_rep(terms, k) for k in range(1, replicas)]

    sent = call(
        functools.partial(back_kernel, norm, sections, replicas),
        [shape((share, width), BF16), shape((2 * share, width), BF16)]
        + [shape((share, width), BF16)] * (replicas - 2),
        [VMEM] * (sections + 4),
        [pltpu.VMEM((plane_rows, width), BF16), pltpu.VMEM((block_rows, width), F32)],
        flops=2 * plane_rows * width * (block_rows + width),
    )(*packs, dense, w_self, w_neigh, act)
    _, *terms = lax.optimization_barrier((sent[0], *terms))
    grad_bias, summed = call(
        functools.partial(level_kernel, rows, factor),
        [shape((1, width), F32), shape((2 * rows, width), BF16)],
        [VMEM] * replicas,
    )(*terms)
    summed, *sent = lax.optimization_barrier((summed, *sent))
    received = [sent[0]] + [swap_level(value, j) for j, value in enumerate(sent[1:])]
    spread = parts // sections
    pieces = [summed] + [swap(summed, k * sections) for k in range(1, spread)]
    received[1], pieces[1] = lax.optimization_barrier((received[1], pieces[1]))
    (act,) = call(
        functools.partial(pick_kernel, sections),
        [shape((share, width), BF16)],
        [VMEM] * 2,
    )(act, received[1])
    act = lax.ppermute(act, ("row", "rep"), list(zip(here, inside)))
    pieces[-1], act, received[2], received[3] = lax.optimization_barrier(
        (pieces[-1], act, received[2], received[3])
    )
    (joined,) = call(
        functools.partial(join_kernel, sections),
        [shape((spread * 2 * rows, width), BF16)],
        [VMEM] * spread,
    )(*pieces)
    joined = [joined] + [swap(joined, k) for k in range(1, sections)]
    grad_self, grad_neigh = call(
        functools.partial(collect_kernel, rows, factor),
        [shape((width, width), F32)] * 2,
        [VMEM] * sections,
    )(*joined)
    grad_features, activations = call(
        last_kernel, [shape((share, width), BF16)] * 2, [VMEM] * (replicas + 1)
    )(*received, act)
    return activations, grad_features, grad_self, grad_neigh, grad_bias[0]


def solution(mesh):
    placed = (
        P("row", None),
        P(),
        P(),
        P(),
        P("row", None),
        P("row", "rep", None, None, None),
        P("row", "rep", None),
        P("row", "rep", None),
        P("row", "rep"),
    )
    return jax.shard_map(
        shards,
        mesh=mesh,
        in_specs=placed,
        out_specs=(P(("row", "rep"), None), P(("row", "rep"), None), P(), P(), P()),
        check_vma=False,
    )
```

```python
import functools
import math

import jax
import jax.numpy as jnp
from jax import lax
from jax.experimental import pallas as pl
from jax.experimental.pallas import tpu as pltpu
from jax.sharding import PartitionSpec as P

F32 = jnp.float32
BF16 = jnp.bfloat16
VMEM = pl.BlockSpec(memory_space=pltpu.VMEM)
HBM = pl.BlockSpec(memory_space=pltpu.HBM)
SMEM = pl.BlockSpec(memory_space=pltpu.SMEM)
LIMIT = 16 * 1024 * 1024


def call(body, outs, ins, scratch=(), flops=0, limit=LIMIT):
    size = sum(math.prod(out.shape) * out.dtype.itemsize for out in outs)
    kernel = pl.pallas_call(
        body,
        out_shape=outs,
        in_specs=ins,
        out_specs=[VMEM] * len(outs),
        scratch_shapes=list(scratch),
        compiler_params=pltpu.CompilerParams(vmem_limit_bytes=limit),
        cost_estimate=pl.CostEstimate(flops=flops, bytes_accessed=2 * size, transcendentals=0),
    )
    return lambda *operands: list(kernel(*operands))


def shape(dims, kind):
    return jax.ShapeDtypeStruct(tuple(dims), kind)


def swap(value, step):
    return lax.ppermute(value, "row", [(i, i ^ step) for i in range(lax.axis_size("row"))])


def swap_rep(value, step):
    return lax.ppermute(value, "rep", [(i, i ^ step) for i in range(lax.axis_size("rep"))])


def contract(left, right, left_dim, right_dim):
    return lax.dot_general(
        left, right, (((left_dim,), (right_dim,)), ((), ())), preferred_element_type=F32
    )


def tree_sum(parts):
    while len(parts) > 1:
        parts = [parts[i] + parts[i + 1] for i in range(0, len(parts), 2)]
    return parts[0]


def place_of(sections):
    me = lax.axis_index("row")
    return me // sections, me % sections


def turn(c, replicas):
    out, bits = 0, replicas.bit_length() - 1
    for i in range(bits):
        out = out | ((c >> i) & 1) << (bits - 1 - i)
    return out


def tile_of(sections):
    return place_of(sections)[0] ^ lax.axis_index("rep")


def masks(first, count):
    first = first or 1
    return [first] + [m for m in range(1, count) if m != first]


def mask_of(first, j):
    first = jnp.where(first == 0, 1, first)
    return first if j == 0 else jnp.where(j >= first, j + 1, j)


def piece_of(ref, index, span):
    return ref[pl.ds(pl.multiple_of(index * span, span), span), :]


def tile_copies(src, dst, live, tiles, dense, sems):
    size = tiles.shape[-1]

    def tile_copy(e):
        row = pl.multiple_of(dst[0, 0, e] * size, size)
        col = pl.multiple_of(src[0, 0, e] * size, size)
        target = dense.at[pl.ds(row, size), pl.ds(col, size)]
        return pltpu.make_async_copy(tiles.at[0, 0, e], target, sems.at[e])

    def start():
        lax.fori_loop(0, live, lambda e, carry: (tile_copy(e).start(), carry)[1], 0)

    def wait():
        lax.fori_loop(0, live, lambda e, carry: (tile_copy(e).wait(), carry)[1], 0)

    return start, wait


def dense_kernel(src, dst, count, tiles, bias, dense, bias_out, sems):
    bias_out[...] = bias[...]
    dense[...] = jnp.zeros_like(dense)
    start, wait = tile_copies(src, dst, count[0, 0], tiles, dense, sems)
    start()
    wait()


def first_kernel(sections, src, dst, count, tiles, field, cotangent, *refs):
    pair, own = refs[:2]
    others, (dense, held, total, sems, own_sems) = refs[2:-5], refs[-5:]
    size = tiles.shape[-1]
    block_rows = field.shape[0]
    share = pair.shape[0] // 2
    chip, s = place_of(sections)
    turned = turn(chip, block_rows // share)
    offset = pl.multiple_of((lax.axis_index("rep") ^ turned ^ chip) * share, share)
    field_copy = pltpu.make_async_copy(field, held, own_sems.at[0])
    field_copy.start()
    cotangent_copy = pltpu.make_async_copy(
        cotangent.at[pl.ds(offset, share), :], pair.at[pl.ds(share, share), :], own_sems.at[1]
    )
    cotangent_copy.start()
    dense[...] = jnp.zeros_like(dense)
    start, wait = tile_copies(src, dst, count[0, 0], tiles, dense, sems)
    start()
    field_copy.wait()
    pair[pl.ds(0, share), :] = held[pl.ds(offset, share), :]
    wait()
    for t in range(dense.shape[1] // size):
        cols = pl.ds(t * size, size)
        total[cols, :] = contract(dense[:, cols], held[...], 0, 0)
    own[...] = piece_of(total, s, block_rows).astype(BF16)
    for k, out in enumerate(others, 1):
        out[...] = piece_of(total, s ^ k, block_rows).astype(BF16)
    cotangent_copy.wait()


def block_kernel(sections, *refs):
    parts, own, others, total = refs[:sections], refs[sections], refs[sections + 1 : -1], refs[-1]
    share = own.shape[0]
    tile = tile_of(sections)
    value = parts[0][...].astype(F32)
    for ref in parts[1:]:
        value = value + ref[...].astype(F32)
    total[...] = value
    own[...] = piece_of(total, tile, share)
    for k, out in enumerate(others, 1):
        out[...] = piece_of(total, tile ^ k, share).astype(BF16)


def middle_kernel(norm, sections, replicas, parts, *refs):
    tiles, (pair, w_self, w_neigh, bias, act) = refs[:replicas], refs[replicas : replicas + 5]
    letters, (turned_f, turned_a) = refs[replicas + 5 : -2], refs[-2:]
    share, width = act.shape
    rows = width // parts
    q, _ = place_of(sections)
    total = tiles[0][...]
    for ref in tiles[1:]:
        total = total + ref[...].astype(F32)
    aggregate = (total * norm).astype(BF16)
    field = pair[pl.ds(0, share), :]
    pre = contract(field, w_self[...], 1, 0) + contract(aggregate, w_neigh[...], 1, 0)
    pre = pre + bias[...]
    slope = jnp.exp(jnp.minimum(pre, 0.0))
    act[...] = jnp.where(pre > 0.0, pre, slope - 1.0).astype(BF16)
    grad = (pair[pl.ds(share, share), :].astype(F32) * slope).astype(BF16)
    turned_f[...] = field.T
    turned_a[...] = aggregate.T
    span = sections * rows
    for k, letter in enumerate(letters):
        slot = (q ^ k) % (parts // sections)
        letter[pl.ds(0, share), :] = grad
        letter[pl.ds(share, span), pl.ds(0, share)] = piece_of(turned_f, slot, span)
        letter[pl.ds(share, span), pl.ds(128, share)] = piece_of(turned_a, slot, span)


def pack_kernel(sections, share, rows, *refs):
    letters, packs = refs[:-sections], refs[-sections:]
    _, s = place_of(sections)
    tile = tile_of(sections)
    block_rows = len(letters) * share
    for k, letter in enumerate(letters):
        here = pl.ds(pl.multiple_of((tile ^ k) * share, share), share)
        turned = pl.ds(pl.multiple_of(block_rows + (tile ^ k) * rows, rows), rows)
        for m, pack in enumerate(packs):
            first = pl.multiple_of(share + (s ^ m) * rows, 16)
            pack[here, :] = letter[pl.ds(0, share), :]
            pack[turned, :] = letter[pl.ds(first, rows), :]


def terms_kernel(share, rows, *refs):
    packs, out = refs[:-1], refs[-1]
    width = out.shape[1]
    replicas = packs[0].shape[0] // (share + rows)
    ones = jnp.ones((16, share), BF16)
    sums = []
    for pack in packs:
        total = jnp.zeros((2 * rows + 16, width), F32)
        for i in range(replicas):
            turned = pl.ds(replicas * share + i * rows, rows)
            field, aggregate = pack[turned, pl.ds(0, share)], pack[turned, pl.ds(128, share)]
            left = jnp.concatenate([field, aggregate, ones])
            total += contract(left, pack[pl.ds(i * share, share), :], 1, 0)
        sums.append(total)
    total = tree_sum(sums)
    tail = total[2 * rows :]
    high = tail.astype(BF16).astype(F32)
    line = lax.broadcasted_iota(jnp.int32, tail.shape, 0)
    out[pl.ds(0, 2 * rows), :] = total[: 2 * rows].astype(BF16)
    out[pl.ds(2 * rows, 16), :] = jnp.where(line == 0, high, tail - high).astype(BF16)


def back_kernel(norm, sections, replicas, *refs):
    packs, (dense, w_self, w_neigh, act) = refs[:sections], refs[sections : sections + 4]
    own, outs, (message, total) = refs[sections + 4], refs[sections + 5 : -2], refs[-2:]
    me_rep = lax.axis_index("rep")
    q, s = place_of(sections)
    block_rows = dense.shape[0]
    share = block_rows // replicas
    for k, pack in enumerate(packs):
        here = pl.ds(pl.multiple_of((s ^ k) * block_rows, block_rows), block_rows)
        grad = pack[pl.ds(0, block_rows), :]
        message[here, :] = contract(grad, w_neigh[...], 1, 1).astype(BF16)
    total[...] = contract(dense[...], message[...], 1, 0) * norm

    @pl.when(me_rep == q)
    def _():
        total[...] += contract(packs[0][pl.ds(0, block_rows), :], w_self[...], 1, 1)

    own[...] = piece_of(total, me_rep, share).astype(BF16)
    for j, out in enumerate(outs):
        out[pl.ds(0, share), :] = piece_of(total, me_rep ^ mask_of(q, j), share).astype(BF16)
    outs[0][pl.ds(share, share), :] = act[...]


def level_kernel(rows, factor, *refs):
    parts, (bias, summed) = refs[:-2], refs[-2:]
    terms = tree_sum([ref[...].astype(F32) for ref in parts])
    tail = terms[2 * rows : 2 * rows + 8]
    bias[...] = (tail[0:1] + tail[1:2]) * factor
    summed[...] = terms[: 2 * rows].astype(BF16)


def pick_kernel(sections, act, came, out):
    q, _ = place_of(sections)
    share = act.shape[0]
    arrived = came[pl.ds(share, share), :].astype(F32)
    out[...] = jnp.where(q == 0, act[...].astype(F32), arrived).astype(BF16)


def last_kernel(*refs):
    parts, (act, grad_features, activations) = refs[:-3], refs[-3:]
    here = pl.ds(0, grad_features.shape[0])
    grad_features[...] = tree_sum([ref[here, :].astype(F32) for ref in parts]).astype(BF16)
    activations[...] = act[...]


def join_kernel(sections, *refs):
    pieces, out = refs[:-1], refs[-1]
    span = pieces[0].shape[0]
    q, _ = place_of(sections)
    for k, piece in enumerate(pieces):
        slot = (q % len(pieces)) ^ k
        out[pl.ds(pl.multiple_of(slot * span, 16), span), :] = piece[...]


def collect_kernel(rows, factor, *refs):
    joined, (grad_self, grad_neigh) = refs[:-2], refs[-2:]
    sections = len(joined)
    _, s = place_of(sections)
    for k, ref in enumerate(joined):
        for j in range(ref.shape[0] // (2 * rows)):
            place = pl.ds(pl.multiple_of((j * sections + (s ^ k)) * rows, rows), rows)
            base = j * 2 * rows
            grad_self[place, :] = ref[pl.ds(base, rows), :].astype(F32) * factor
            grad_neigh[place, :] = ref[pl.ds(base + rows, rows), :].astype(F32) * factor


def shards(
    features, w_self, w_neigh, bias_vector, cotangent, adj_values, src_slots, dst_slots, slot_counts
):
    block_rows, width = features.shape
    blocks, replicas = lax.axis_size("row"), lax.axis_size("rep")
    sections = blocks // replicas
    share = block_rows // replicas
    slot_total, size = adj_values.shape[2], adj_values.shape[-1]
    norm = 1.0 / math.sqrt(slot_total * replicas / (block_rows // size))
    factor = 1.0 / math.sqrt(block_rows * blocks)
    parts = min(blocks, width // 16)
    rows = width // parts

    def flat(q, s, c):
        return (q * sections + s) * replicas + c

    places = [
        (q, s, c) for q in range(replicas) for s in range(sections) for c in range(replicas)
    ]
    here = [flat(q, s, c) for q, s, c in places]
    source = [flat(c, s, q ^ turn(c, replicas)) for q, s, c in places]
    inside = [flat(q ^ c, s, c) for q, s, c in places]

    def swap_level(value, j):
        level = [flat(q, s, c ^ masks(q, replicas)[j]) for q, s, c in places]
        return lax.ppermute(value, ("row", "rep"), list(zip(here, level)))

    plane_rows = sections * block_rows
    pair, own, *sent = call(
        functools.partial(first_kernel, sections),
        [shape((2 * share, width), BF16)]
        + [shape((block_rows, width), BF16)] * sections,
        [SMEM] * 3 + [HBM] * 3,
        [
            pltpu.VMEM((block_rows, plane_rows), BF16),
            pltpu.VMEM((block_rows, width), BF16),
            pltpu.VMEM((plane_rows, width), F32),
            pltpu.SemaphoreType.DMA((slot_total,)),
            pltpu.SemaphoreType.DMA((2,)),
        ],
        flops=2 * plane_rows * block_rows * width,
        limit=60 * 1024 * 1024,
    )(src_slots, dst_slots, slot_counts, adj_values, features, cotangent)
    pair = lax.ppermute(pair, ("row", "rep"), list(zip(source, here)))
    received = [swap(value, k) for k, value in enumerate(sent, 1)]

    own, *sent = call(
        functools.partial(block_kernel, sections),
        [shape((share, width), F32)] + [shape((share, width), BF16)] * (replicas - 1),
        [VMEM] * sections,
        [pltpu.VMEM((block_rows, width), F32)],
    )(own, *received)
    received = [swap(value, k * sections) for k, value in enumerate(sent, 1)]

    dense, bias = call(
        dense_kernel,
        [shape((block_rows, plane_rows), BF16), shape((1, width), F32)],
        [SMEM] * 3 + [HBM, VMEM],
        [pltpu.SemaphoreType.DMA((slot_total,))],
        limit=51 * 1024 * 1024,
    )(src_slots, dst_slots, slot_counts, adj_values, bias_vector[None, :])
    dense, received[0] = lax.optimization_barrier((dense, received[0]))
    act, *letters = call(
        functools.partial(middle_kernel, norm, sections, replicas, parts),
        [shape((share, width), BF16)]
        + [shape((share + sections * rows, width), BF16)] * replicas,
        [VMEM] * (replicas + 4),
        [pltpu.VMEM((width, share), BF16)] * 2,
    )(own, *received, pair, w_self, w_neigh, bias)
    letters = letters[:1] + [swap(v, k * sections) for k, v in enumerate(letters[1:], 1)]

    packs = call(
        functools.partial(pack_kernel, sections, share, rows),
        [shape((replicas * (share + rows), width), BF16)] * sections,
        [VMEM] * replicas,
    )(*letters)
    packs = packs[:1] + [swap(value, k) for k, value in enumerate(packs[1:], 1)]

    (terms,) = call(
        functools.partial(terms_kernel, share, rows),
        [shape((2 * rows + 16, width), BF16)],
        [VMEM] * sections,
        flops=2 * plane_rows * width * (2 * rows + 16),
    )(*packs)
    terms, *packs = lax.optimization_barrier((terms, *packs))
    terms = [terms] + [swap_rep(terms, k) for k in range(1, replicas)]

    sent = call(
        functools.partial(back_kernel, norm, sections, replicas),
        [shape((share, width), BF16), shape((2 * share, width), BF16)]
        + [shape((share, width), BF16)] * (replicas - 2),
        [VMEM] * (sections + 4),
        [pltpu.VMEM((plane_rows, width), BF16), pltpu.VMEM((block_rows, width), F32)],
        flops=2 * plane_rows * width * (block_rows + width),
    )(*packs, dense, w_self, w_neigh, act)
    received = [swap_level(value, j) for j, value in enumerate(sent[2:], 1)]
    _, *terms = lax.optimization_barrier((sent[0], *terms))
    grad_bias, summed = call(
        functools.partial(level_kernel, rows, factor),
        [shape((1, width), F32), shape((2 * rows, width), BF16)],
        [VMEM] * replicas,
    )(*terms)
    summed, loaded = lax.optimization_barrier((summed, sent[1]))
    loaded = swap_level(loaded, 0)
    (act,) = call(
        functools.partial(pick_kernel, sections),
        [shape((share, width), BF16)],
        [VMEM] * 2,
    )(act, loaded)
    act = lax.ppermute(act, ("row", "rep"), list(zip(here, inside)))
    spread = parts // sections
    pieces = [summed] + [swap(summed, k * sections) for k in range(1, spread)]
    pieces[-1], *received = lax.optimization_barrier((pieces[-1], *received))
    (joined,) = call(
        functools.partial(join_kernel, sections),
        [shape((spread * 2 * rows, width), BF16)],
        [VMEM] * spread,
    )(*pieces)
    joined = [joined] + [swap(joined, k) for k in range(1, sections)]
    grad_self, grad_neigh = call(
        functools.partial(collect_kernel, rows, factor),
        [shape((width, width), F32)] * 2,
        [VMEM] * sections,
    )(*joined)
    grad_features, activations = call(
        last_kernel, [shape((share, width), BF16)] * 2, [VMEM] * (replicas + 1)
    )(sent[0], loaded, *received, act)
    return activations, grad_features, grad_self, grad_neigh, grad_bias[0]


def solution(mesh):
    placed = (
        P("row", None),
        P(),
        P(),
        P(),
        P("row", None),
        P("row", "rep", None, None, None),
        P("row", "rep", None),
        P("row", "rep", None),
        P("row", "rep"),
    )
    return jax.shard_map(
        shards,
        mesh=mesh,
        in_specs=placed,
        out_specs=(P(("row", "rep"), None), P(("row", "rep"), None), P(), P(), P()),
        check_vma=False,
    )
```

```python
import functools
import math

import jax
import jax.numpy as jnp
from jax import lax
from jax.experimental import pallas as pl
from jax.experimental.pallas import tpu as pltpu
from jax.sharding import PartitionSpec as P

F32 = jnp.float32
BF16 = jnp.bfloat16
VMEM = pl.BlockSpec(memory_space=pltpu.VMEM)
HBM = pl.BlockSpec(memory_space=pltpu.HBM)
SMEM = pl.BlockSpec(memory_space=pltpu.SMEM)
LIMIT = 16 * 1024 * 1024


def call(body, outs, ins, scratch=(), flops=0, limit=LIMIT):
    size = sum(math.prod(out.shape) * out.dtype.itemsize for out in outs)
    kernel = pl.pallas_call(
        body,
        out_shape=outs,
        in_specs=ins,
        out_specs=[VMEM] * len(outs),
        scratch_shapes=list(scratch),
        compiler_params=pltpu.CompilerParams(vmem_limit_bytes=limit),
        cost_estimate=pl.CostEstimate(flops=flops, bytes_accessed=2 * size, transcendentals=0),
    )
    return lambda *operands: list(kernel(*operands))


def shape(dims, kind):
    return jax.ShapeDtypeStruct(tuple(dims), kind)


def swap(value, step):
    return lax.ppermute(value, "row", [(i, i ^ step) for i in range(lax.axis_size("row"))])


def swap_rep(value, step):
    return lax.ppermute(value, "rep", [(i, i ^ step) for i in range(lax.axis_size("rep"))])


def contract(left, right, left_dim, right_dim):
    return lax.dot_general(
        left, right, (((left_dim,), (right_dim,)), ((), ())), preferred_element_type=F32
    )


def tree_sum(parts):
    while len(parts) > 1:
        parts = [parts[i] + parts[i + 1] for i in range(0, len(parts), 2)]
    return parts[0]


def place_of(sections):
    me = lax.axis_index("row")
    return me // sections, me % sections


def turn(c, replicas):
    out, bits = 0, replicas.bit_length() - 1
    for i in range(bits):
        out = out | ((c >> i) & 1) << (bits - 1 - i)
    return out


def tile_of(sections):
    return place_of(sections)[0] ^ lax.axis_index("rep")


def masks(first, count):
    first = first or 1
    return [first] + [m for m in range(1, count) if m != first]


def mask_of(first, j):
    first = jnp.where(first == 0, 1, first)
    return first if j == 0 else jnp.where(j >= first, j + 1, j)


def piece_of(ref, index, span):
    return ref[pl.ds(pl.multiple_of(index * span, span), span), :]


def tile_copies(src, dst, live, tiles, dense, sems):
    size = tiles.shape[-1]

    def tile_copy(e):
        row = pl.multiple_of(dst[0, 0, e] * size, size)
        col = pl.multiple_of(src[0, 0, e] * size, size)
        target = dense.at[pl.ds(row, size), pl.ds(col, size)]
        return pltpu.make_async_copy(tiles.at[0, 0, e], target, sems.at[e])

    def start():
        lax.fori_loop(0, live, lambda e, carry: (tile_copy(e).start(), carry)[1], 0)

    def wait():
        lax.fori_loop(0, live, lambda e, carry: (tile_copy(e).wait(), carry)[1], 0)

    return start, wait


def dense_kernel(src, dst, count, tiles, bias, dense, bias_out, sems):
    bias_out[...] = bias[...]
    dense[...] = jnp.zeros_like(dense)
    start, wait = tile_copies(src, dst, count[0, 0], tiles, dense, sems)
    start()
    wait()


def first_kernel(sections, src, dst, count, tiles, field, cotangent, *refs):
    pair, own = refs[:2]
    others, (dense, held, total, sems, own_sems) = refs[2:-5], refs[-5:]
    size = tiles.shape[-1]
    block_rows = field.shape[0]
    share = pair.shape[0] // 2
    chip, s = place_of(sections)
    turned = turn(chip, block_rows // share)
    offset = pl.multiple_of((lax.axis_index("rep") ^ turned ^ chip) * share, share)
    field_copy = pltpu.make_async_copy(field, held, own_sems.at[0])
    field_copy.start()
    cotangent_copy = pltpu.make_async_copy(
        cotangent.at[pl.ds(offset, share), :], pair.at[pl.ds(share, share), :], own_sems.at[1]
    )
    cotangent_copy.start()
    dense[...] = jnp.zeros_like(dense)
    start, wait = tile_copies(src, dst, count[0, 0], tiles, dense, sems)
    start()
    field_copy.wait()
    pair[pl.ds(0, share), :] = held[pl.ds(offset, share), :]
    wait()
    for t in range(dense.shape[1] // size):
        cols = pl.ds(t * size, size)
        total[cols, :] = contract(dense[:, cols], held[...], 0, 0)
    own[...] = piece_of(total, s, block_rows).astype(BF16)
    for k, out in enumerate(others, 1):
        out[...] = piece_of(total, s ^ k, block_rows).astype(BF16)
    cotangent_copy.wait()


def block_kernel(sections, *refs):
    parts, own, others, total = refs[:sections], refs[sections], refs[sections + 1 : -1], refs[-1]
    share = own.shape[0]
    tile = tile_of(sections)
    value = parts[0][...].astype(F32)
    for ref in parts[1:]:
        value = value + ref[...].astype(F32)
    total[...] = value
    own[...] = piece_of(total, tile, share)
    for k, out in enumerate(others, 1):
        out[...] = piece_of(total, tile ^ k, share).astype(BF16)


def middle_kernel(norm, sections, replicas, parts, *refs):
    tiles, (pair, w_self, w_neigh, bias, act) = refs[:replicas], refs[replicas : replicas + 5]
    letters, (turned_f, turned_a) = refs[replicas + 5 : -2], refs[-2:]
    share, width = act.shape
    rows = width // parts
    q, _ = place_of(sections)
    total = tiles[0][...]
    for ref in tiles[1:]:
        total = total + ref[...].astype(F32)
    aggregate = (total * norm).astype(BF16)
    field = pair[pl.ds(0, share), :]
    pre = contract(field, w_self[...], 1, 0) + contract(aggregate, w_neigh[...], 1, 0)
    pre = pre + bias[...]
    slope = jnp.exp(jnp.minimum(pre, 0.0))
    act[...] = jnp.where(pre > 0.0, pre, slope - 1.0).astype(BF16)
    grad = (pair[pl.ds(share, share), :].astype(F32) * slope).astype(BF16)
    turned_f[...] = field.T
    turned_a[...] = aggregate.T
    span = sections * rows
    for k, letter in enumerate(letters):
        slot = (q ^ k) % (parts // sections)
        letter[pl.ds(0, share), :] = grad
        letter[pl.ds(share, span), pl.ds(0, share)] = piece_of(turned_f, slot, span)
        letter[pl.ds(share, span), pl.ds(128, share)] = piece_of(turned_a, slot, span)


def pack_kernel(sections, share, rows, *refs):
    letters, packs = refs[:-sections], refs[-sections:]
    _, s = place_of(sections)
    tile = tile_of(sections)
    block_rows = len(letters) * share
    for k, letter in enumerate(letters):
        here = pl.ds(pl.multiple_of((tile ^ k) * share, share), share)
        turned = pl.ds(pl.multiple_of(block_rows + (tile ^ k) * rows, rows), rows)
        for m, pack in enumerate(packs):
            first = pl.multiple_of(share + (s ^ m) * rows, 16)
            pack[here, :] = letter[pl.ds(0, share), :]
            pack[turned, :] = letter[pl.ds(first, rows), :]


def terms_kernel(share, rows, *refs):
    packs, out = refs[:-1], refs[-1]
    width = out.shape[1]
    replicas = packs[0].shape[0] // (share + rows)
    ones = jnp.ones((16, share), BF16)
    sums = []
    for pack in packs:
        total = jnp.zeros((2 * rows + 16, width), F32)
        for i in range(replicas):
            turned = pl.ds(replicas * share + i * rows, rows)
            field, aggregate = pack[turned, pl.ds(0, share)], pack[turned, pl.ds(128, share)]
            left = jnp.concatenate([field, aggregate, ones])
            total += contract(left, pack[pl.ds(i * share, share), :], 1, 0)
        sums.append(total)
    total = tree_sum(sums)
    tail = total[2 * rows :]
    high = tail.astype(BF16).astype(F32)
    line = lax.broadcasted_iota(jnp.int32, tail.shape, 0)
    out[pl.ds(0, 2 * rows), :] = total[: 2 * rows].astype(BF16)
    out[pl.ds(2 * rows, 16), :] = jnp.where(line == 0, high, tail - high).astype(BF16)


def back_kernel(norm, sections, replicas, *refs):
    packs, (dense, w_self, w_neigh, act) = refs[:sections], refs[sections : sections + 4]
    own, outs, (message, total) = refs[sections + 4], refs[sections + 5 : -2], refs[-2:]
    me_rep = lax.axis_index("rep")
    q, s = place_of(sections)
    block_rows = dense.shape[0]
    share = block_rows // replicas
    for k, pack in enumerate(packs):
        here = pl.ds(pl.multiple_of((s ^ k) * block_rows, block_rows), block_rows)
        grad = pack[pl.ds(0, block_rows), :]
        message[here, :] = contract(grad, w_neigh[...], 1, 1).astype(BF16)
    total[...] = contract(dense[...], message[...], 1, 0) * norm

    @pl.when(me_rep == q)
    def _():
        total[...] += contract(packs[0][pl.ds(0, block_rows), :], w_self[...], 1, 1)

    own[...] = piece_of(total, me_rep, share).astype(BF16)
    for j, out in enumerate(outs):
        out[pl.ds(0, share), :] = piece_of(total, me_rep ^ mask_of(q, j), share).astype(BF16)
    outs[0][pl.ds(share, share), :] = act[...]


def level_kernel(rows, factor, *refs):
    parts, (bias, summed) = refs[:-2], refs[-2:]
    terms = tree_sum([ref[...].astype(F32) for ref in parts])
    tail = terms[2 * rows : 2 * rows + 8]
    bias[...] = (tail[0:1] + tail[1:2]) * factor
    summed[...] = terms[: 2 * rows].astype(BF16)


def pick_kernel(sections, act, came, out):
    q, _ = place_of(sections)
    share = act.shape[0]
    arrived = came[pl.ds(share, share), :].astype(F32)
    out[...] = jnp.where(q == 0, act[...].astype(F32), arrived).astype(BF16)


def last_kernel(*refs):
    parts, (act, grad_features, activations) = refs[:-3], refs[-3:]
    here = pl.ds(0, grad_features.shape[0])
    grad_features[...] = tree_sum([ref[here, :].astype(F32) for ref in parts]).astype(BF16)
    activations[...] = act[...]


def join_kernel(sections, *refs):
    pieces, out = refs[:-1], refs[-1]
    span = pieces[0].shape[0]
    q, _ = place_of(sections)
    for k, piece in enumerate(pieces):
        slot = (q % len(pieces)) ^ k
        out[pl.ds(pl.multiple_of(slot * span, 16), span), :] = piece[...]


def collect_kernel(rows, factor, *refs):
    joined, (grad_self, grad_neigh) = refs[:-2], refs[-2:]
    sections = len(joined)
    _, s = place_of(sections)
    for k, ref in enumerate(joined):
        for j in range(ref.shape[0] // (2 * rows)):
            place = pl.ds(pl.multiple_of((j * sections + (s ^ k)) * rows, rows), rows)
            base = j * 2 * rows
            grad_self[place, :] = ref[pl.ds(base, rows), :].astype(F32) * factor
            grad_neigh[place, :] = ref[pl.ds(base + rows, rows), :].astype(F32) * factor


def shards(
    features, w_self, w_neigh, bias_vector, cotangent, adj_values, src_slots, dst_slots, slot_counts
):
    block_rows, width = features.shape
    blocks, replicas = lax.axis_size("row"), lax.axis_size("rep")
    sections = blocks // replicas
    share = block_rows // replicas
    slot_total, size = adj_values.shape[2], adj_values.shape[-1]
    norm = 1.0 / math.sqrt(slot_total * replicas / (block_rows // size))
    factor = 1.0 / math.sqrt(block_rows * blocks)
    parts = min(blocks, width // 16)
    rows = width // parts

    def flat(q, s, c):
        return (q * sections + s) * replicas + c

    places = [
        (q, s, c) for q in range(replicas) for s in range(sections) for c in range(replicas)
    ]
    here = [flat(q, s, c) for q, s, c in places]
    source = [flat(c, s, q ^ turn(c, replicas)) for q, s, c in places]
    inside = [flat(q ^ c, s, c) for q, s, c in places]

    def swap_level(value, j):
        level = [flat(q, s, c ^ masks(q, replicas)[j]) for q, s, c in places]
        return lax.ppermute(value, ("row", "rep"), list(zip(here, level)))

    plane_rows = sections * block_rows
    pair, own, *sent = call(
        functools.partial(first_kernel, sections),
        [shape((2 * share, width), BF16)]
        + [shape((block_rows, width), BF16)] * sections,
        [SMEM] * 3 + [HBM] * 3,
        [
            pltpu.VMEM((block_rows, plane_rows), BF16),
            pltpu.VMEM((block_rows, width), BF16),
            pltpu.VMEM((plane_rows, width), F32),
            pltpu.SemaphoreType.DMA((slot_total,)),
            pltpu.SemaphoreType.DMA((2,)),
        ],
        flops=2 * plane_rows * block_rows * width,
        limit=54400 * 1024,
    )(src_slots, dst_slots, slot_counts, adj_values, features, cotangent)
    pair = lax.ppermute(pair, ("row", "rep"), list(zip(source, here)))
    received = [swap(value, k) for k, value in enumerate(sent, 1)]

    own, *sent = call(
        functools.partial(block_kernel, sections),
        [shape((share, width), F32)] + [shape((share, width), BF16)] * (replicas - 1),
        [VMEM] * sections,
        [pltpu.VMEM((block_rows, width), F32)],
    )(own, *received)
    received = [swap(value, k * sections) for k, value in enumerate(sent, 1)]

    dense, bias = call(
        dense_kernel,
        [shape((block_rows, plane_rows), BF16), shape((1, width), F32)],
        [SMEM] * 3 + [HBM, VMEM],
        [pltpu.SemaphoreType.DMA((slot_total,))],
        limit=51 * 1024 * 1024,
    )(src_slots, dst_slots, slot_counts, adj_values, bias_vector[None, :])
    dense, received[0] = lax.optimization_barrier((dense, received[0]))
    act, *letters = call(
        functools.partial(middle_kernel, norm, sections, replicas, parts),
        [shape((share, width), BF16)]
        + [shape((share + sections * rows, width), BF16)] * replicas,
        [VMEM] * (replicas + 4),
        [pltpu.VMEM((width, share), BF16)] * 2,
    )(own, *received, pair, w_self, w_neigh, bias)
    letters = letters[:1] + [swap(v, k * sections) for k, v in enumerate(letters[1:], 1)]

    packs = call(
        functools.partial(pack_kernel, sections, share, rows),
        [shape((replicas * (share + rows), width), BF16)] * sections,
        [VMEM] * replicas,
    )(*letters)
    packs = packs[:1] + [swap(value, k) for k, value in enumerate(packs[1:], 1)]

    (terms,) = call(
        functools.partial(terms_kernel, share, rows),
        [shape((2 * rows + 16, width), BF16)],
        [VMEM] * sections,
        flops=2 * plane_rows * width * (2 * rows + 16),
    )(*packs)
    terms, *packs = lax.optimization_barrier((terms, *packs))
    terms = [terms] + [swap_rep(terms, k) for k in range(1, replicas)]

    sent = call(
        functools.partial(back_kernel, norm, sections, replicas),
        [shape((share, width), BF16), shape((2 * share, width), BF16)]
        + [shape((share, width), BF16)] * (replicas - 2),
        [VMEM] * (sections + 4),
        [pltpu.VMEM((plane_rows, width), BF16), pltpu.VMEM((block_rows, width), F32)],
        flops=2 * plane_rows * width * (block_rows + width),
    )(*packs, dense, w_self, w_neigh, act)
    received = [swap_level(value, j) for j, value in enumerate(sent[2:], 1)]
    _, *terms = lax.optimization_barrier((sent[0], *terms))
    grad_bias, summed = call(
        functools.partial(level_kernel, rows, factor),
        [shape((1, width), F32), shape((2 * rows, width), BF16)],
        [VMEM] * replicas,
    )(*terms)
    summed, loaded = lax.optimization_barrier((summed, sent[1]))
    loaded = swap_level(loaded, 0)
    (act,) = call(
        functools.partial(pick_kernel, sections),
        [shape((share, width), BF16)],
        [VMEM] * 2,
    )(act, loaded)
    act = lax.ppermute(act, ("row", "rep"), list(zip(here, inside)))
    spread = parts // sections
    pieces = [summed] + [swap(summed, k * sections) for k in range(1, spread)]
    pieces[-1], *received = lax.optimization_barrier((pieces[-1], *received))
    (joined,) = call(
        functools.partial(join_kernel, sections),
        [shape((spread * 2 * rows, width), BF16)],
        [VMEM] * spread,
    )(*pieces)
    joined = [joined] + [swap(joined, k) for k in range(1, sections)]
    grad_self, grad_neigh = call(
        functools.partial(collect_kernel, rows, factor),
        [shape((width, width), F32)] * 2,
        [VMEM] * sections,
    )(*joined)
    grad_features, activations = call(
        last_kernel, [shape((share, width), BF16)] * 2, [VMEM] * (replicas + 1)
    )(sent[0], loaded, *received, act)
    return activations, grad_features, grad_self, grad_neigh, grad_bias[0]


def solution(mesh):
    placed = (
        P("row", None),
        P(),
        P(),
        P(),
        P("row", None),
        P("row", "rep", None, None, None),
        P("row", "rep", None),
        P("row", "rep", None),
        P("row", "rep"),
    )
    return jax.shard_map(
        shards,
        mesh=mesh,
        in_specs=placed,
        out_specs=(P(("row", "rep"), None), P(("row", "rep"), None), P(), P(), P()),
        check_vma=False,
    )
```

```python
import functools
import math

import jax
import jax.numpy as jnp
from jax import lax
from jax.experimental import pallas as pl
from jax.experimental.pallas import tpu as pltpu
from jax.sharding import PartitionSpec as P

F32 = jnp.float32
BF16 = jnp.bfloat16
VMEM = pl.BlockSpec(memory_space=pltpu.VMEM)
HBM = pl.BlockSpec(memory_space=pltpu.HBM)
SMEM = pl.BlockSpec(memory_space=pltpu.SMEM)
LIMIT = 16 * 1024 * 1024


def call(body, outs, ins, scratch=(), flops=0, limit=LIMIT):
    size = sum(math.prod(out.shape) * out.dtype.itemsize for out in outs)
    kernel = pl.pallas_call(
        body,
        out_shape=outs,
        in_specs=ins,
        out_specs=[VMEM] * len(outs),
        scratch_shapes=list(scratch),
        compiler_params=pltpu.CompilerParams(vmem_limit_bytes=limit),
        cost_estimate=pl.CostEstimate(flops=flops, bytes_accessed=2 * size, transcendentals=0),
    )
    return lambda *operands: list(kernel(*operands))


def shape(dims, kind):
    return jax.ShapeDtypeStruct(tuple(dims), kind)


def swap(value, step):
    return lax.ppermute(value, "row", [(i, i ^ step) for i in range(lax.axis_size("row"))])


def swap_rep(value, step):
    return lax.ppermute(value, "rep", [(i, i ^ step) for i in range(lax.axis_size("rep"))])


def contract(left, right, left_dim, right_dim):
    return lax.dot_general(
        left, right, (((left_dim,), (right_dim,)), ((), ())), preferred_element_type=F32
    )


def tree_sum(parts):
    while len(parts) > 1:
        parts = [parts[i] + parts[i + 1] for i in range(0, len(parts), 2)]
    return parts[0]


def place_of(sections):
    me = lax.axis_index("row")
    return me // sections, me % sections


def turn(c, replicas):
    out, bits = 0, replicas.bit_length() - 1
    for i in range(bits):
        out = out | ((c >> i) & 1) << (bits - 1 - i)
    return out


def tile_of(sections):
    return place_of(sections)[0] ^ lax.axis_index("rep")


def masks(first, count):
    first = first or 1
    return [first] + [m for m in range(1, count) if m != first]


def mask_of(first, j):
    first = jnp.where(first == 0, 1, first)
    return first if j == 0 else jnp.where(j >= first, j + 1, j)


def piece_of(ref, index, span):
    return ref[pl.ds(pl.multiple_of(index * span, span), span), :]


def tile_copies(src, dst, live, tiles, dense, sems):
    size = tiles.shape[-1]

    def tile_copy(e):
        row = pl.multiple_of(dst[0, 0, e] * size, size)
        col = pl.multiple_of(src[0, 0, e] * size, size)
        target = dense.at[pl.ds(row, size), pl.ds(col, size)]
        return pltpu.make_async_copy(tiles.at[0, 0, e], target, sems.at[e])

    def start():
        lax.fori_loop(0, live, lambda e, carry: (tile_copy(e).start(), carry)[1], 0)

    def wait():
        lax.fori_loop(0, live, lambda e, carry: (tile_copy(e).wait(), carry)[1], 0)

    return start, wait


def dense_kernel(src, dst, count, tiles, bias, dense, bias_out, sems):
    bias_out[...] = bias[...]
    dense[...] = jnp.zeros_like(dense)
    start, wait = tile_copies(src, dst, count[0, 0], tiles, dense, sems)
    start()
    wait()


def first_kernel(sections, src, dst, count, tiles, field, cotangent, *refs):
    pair, own = refs[:2]
    others, (dense, held, total, sems, own_sems) = refs[2:-5], refs[-5:]
    size = tiles.shape[-1]
    block_rows = field.shape[0]
    share = pair.shape[0] // 2
    chip, s = place_of(sections)
    turned = turn(chip, block_rows // share)
    offset = pl.multiple_of((lax.axis_index("rep") ^ turned ^ chip) * share, share)
    field_copy = pltpu.make_async_copy(field, held, own_sems.at[0])
    field_copy.start()
    cotangent_copy = pltpu.make_async_copy(
        cotangent.at[pl.ds(offset, share), :], pair.at[pl.ds(share, share), :], own_sems.at[1]
    )
    cotangent_copy.start()
    dense[...] = jnp.zeros_like(dense)
    start, wait = tile_copies(src, dst, count[0, 0], tiles, dense, sems)
    start()
    field_copy.wait()
    pair[pl.ds(0, share), :] = held[pl.ds(offset, share), :]
    wait()
    for t in range(dense.shape[1] // size):
        cols = pl.ds(t * size, size)
        total[cols, :] = contract(dense[:, cols], held[...], 0, 0)
    own[...] = piece_of(total, s, block_rows).astype(BF16)
    for k, out in enumerate(others, 1):
        out[...] = piece_of(total, s ^ k, block_rows).astype(BF16)
    cotangent_copy.wait()


def block_kernel(sections, *refs):
    parts, own, others, total = refs[:sections], refs[sections], refs[sections + 1 : -1], refs[-1]
    share = own.shape[0]
    tile = tile_of(sections)
    value = parts[0][...].astype(F32)
    for ref in parts[1:]:
        value = value + ref[...].astype(F32)
    total[...] = value
    own[...] = piece_of(total, tile, share)
    for k, out in enumerate(others, 1):
        out[...] = piece_of(total, tile ^ k, share).astype(BF16)


def middle_kernel(norm, sections, replicas, parts, *refs):
    tiles, (pair, w_self, w_neigh, bias, act) = refs[:replicas], refs[replicas : replicas + 5]
    letters, (turned_f, turned_a) = refs[replicas + 5 : -2], refs[-2:]
    share, width = act.shape
    rows = width // parts
    q, _ = place_of(sections)
    total = tiles[0][...]
    for ref in tiles[1:]:
        total = total + ref[...].astype(F32)
    aggregate = (total * norm).astype(BF16)
    field = pair[pl.ds(0, share), :]
    pre = contract(field, w_self[...], 1, 0) + contract(aggregate, w_neigh[...], 1, 0)
    pre = pre + bias[...]
    slope = jnp.exp(jnp.minimum(pre, 0.0))
    act[...] = jnp.where(pre > 0.0, pre, slope - 1.0).astype(BF16)
    grad = (pair[pl.ds(share, share), :].astype(F32) * slope).astype(BF16)
    turned_f[...] = field.T
    turned_a[...] = aggregate.T
    span = sections * rows
    for k, letter in enumerate(letters):
        slot = (q ^ k) % (parts // sections)
        letter[pl.ds(0, share), :] = grad
        letter[pl.ds(share, span), pl.ds(0, share)] = piece_of(turned_f, slot, span)
        letter[pl.ds(share, span), pl.ds(128, share)] = piece_of(turned_a, slot, span)


def pack_kernel(sections, share, rows, *refs):
    letters, packs = refs[:-sections], refs[-sections:]
    _, s = place_of(sections)
    tile = tile_of(sections)
    block_rows = len(letters) * share
    for k, letter in enumerate(letters):
        here = pl.ds(pl.multiple_of((tile ^ k) * share, share), share)
        turned = pl.ds(pl.multiple_of(block_rows + (tile ^ k) * rows, rows), rows)
        for m, pack in enumerate(packs):
            first = pl.multiple_of(share + (s ^ m) * rows, 16)
            pack[here, :] = letter[pl.ds(0, share), :]
            pack[turned, :] = letter[pl.ds(first, rows), :]


def terms_kernel(share, rows, *refs):
    packs, out = refs[:-1], refs[-1]
    width = out.shape[1]
    replicas = packs[0].shape[0] // (share + rows)
    ones = jnp.ones((16, share), BF16)
    sums = []
    for pack in packs:
        total = jnp.zeros((2 * rows + 16, width), F32)
        for i in range(replicas):
            turned = pl.ds(replicas * share + i * rows, rows)
            field, aggregate = pack[turned, pl.ds(0, share)], pack[turned, pl.ds(128, share)]
            left = jnp.concatenate([field, aggregate, ones])
            total += contract(left, pack[pl.ds(i * share, share), :], 1, 0)
        sums.append(total)
    total = tree_sum(sums)
    tail = total[2 * rows :]
    high = tail.astype(BF16).astype(F32)
    line = lax.broadcasted_iota(jnp.int32, tail.shape, 0)
    out[pl.ds(0, 2 * rows), :] = total[: 2 * rows].astype(BF16)
    out[pl.ds(2 * rows, 16), :] = jnp.where(line == 0, high, tail - high).astype(BF16)


def back_kernel(norm, sections, replicas, *refs):
    packs, (dense, w_self, w_neigh, act) = refs[:sections], refs[sections : sections + 4]
    own, outs, (message, total) = refs[sections + 4], refs[sections + 5 : -2], refs[-2:]
    me_rep = lax.axis_index("rep")
    q, s = place_of(sections)
    block_rows = dense.shape[0]
    share = block_rows // replicas
    for k, pack in enumerate(packs):
        here = pl.ds(pl.multiple_of((s ^ k) * block_rows, block_rows), block_rows)
        grad = pack[pl.ds(0, block_rows), :]
        message[here, :] = contract(grad, w_neigh[...], 1, 1).astype(BF16)
    total[...] = contract(dense[...], message[...], 1, 0) * norm

    @pl.when(me_rep == q)
    def _():
        total[...] += contract(packs[0][pl.ds(0, block_rows), :], w_self[...], 1, 1)

    own[...] = piece_of(total, me_rep, share).astype(BF16)
    for j, out in enumerate(outs):
        out[pl.ds(0, share), :] = piece_of(total, me_rep ^ mask_of(q, j), share).astype(BF16)
    outs[0][pl.ds(share, share), :] = act[...]


def level_kernel(rows, factor, *refs):
    parts, (bias, summed) = refs[:-2], refs[-2:]
    terms = tree_sum([ref[...].astype(F32) for ref in parts])
    tail = terms[2 * rows : 2 * rows + 8]
    bias[...] = (tail[0:1] + tail[1:2]) * factor
    summed[...] = terms[: 2 * rows].astype(BF16)


def pick_kernel(sections, act, came, out):
    q, _ = place_of(sections)
    share = act.shape[0]
    arrived = came[pl.ds(share, share), :].astype(F32)
    out[...] = jnp.where(q == 0, act[...].astype(F32), arrived).astype(BF16)


def last_kernel(*refs):
    parts, (act, bias, grad_features, activations, grad_bias) = refs[:-5], refs[-5:]
    here = pl.ds(0, grad_features.shape[0])
    grad_features[...] = tree_sum([ref[here, :].astype(F32) for ref in parts]).astype(BF16)
    activations[...] = act[...]
    grad_bias[...] = bias[...]


def join_kernel(sections, *refs):
    pieces, out = refs[:-1], refs[-1]
    span = pieces[0].shape[0]
    q, _ = place_of(sections)
    for k, piece in enumerate(pieces):
        slot = (q % len(pieces)) ^ k
        out[pl.ds(pl.multiple_of(slot * span, 16), span), :] = piece[...]


def collect_kernel(rows, factor, *refs):
    joined, (grad_self, grad_neigh) = refs[:-2], refs[-2:]
    sections = len(joined)
    _, s = place_of(sections)
    for k, ref in enumerate(joined):
        for j in range(ref.shape[0] // (2 * rows)):
            place = pl.ds(pl.multiple_of((j * sections + (s ^ k)) * rows, rows), rows)
            base = j * 2 * rows
            grad_self[place, :] = ref[pl.ds(base, rows), :].astype(F32) * factor
            grad_neigh[place, :] = ref[pl.ds(base + rows, rows), :].astype(F32) * factor


def shards(
    features, w_self, w_neigh, bias_vector, cotangent, adj_values, src_slots, dst_slots, slot_counts
):
    block_rows, width = features.shape
    blocks, replicas = lax.axis_size("row"), lax.axis_size("rep")
    sections = blocks // replicas
    share = block_rows // replicas
    slot_total, size = adj_values.shape[2], adj_values.shape[-1]
    norm = 1.0 / math.sqrt(slot_total * replicas / (block_rows // size))
    factor = 1.0 / math.sqrt(block_rows * blocks)
    parts = min(blocks, width // 16)
    rows = width // parts

    def flat(q, s, c):
        return (q * sections + s) * replicas + c

    places = [
        (q, s, c) for q in range(replicas) for s in range(sections) for c in range(replicas)
    ]
    here = [flat(q, s, c) for q, s, c in places]
    source = [flat(c, s, q ^ turn(c, replicas)) for q, s, c in places]
    inside = [flat(q ^ c, s, c) for q, s, c in places]

    def swap_level(value, j):
        level = [flat(q, s, c ^ masks(q, replicas)[j]) for q, s, c in places]
        return lax.ppermute(value, ("row", "rep"), list(zip(here, level)))

    plane_rows = sections * block_rows
    pair, own, *sent = call(
        functools.partial(first_kernel, sections),
        [shape((2 * share, width), BF16)]
        + [shape((block_rows, width), BF16)] * sections,
        [SMEM] * 3 + [HBM] * 3,
        [
            pltpu.VMEM((block_rows, plane_rows), BF16),
            pltpu.VMEM((block_rows, width), BF16),
            pltpu.VMEM((plane_rows, width), F32),
            pltpu.SemaphoreType.DMA((slot_total,)),
            pltpu.SemaphoreType.DMA((2,)),
        ],
        flops=2 * plane_rows * block_rows * width,
        limit=54400 * 1024,
    )(src_slots, dst_slots, slot_counts, adj_values, features, cotangent)
    pair = lax.ppermute(pair, ("row", "rep"), list(zip(source, here)))
    received = [swap(value, k) for k, value in enumerate(sent, 1)]

    own, *sent = call(
        functools.partial(block_kernel, sections),
        [shape((share, width), F32)] + [shape((share, width), BF16)] * (replicas - 1),
        [VMEM] * sections,
        [pltpu.VMEM((block_rows, width), F32)],
    )(own, *received)
    received = [swap(value, k * sections) for k, value in enumerate(sent, 1)]

    dense, bias = call(
        dense_kernel,
        [shape((block_rows, plane_rows), BF16), shape((1, width), F32)],
        [SMEM] * 3 + [HBM, VMEM],
        [pltpu.SemaphoreType.DMA((slot_total,))],
        limit=51 * 1024 * 1024,
    )(src_slots, dst_slots, slot_counts, adj_values, bias_vector[None, :])
    dense, received[0] = lax.optimization_barrier((dense, received[0]))
    act, *letters = call(
        functools.partial(middle_kernel, norm, sections, replicas, parts),
        [shape((share, width), BF16)]
        + [shape((share + sections * rows, width), BF16)] * replicas,
        [VMEM] * (replicas + 4),
        [pltpu.VMEM((width, share), BF16)] * 2,
    )(own, *received, pair, w_self, w_neigh, bias)
    letters = letters[:1] + [swap(v, k * sections) for k, v in enumerate(letters[1:], 1)]

    packs = call(
        functools.partial(pack_kernel, sections, share, rows),
        [shape((replicas * (share + rows), width), BF16)] * sections,
        [VMEM] * replicas,
    )(*letters)
    packs = packs[:1] + [swap(value, k) for k, value in enumerate(packs[1:], 1)]

    (terms,) = call(
        functools.partial(terms_kernel, share, rows),
        [shape((2 * rows + 16, width), BF16)],
        [VMEM] * sections,
        flops=2 * plane_rows * width * (2 * rows + 16),
    )(*packs)
    terms, *packs = lax.optimization_barrier((terms, *packs))
    terms = [terms] + [swap_rep(terms, k) for k in range(1, replicas)]

    sent = call(
        functools.partial(back_kernel, norm, sections, replicas),
        [shape((share, width), BF16), shape((2 * share, width), BF16)]
        + [shape((share, width), BF16)] * (replicas - 2),
        [VMEM] * (sections + 4),
        [pltpu.VMEM((plane_rows, width), BF16), pltpu.VMEM((block_rows, width), F32)],
        flops=2 * plane_rows * width * (block_rows + width),
    )(*packs, dense, w_self, w_neigh, act)
    received = [swap_level(value, j) for j, value in enumerate(sent[2:], 1)]
    _, *terms = lax.optimization_barrier((sent[0], *terms))
    grad_bias, summed = call(
        functools.partial(level_kernel, rows, factor),
        [shape((1, width), F32), shape((2 * rows, width), BF16)],
        [VMEM] * replicas,
    )(*terms)
    summed, loaded = lax.optimization_barrier((summed, sent[1]))
    loaded = swap_level(loaded, 0)
    (act,) = call(
        functools.partial(pick_kernel, sections),
        [shape((share, width), BF16)],
        [VMEM] * 2,
    )(act, loaded)
    act = lax.ppermute(act, ("row", "rep"), list(zip(here, inside)))
    spread = parts // sections
    pieces = [summed] + [swap(summed, k * sections) for k in range(1, spread)]
    pieces[-1], *received = lax.optimization_barrier((pieces[-1], *received))
    (joined,) = call(
        functools.partial(join_kernel, sections),
        [shape((spread * 2 * rows, width), BF16)],
        [VMEM] * spread,
    )(*pieces)
    joined = [joined] + [swap(joined, k) for k in range(1, sections)]
    grad_self, grad_neigh = call(
        functools.partial(collect_kernel, rows, factor),
        [shape((width, width), F32)] * 2,
        [VMEM] * sections,
    )(*joined)
    grad_features, activations, grad_bias = call(
        last_kernel,
        [shape((share, width), BF16)] * 2 + [shape((1, width), F32)],
        [VMEM] * (replicas + 2),
    )(sent[0], loaded, *received, act, grad_bias)
    return activations, grad_features, grad_self, grad_neigh, grad_bias[0]


def solution(mesh):
    placed = (
        P("row", None),
        P(),
        P(),
        P(),
        P("row", None),
        P("row", "rep", None, None, None),
        P("row", "rep", None),
        P("row", "rep", None),
        P("row", "rep"),
    )
    return jax.shard_map(
        shards,
        mesh=mesh,
        in_specs=placed,
        out_specs=(P(("row", "rep"), None), P(("row", "rep"), None), P(), P(), P()),
        check_vma=False,
    )
```

```python
import functools
import math

import jax
import jax.numpy as jnp
from jax import lax
from jax.experimental import pallas as pl
from jax.experimental.pallas import tpu as pltpu
from jax.sharding import PartitionSpec as P

F32 = jnp.float32
BF16 = jnp.bfloat16
VMEM = pl.BlockSpec(memory_space=pltpu.VMEM)
HBM = pl.BlockSpec(memory_space=pltpu.HBM)
SMEM = pl.BlockSpec(memory_space=pltpu.SMEM)
LIMIT = 16 * 1024 * 1024


def call(body, outs, ins, scratch=(), flops=0, limit=LIMIT):
    size = sum(math.prod(out.shape) * out.dtype.itemsize for out in outs)
    kernel = pl.pallas_call(
        body,
        out_shape=outs,
        in_specs=ins,
        out_specs=[VMEM] * len(outs),
        scratch_shapes=list(scratch),
        compiler_params=pltpu.CompilerParams(vmem_limit_bytes=limit),
        cost_estimate=pl.CostEstimate(flops=flops, bytes_accessed=2 * size, transcendentals=0),
    )
    return lambda *operands: list(kernel(*operands))


def shape(dims, kind):
    return jax.ShapeDtypeStruct(tuple(dims), kind)


def swap(value, step):
    return lax.ppermute(value, "row", [(i, i ^ step) for i in range(lax.axis_size("row"))])


def swap_rep(value, step):
    return lax.ppermute(value, "rep", [(i, i ^ step) for i in range(lax.axis_size("rep"))])


def contract(left, right, left_dim, right_dim):
    return lax.dot_general(
        left, right, (((left_dim,), (right_dim,)), ((), ())), preferred_element_type=F32
    )


def tree_sum(parts):
    while len(parts) > 1:
        parts = [parts[i] + parts[i + 1] for i in range(0, len(parts), 2)]
    return parts[0]


def place_of(sections):
    me = lax.axis_index("row")
    return me // sections, me % sections


def turn(c, replicas):
    out, bits = 0, replicas.bit_length() - 1
    for i in range(bits):
        out = out | ((c >> i) & 1) << (bits - 1 - i)
    return out


def tile_of(sections):
    return place_of(sections)[0] ^ lax.axis_index("rep")


def masks(first, count):
    first = first or 1
    return [first] + [m for m in range(1, count) if m != first]


def mask_of(first, j):
    first = jnp.where(first == 0, 1, first)
    return first if j == 0 else jnp.where(j >= first, j + 1, j)


def piece_of(ref, index, span):
    return ref[pl.ds(pl.multiple_of(index * span, span), span), :]


def tile_copies(src, dst, live, tiles, dense, sems):
    size = tiles.shape[-1]

    def tile_copy(e):
        row = pl.multiple_of(dst[0, 0, e] * size, size)
        col = pl.multiple_of(src[0, 0, e] * size, size)
        target = dense.at[pl.ds(row, size), pl.ds(col, size)]
        return pltpu.make_async_copy(tiles.at[0, 0, e], target, sems.at[e])

    def start():
        lax.fori_loop(0, live, lambda e, carry: (tile_copy(e).start(), carry)[1], 0)

    def wait():
        lax.fori_loop(0, live, lambda e, carry: (tile_copy(e).wait(), carry)[1], 0)

    return start, wait


def dense_kernel(src, dst, count, tiles, bias, dense, bias_out, sems):
    bias_out[...] = bias[...]
    dense[...] = jnp.zeros_like(dense)
    start, wait = tile_copies(src, dst, count[0, 0], tiles, dense, sems)
    start()
    wait()


def first_kernel(sections, src, dst, count, tiles, field, cotangent, *refs):
    pair, own = refs[:2]
    others, (dense, held, total, sems, own_sems) = refs[2:-5], refs[-5:]
    size = tiles.shape[-1]
    block_rows = field.shape[0]
    share = pair.shape[0] // 2
    chip, s = place_of(sections)
    turned = turn(chip, block_rows // share)
    offset = pl.multiple_of((lax.axis_index("rep") ^ turned ^ chip) * share, share)
    field_copy = pltpu.make_async_copy(field, held, own_sems.at[0])
    field_copy.start()
    cotangent_copy = pltpu.make_async_copy(
        cotangent.at[pl.ds(offset, share), :], pair.at[pl.ds(share, share), :], own_sems.at[1]
    )
    cotangent_copy.start()
    dense[...] = jnp.zeros_like(dense)
    start, wait = tile_copies(src, dst, count[0, 0], tiles, dense, sems)
    start()
    field_copy.wait()
    pair[pl.ds(0, share), :] = held[pl.ds(offset, share), :]
    wait()
    for t in range(dense.shape[1] // size):
        cols = pl.ds(t * size, size)
        total[cols, :] = contract(dense[:, cols], held[...], 0, 0)
    own[...] = piece_of(total, s, block_rows).astype(BF16)
    for k, out in enumerate(others, 1):
        out[...] = piece_of(total, s ^ k, block_rows).astype(BF16)
    cotangent_copy.wait()


def block_kernel(sections, *refs):
    parts, own, others, total = refs[:sections], refs[sections], refs[sections + 1 : -1], refs[-1]
    share = own.shape[0]
    tile = tile_of(sections)
    value = parts[0][...].astype(F32)
    for ref in parts[1:]:
        value = value + ref[...].astype(F32)
    total[...] = value
    own[...] = piece_of(total, tile, share)
    for k, out in enumerate(others, 1):
        out[...] = piece_of(total, tile ^ k, share).astype(BF16)


def middle_kernel(norm, sections, replicas, parts, *refs):
    tiles, (pair, w_self, w_neigh, bias, act) = refs[:replicas], refs[replicas : replicas + 5]
    letters, (turned_f, turned_a) = refs[replicas + 5 : -2], refs[-2:]
    share, width = act.shape
    rows = width // parts
    q, _ = place_of(sections)
    total = tiles[0][...]
    for ref in tiles[1:]:
        total = total + ref[...].astype(F32)
    aggregate = (total * norm).astype(BF16)
    field = pair[pl.ds(0, share), :]
    pre = contract(field, w_self[...], 1, 0) + contract(aggregate, w_neigh[...], 1, 0)
    pre = pre + bias[...]
    slope = jnp.exp(jnp.minimum(pre, 0.0))
    act[...] = jnp.where(pre > 0.0, pre, slope - 1.0).astype(BF16)
    grad = (pair[pl.ds(share, share), :].astype(F32) * slope).astype(BF16)
    turned_f[...] = field.T
    turned_a[...] = aggregate.T
    span = sections * rows
    for k, letter in enumerate(letters):
        slot = (q ^ k) % (parts // sections)
        letter[pl.ds(0, share), :] = grad
        letter[pl.ds(share, span), pl.ds(0, share)] = piece_of(turned_f, slot, span)
        letter[pl.ds(share, span), pl.ds(128, share)] = piece_of(turned_a, slot, span)


def pack_kernel(sections, share, rows, *refs):
    letters, packs = refs[:-sections], refs[-sections:]
    _, s = place_of(sections)
    tile = tile_of(sections)
    block_rows = len(letters) * share
    for k, letter in enumerate(letters):
        here = pl.ds(pl.multiple_of((tile ^ k) * share, share), share)
        turned = pl.ds(pl.multiple_of(block_rows + (tile ^ k) * rows, rows), rows)
        for m, pack in enumerate(packs):
            first = pl.multiple_of(share + (s ^ m) * rows, 16)
            pack[here, :] = letter[pl.ds(0, share), :]
            pack[turned, :] = letter[pl.ds(first, rows), :]


def terms_kernel(share, rows, *refs):
    packs, out = refs[:-1], refs[-1]
    width = out.shape[1]
    replicas = packs[0].shape[0] // (share + rows)
    ones = jnp.ones((16, share), BF16)
    sums = []
    for pack in packs:
        total = jnp.zeros((2 * rows + 16, width), F32)
        for i in range(replicas):
            turned = pl.ds(replicas * share + i * rows, rows)
            field, aggregate = pack[turned, pl.ds(0, share)], pack[turned, pl.ds(128, share)]
            left = jnp.concatenate([field, aggregate, ones])
            total += contract(left, pack[pl.ds(i * share, share), :], 1, 0)
        sums.append(total)
    total = tree_sum(sums)
    tail = total[2 * rows :]
    high = tail.astype(BF16).astype(F32)
    line = lax.broadcasted_iota(jnp.int32, tail.shape, 0)
    out[pl.ds(0, 2 * rows), :] = total[: 2 * rows].astype(BF16)
    out[pl.ds(2 * rows, 16), :] = jnp.where(line == 0, high, tail - high).astype(BF16)


def back_kernel(norm, sections, replicas, *refs):
    packs, (dense, w_self, w_neigh, act) = refs[:sections], refs[sections : sections + 4]
    own, outs, (message, total) = refs[sections + 4], refs[sections + 5 : -2], refs[-2:]
    me_rep = lax.axis_index("rep")
    q, s = place_of(sections)
    block_rows = dense.shape[0]
    share = block_rows // replicas
    for k, pack in enumerate(packs):
        here = pl.ds(pl.multiple_of((s ^ k) * block_rows, block_rows), block_rows)
        grad = pack[pl.ds(0, block_rows), :]
        message[here, :] = contract(grad, w_neigh[...], 1, 1).astype(BF16)
    total[...] = contract(dense[...], message[...], 1, 0) * norm

    @pl.when(me_rep == q)
    def _():
        total[...] += contract(packs[0][pl.ds(0, block_rows), :], w_self[...], 1, 1)

    own[...] = piece_of(total, me_rep, share).astype(BF16)
    for j, out in enumerate(outs):
        out[pl.ds(0, share), :] = piece_of(total, me_rep ^ mask_of(q, j), share).astype(BF16)
    outs[0][pl.ds(share, share), :] = act[...]


def level_kernel(rows, factor, *refs):
    parts, (bias, summed) = refs[:-2], refs[-2:]
    terms = tree_sum([ref[...].astype(F32) for ref in parts])
    tail = terms[2 * rows : 2 * rows + 8]
    bias[...] = (tail[0:1] + tail[1:2]) * factor
    summed[...] = terms[: 2 * rows].astype(BF16)


def pick_kernel(sections, act, came, out):
    q, _ = place_of(sections)
    share = act.shape[0]
    arrived = came[pl.ds(share, share), :].astype(F32)
    out[...] = jnp.where(q == 0, act[...].astype(F32), arrived).astype(BF16)


def last_kernel(*refs):
    parts, (act, bias, grad_features, activations, grad_bias) = refs[:-5], refs[-5:]
    here = pl.ds(0, grad_features.shape[0])
    grad_features[...] = tree_sum([ref[here, :].astype(F32) for ref in parts]).astype(BF16)
    activations[...] = act[...]
    grad_bias[...] = bias[...]


def join_kernel(sections, *refs):
    pieces, out = refs[:-1], refs[-1]
    span = pieces[0].shape[0]
    q, _ = place_of(sections)
    for k, piece in enumerate(pieces):
        slot = (q % len(pieces)) ^ k
        out[pl.ds(pl.multiple_of(slot * span, 16), span), :] = piece[...]


def collect_kernel(rows, factor, *refs):
    joined, (grad_self, grad_neigh) = refs[:-2], refs[-2:]
    sections = len(joined)
    _, s = place_of(sections)
    for k, ref in enumerate(joined):
        for j in range(ref.shape[0] // (2 * rows)):
            place = pl.ds(pl.multiple_of((j * sections + (s ^ k)) * rows, rows), rows)
            base = j * 2 * rows
            grad_self[place, :] = ref[pl.ds(base, rows), :].astype(F32) * factor
            grad_neigh[place, :] = ref[pl.ds(base + rows, rows), :].astype(F32) * factor


def shards(
    features, w_self, w_neigh, bias_vector, cotangent, adj_values, src_slots, dst_slots, slot_counts
):
    block_rows, width = features.shape
    blocks, replicas = lax.axis_size("row"), lax.axis_size("rep")
    sections = blocks // replicas
    share = block_rows // replicas
    slot_total, size = adj_values.shape[2], adj_values.shape[-1]
    norm = 1.0 / math.sqrt(slot_total * replicas / (block_rows // size))
    factor = 1.0 / math.sqrt(block_rows * blocks)
    parts = min(blocks, width // 16)
    rows = width // parts

    def flat(q, s, c):
        return (q * sections + s) * replicas + c

    places = [
        (q, s, c) for q in range(replicas) for s in range(sections) for c in range(replicas)
    ]
    here = [flat(q, s, c) for q, s, c in places]
    source = [flat(c, s, q ^ turn(c, replicas)) for q, s, c in places]
    inside = [flat(q ^ c, s, c) for q, s, c in places]

    def swap_level(value, j):
        level = [flat(q, s, c ^ masks(q, replicas)[j]) for q, s, c in places]
        return lax.ppermute(value, ("row", "rep"), list(zip(here, level)))

    plane_rows = sections * block_rows
    pair, own, *sent = call(
        functools.partial(first_kernel, sections),
        [shape((2 * share, width), BF16)]
        + [shape((block_rows, width), BF16)] * sections,
        [SMEM] * 3 + [HBM] * 3,
        [
            pltpu.VMEM((block_rows, plane_rows), BF16),
            pltpu.VMEM((block_rows, width), BF16),
            pltpu.VMEM((plane_rows, width), F32),
            pltpu.SemaphoreType.DMA((slot_total,)),
            pltpu.SemaphoreType.DMA((2,)),
        ],
        flops=2 * plane_rows * block_rows * width,
        limit=54400 * 1024,
    )(src_slots, dst_slots, slot_counts, adj_values, features, cotangent)
    pair = lax.ppermute(pair, ("row", "rep"), list(zip(source, here)))
    received = [swap(value, k) for k, value in enumerate(sent, 1)]

    own, *sent = call(
        functools.partial(block_kernel, sections),
        [shape((share, width), F32)] + [shape((share, width), BF16)] * (replicas - 1),
        [VMEM] * sections,
        [pltpu.VMEM((block_rows, width), F32)],
    )(own, *received)
    received = [swap(value, k * sections) for k, value in enumerate(sent, 1)]

    dense, bias = call(
        dense_kernel,
        [shape((block_rows, plane_rows), BF16), shape((1, width), F32)],
        [SMEM] * 3 + [HBM, VMEM],
        [pltpu.SemaphoreType.DMA((slot_total,))],
        limit=51 * 1024 * 1024,
    )(src_slots, dst_slots, slot_counts, adj_values, bias_vector[None, :])
    dense, received[0] = lax.optimization_barrier((dense, received[0]))
    act, *letters = call(
        functools.partial(middle_kernel, norm, sections, replicas, parts),
        [shape((share, width), BF16)]
        + [shape((share + sections * rows, width), BF16)] * replicas,
        [VMEM] * (replicas + 4),
        [pltpu.VMEM((width, share), BF16)] * 2,
    )(own, *received, pair, w_self, w_neigh, bias)
    letters = letters[:1] + [swap(v, k * sections) for k, v in enumerate(letters[1:], 1)]

    packs = call(
        functools.partial(pack_kernel, sections, share, rows),
        [shape((replicas * (share + rows), width), BF16)] * sections,
        [VMEM] * replicas,
    )(*letters)
    packs = packs[:1] + [swap(value, k) for k, value in enumerate(packs[1:], 1)]

    (terms,) = call(
        functools.partial(terms_kernel, share, rows),
        [shape((2 * rows + 16, width), BF16)],
        [VMEM] * sections,
        flops=2 * plane_rows * width * (2 * rows + 16),
    )(*packs)
    terms, *packs = lax.optimization_barrier((terms, *packs))
    terms = [terms] + [swap_rep(terms, k) for k in range(1, replicas)]

    sent = call(
        functools.partial(back_kernel, norm, sections, replicas),
        [shape((share, width), BF16), shape((2 * share, width), BF16)]
        + [shape((share, width), BF16)] * (replicas - 2),
        [VMEM] * (sections + 4),
        [pltpu.VMEM((plane_rows, width), BF16), pltpu.VMEM((block_rows, width), F32)],
        flops=2 * plane_rows * width * (block_rows + width),
    )(*packs, dense, w_self, w_neigh, act)
    received = [swap_level(value, j) for j, value in enumerate(sent[2:-1], 1)]
    _, *terms = lax.optimization_barrier((sent[0], *terms))
    grad_bias, summed = call(
        functools.partial(level_kernel, rows, factor),
        [shape((1, width), F32), shape((2 * rows, width), BF16)],
        [VMEM] * replicas,
    )(*terms)
    summed, loaded, far = lax.optimization_barrier((summed, sent[1], sent[-1]))
    loaded = swap_level(loaded, 0)
    far = swap_level(far, replicas - 2)
    (act,) = call(
        functools.partial(pick_kernel, sections),
        [shape((share, width), BF16)],
        [VMEM] * 2,
    )(act, loaded)
    act = lax.ppermute(act, ("row", "rep"), list(zip(here, inside)))
    spread = parts // sections
    pieces = [summed] + [swap(summed, k * sections) for k in range(1, spread)]
    pieces[-1], *received = lax.optimization_barrier((pieces[-1], *received))
    (joined,) = call(
        functools.partial(join_kernel, sections),
        [shape((spread * 2 * rows, width), BF16)],
        [VMEM] * spread,
    )(*pieces)
    joined = [joined] + [swap(joined, k) for k in range(1, sections)]
    grad_self, grad_neigh = call(
        functools.partial(collect_kernel, rows, factor),
        [shape((width, width), F32)] * 2,
        [VMEM] * sections,
    )(*joined)
    grad_features, activations, grad_bias = call(
        last_kernel,
        [shape((share, width), BF16)] * 2 + [shape((1, width), F32)],
        [VMEM] * (replicas + 2),
    )(sent[0], loaded, *received, far, act, grad_bias)
    return activations, grad_features, grad_self, grad_neigh, grad_bias[0]


def solution(mesh):
    placed = (
        P("row", None),
        P(),
        P(),
        P(),
        P("row", None),
        P("row", "rep", None, None, None),
        P("row", "rep", None),
        P("row", "rep", None),
        P("row", "rep"),
    )
    return jax.shard_map(
        shards,
        mesh=mesh,
        in_specs=placed,
        out_specs=(P(("row", "rep"), None), P(("row", "rep"), None), P(), P(), P()),
        check_vma=False,
    )
```

```python
import functools
import math

import jax
import jax.numpy as jnp
from jax import lax
from jax.experimental import pallas as pl
from jax.experimental.pallas import tpu as pltpu
from jax.sharding import PartitionSpec as P

F32 = jnp.float32
BF16 = jnp.bfloat16
VMEM = pl.BlockSpec(memory_space=pltpu.VMEM)
HBM = pl.BlockSpec(memory_space=pltpu.HBM)
SMEM = pl.BlockSpec(memory_space=pltpu.SMEM)
LIMIT = 16 * 1024 * 1024


def call(body, outs, ins, scratch=(), flops=0, limit=LIMIT):
    size = sum(math.prod(out.shape) * out.dtype.itemsize for out in outs)
    kernel = pl.pallas_call(
        body,
        out_shape=outs,
        in_specs=ins,
        out_specs=[VMEM] * len(outs),
        scratch_shapes=list(scratch),
        compiler_params=pltpu.CompilerParams(vmem_limit_bytes=limit),
        cost_estimate=pl.CostEstimate(flops=flops, bytes_accessed=2 * size, transcendentals=0),
    )
    return lambda *operands: list(kernel(*operands))


def shape(dims, kind):
    return jax.ShapeDtypeStruct(tuple(dims), kind)


def swap(value, step):
    return lax.ppermute(value, "row", [(i, i ^ step) for i in range(lax.axis_size("row"))])


def swap_rep(value, step):
    return lax.ppermute(value, "rep", [(i, i ^ step) for i in range(lax.axis_size("rep"))])


def contract(left, right, left_dim, right_dim):
    return lax.dot_general(
        left, right, (((left_dim,), (right_dim,)), ((), ())), preferred_element_type=F32
    )


def tree_sum(parts):
    while len(parts) > 1:
        parts = [parts[i] + parts[i + 1] for i in range(0, len(parts), 2)]
    return parts[0]


def place_of(sections):
    me = lax.axis_index("row")
    return me // sections, me % sections


def turn(c, replicas):
    out, bits = 0, replicas.bit_length() - 1
    for i in range(bits):
        out = out | ((c >> i) & 1) << (bits - 1 - i)
    return out


def tile_of(sections):
    return place_of(sections)[0] ^ lax.axis_index("rep")


def masks(first, count):
    first = first or 1
    return [first] + [m for m in range(1, count) if m != first]


def mask_of(first, j):
    first = jnp.where(first == 0, 1, first)
    return first if j == 0 else jnp.where(j >= first, j + 1, j)


def piece_of(ref, index, span):
    return ref[pl.ds(pl.multiple_of(index * span, span), span), :]


def tile_copies(src, dst, live, tiles, dense, sems):
    size = tiles.shape[-1]

    def tile_copy(e):
        row = pl.multiple_of(dst[0, 0, e] * size, size)
        col = pl.multiple_of(src[0, 0, e] * size, size)
        target = dense.at[pl.ds(row, size), pl.ds(col, size)]
        return pltpu.make_async_copy(tiles.at[0, 0, e], target, sems.at[e])

    def start():
        lax.fori_loop(0, live, lambda e, carry: (tile_copy(e).start(), carry)[1], 0)

    def wait():
        lax.fori_loop(0, live, lambda e, carry: (tile_copy(e).wait(), carry)[1], 0)

    return start, wait


def dense_kernel(src, dst, count, tiles, bias, dense, bias_out, sems):
    bias_out[...] = bias[...]
    dense[...] = jnp.zeros_like(dense)
    start, wait = tile_copies(src, dst, count[0, 0], tiles, dense, sems)
    start()
    wait()


def first_kernel(sections, src, dst, count, tiles, field, cotangent, *refs):
    pair, own = refs[:2]
    others, (dense, held, total, sems, own_sems) = refs[2:-5], refs[-5:]
    size = tiles.shape[-1]
    block_rows = field.shape[0]
    share = pair.shape[0] // 2
    chip, s = place_of(sections)
    turned = turn(chip, block_rows // share)
    offset = pl.multiple_of((lax.axis_index("rep") ^ turned ^ chip) * share, share)
    field_copy = pltpu.make_async_copy(field, held, own_sems.at[0])
    field_copy.start()
    cotangent_copy = pltpu.make_async_copy(
        cotangent.at[pl.ds(offset, share), :], pair.at[pl.ds(share, share), :], own_sems.at[1]
    )
    cotangent_copy.start()
    dense[...] = jnp.zeros_like(dense)
    start, wait = tile_copies(src, dst, count[0, 0], tiles, dense, sems)
    start()
    field_copy.wait()
    pair[pl.ds(0, share), :] = held[pl.ds(offset, share), :]
    wait()
    for t in range(dense.shape[1] // size):
        cols = pl.ds(t * size, size)
        total[cols, :] = contract(dense[:, cols], held[...], 0, 0)
    own[...] = piece_of(total, s, block_rows).astype(BF16)
    for k, out in enumerate(others, 1):
        out[...] = piece_of(total, s ^ k, block_rows).astype(BF16)
    cotangent_copy.wait()


def block_kernel(sections, *refs):
    parts, own, others, total = refs[:sections], refs[sections], refs[sections + 1 : -1], refs[-1]
    share = own.shape[0]
    tile = tile_of(sections)
    value = parts[0][...].astype(F32)
    for ref in parts[1:]:
        value = value + ref[...].astype(F32)
    total[...] = value
    own[...] = piece_of(total, tile, share)
    for k, out in enumerate(others, 1):
        out[...] = piece_of(total, tile ^ k, share).astype(BF16)


def middle_kernel(norm, sections, replicas, parts, *refs):
    tiles, (pair, w_self, w_neigh, bias, act) = refs[:replicas], refs[replicas : replicas + 5]
    letters, (turned_f, turned_a) = refs[replicas + 5 : -2], refs[-2:]
    share, width = act.shape
    rows = width // parts
    q, _ = place_of(sections)
    total = tiles[0][...]
    for ref in tiles[1:]:
        total = total + ref[...].astype(F32)
    aggregate = (total * norm).astype(BF16)
    field = pair[pl.ds(0, share), :]
    pre = contract(field, w_self[...], 1, 0) + contract(aggregate, w_neigh[...], 1, 0)
    pre = pre + bias[...]
    slope = jnp.exp(jnp.minimum(pre, 0.0))
    act[...] = jnp.where(pre > 0.0, pre, slope - 1.0).astype(BF16)
    grad = (pair[pl.ds(share, share), :].astype(F32) * slope).astype(BF16)
    turned_f[...] = field.T
    turned_a[...] = aggregate.T
    span = sections * rows
    for k, letter in enumerate(letters):
        slot = (q ^ k) % (parts // sections)
        letter[pl.ds(0, share), :] = grad
        letter[pl.ds(share, span), pl.ds(0, share)] = piece_of(turned_f, slot, span)
        letter[pl.ds(share, span), pl.ds(128, share)] = piece_of(turned_a, slot, span)


def pack_kernel(sections, share, rows, *refs):
    letters, packs = refs[:-sections], refs[-sections:]
    _, s = place_of(sections)
    tile = tile_of(sections)
    block_rows = len(letters) * share
    for k, letter in enumerate(letters):
        here = pl.ds(pl.multiple_of((tile ^ k) * share, share), share)
        turned = pl.ds(pl.multiple_of(block_rows + (tile ^ k) * rows, rows), rows)
        for m, pack in enumerate(packs):
            first = pl.multiple_of(share + (s ^ m) * rows, 16)
            pack[here, :] = letter[pl.ds(0, share), :]
            pack[turned, :] = letter[pl.ds(first, rows), :]


def terms_kernel(share, rows, *refs):
    packs, out = refs[:-1], refs[-1]
    width = out.shape[1]
    replicas = packs[0].shape[0] // (share + rows)
    ones = jnp.ones((16, share), BF16)
    sums = []
    for pack in packs:
        total = jnp.zeros((2 * rows + 16, width), F32)
        for i in range(replicas):
            turned = pl.ds(replicas * share + i * rows, rows)
            field, aggregate = pack[turned, pl.ds(0, share)], pack[turned, pl.ds(128, share)]
            left = jnp.concatenate([field, aggregate, ones])
            total += contract(left, pack[pl.ds(i * share, share), :], 1, 0)
        sums.append(total)
    total = tree_sum(sums)
    tail = total[2 * rows :]
    high = tail.astype(BF16).astype(F32)
    line = lax.broadcasted_iota(jnp.int32, tail.shape, 0)
    out[pl.ds(0, 2 * rows), :] = total[: 2 * rows].astype(BF16)
    out[pl.ds(2 * rows, 16), :] = jnp.where(line == 0, high, tail - high).astype(BF16)


def back_kernel(norm, sections, replicas, *refs):
    packs, (dense, w_self, w_neigh, act) = refs[:sections], refs[sections : sections + 4]
    own, outs, (message, total) = refs[sections + 4], refs[sections + 5 : -2], refs[-2:]
    me_rep = lax.axis_index("rep")
    q, s = place_of(sections)
    block_rows = dense.shape[0]
    share = block_rows // replicas
    for k, pack in enumerate(packs):
        here = pl.ds(pl.multiple_of((s ^ k) * block_rows, block_rows), block_rows)
        grad = pack[pl.ds(0, block_rows), :]
        message[here, :] = contract(grad, w_neigh[...], 1, 1).astype(BF16)
    total[...] = contract(dense[...], message[...], 1, 0) * norm

    @pl.when(me_rep == q)
    def _():
        total[...] += contract(packs[0][pl.ds(0, block_rows), :], w_self[...], 1, 1)

    own[...] = piece_of(total, me_rep, share).astype(BF16)
    for j, out in enumerate(outs):
        out[pl.ds(0, share), :] = piece_of(total, me_rep ^ mask_of(q, j), share).astype(BF16)
    outs[0][pl.ds(share, share), :] = act[...]


def level_kernel(rows, factor, *refs):
    parts, (bias, summed) = refs[:-2], refs[-2:]
    terms = tree_sum([ref[...].astype(F32) for ref in parts])
    tail = terms[2 * rows : 2 * rows + 8]
    bias[...] = (tail[0:1] + tail[1:2]) * factor
    summed[...] = terms[: 2 * rows].astype(BF16)


def pick_kernel(sections, act, came, out):
    q, _ = place_of(sections)
    share = act.shape[0]
    arrived = came[pl.ds(share, share), :].astype(F32)
    out[...] = jnp.where(q == 0, act[...].astype(F32), arrived).astype(BF16)


def last_kernel(*refs):
    parts, (act, bias, grad_features, activations, grad_bias) = refs[:-5], refs[-5:]
    here = pl.ds(0, grad_features.shape[0])
    grad_features[...] = tree_sum([ref[here, :].astype(F32) for ref in parts]).astype(BF16)
    activations[...] = act[...]
    grad_bias[...] = bias[...]


def join_kernel(sections, *refs):
    pieces, out = refs[:-1], refs[-1]
    span = pieces[0].shape[0]
    q, _ = place_of(sections)
    for k, piece in enumerate(pieces):
        slot = (q % len(pieces)) ^ k
        out[pl.ds(pl.multiple_of(slot * span, 16), span), :] = piece[...]


def collect_kernel(rows, factor, *refs):
    joined, (grad_self, grad_neigh) = refs[:-2], refs[-2:]
    sections = len(joined)
    _, s = place_of(sections)
    for k, ref in enumerate(joined):
        for j in range(ref.shape[0] // (2 * rows)):
            place = pl.ds(pl.multiple_of((j * sections + (s ^ k)) * rows, rows), rows)
            base = j * 2 * rows
            grad_self[place, :] = ref[pl.ds(base, rows), :].astype(F32) * factor
            grad_neigh[place, :] = ref[pl.ds(base + rows, rows), :].astype(F32) * factor


def shards(
    features, w_self, w_neigh, bias_vector, cotangent, adj_values, src_slots, dst_slots, slot_counts
):
    block_rows, width = features.shape
    blocks, replicas = lax.axis_size("row"), lax.axis_size("rep")
    sections = blocks // replicas
    share = block_rows // replicas
    slot_total, size = adj_values.shape[2], adj_values.shape[-1]
    norm = 1.0 / math.sqrt(slot_total * replicas / (block_rows // size))
    factor = 1.0 / math.sqrt(block_rows * blocks)
    parts = min(blocks, width // 16)
    rows = width // parts

    def flat(q, s, c):
        return (q * sections + s) * replicas + c

    places = [
        (q, s, c) for q in range(replicas) for s in range(sections) for c in range(replicas)
    ]
    here = [flat(q, s, c) for q, s, c in places]
    source = [flat(c, s, q ^ turn(c, replicas)) for q, s, c in places]
    inside = [flat(q ^ c, s, c) for q, s, c in places]

    def swap_level(value, j):
        level = [flat(q, s, c ^ masks(q, replicas)[j]) for q, s, c in places]
        return lax.ppermute(value, ("row", "rep"), list(zip(here, level)))

    plane_rows = sections * block_rows
    pair, own, *sent = call(
        functools.partial(first_kernel, sections),
        [shape((2 * share, width), BF16)]
        + [shape((block_rows, width), BF16)] * sections,
        [SMEM] * 3 + [HBM] * 3,
        [
            pltpu.VMEM((block_rows, plane_rows), BF16),
            pltpu.VMEM((block_rows, width), BF16),
            pltpu.VMEM((plane_rows, width), F32),
            pltpu.SemaphoreType.DMA((slot_total,)),
            pltpu.SemaphoreType.DMA((2,)),
        ],
        flops=2 * plane_rows * block_rows * width,
        limit=54400 * 1024,
    )(src_slots, dst_slots, slot_counts, adj_values, features, cotangent)
    pair = lax.ppermute(pair, ("row", "rep"), list(zip(source, here)))
    received = [swap(value, k) for k, value in enumerate(sent, 1)]

    own, *sent = call(
        functools.partial(block_kernel, sections),
        [shape((share, width), F32)] + [shape((share, width), BF16)] * (replicas - 1),
        [VMEM] * sections,
        [pltpu.VMEM((block_rows, width), F32)],
    )(own, *received)
    received = [swap(value, k * sections) for k, value in enumerate(sent, 1)]

    dense, bias = call(
        dense_kernel,
        [shape((block_rows, plane_rows), BF16), shape((1, width), F32)],
        [SMEM] * 3 + [HBM, VMEM],
        [pltpu.SemaphoreType.DMA((slot_total,))],
        limit=51 * 1024 * 1024,
    )(src_slots, dst_slots, slot_counts, adj_values, bias_vector[None, :])
    dense, received[0] = lax.optimization_barrier((dense, received[0]))
    act, *letters = call(
        functools.partial(middle_kernel, norm, sections, replicas, parts),
        [shape((share, width), BF16)]
        + [shape((share + sections * rows, width), BF16)] * replicas,
        [VMEM] * (replicas + 4),
        [pltpu.VMEM((width, share), BF16)] * 2,
    )(own, *received, pair, w_self, w_neigh, bias)
    letters = letters[:1] + [swap(v, k * sections) for k, v in enumerate(letters[1:], 1)]

    packs = call(
        functools.partial(pack_kernel, sections, share, rows),
        [shape((replicas * (share + rows), width), BF16)] * sections,
        [VMEM] * replicas,
    )(*letters)
    packs = packs[:1] + [swap(value, k) for k, value in enumerate(packs[1:], 1)]

    (terms,) = call(
        functools.partial(terms_kernel, share, rows),
        [shape((2 * rows + 16, width), BF16)],
        [VMEM] * sections,
        flops=2 * plane_rows * width * (2 * rows + 16),
    )(*packs)
    terms, *packs = lax.optimization_barrier((terms, *packs))
    terms = [terms] + [swap_rep(terms, k) for k in range(1, replicas)]

    sent = call(
        functools.partial(back_kernel, norm, sections, replicas),
        [shape((share, width), BF16), shape((2 * share, width), BF16)]
        + [shape((share, width), BF16)] * (replicas - 2),
        [VMEM] * (sections + 4),
        [pltpu.VMEM((plane_rows, width), BF16), pltpu.VMEM((block_rows, width), F32)],
        flops=2 * plane_rows * width * (block_rows + width),
    )(*packs, dense, w_self, w_neigh, act)
    received = [swap_level(value, j) for j, value in enumerate(sent[3:], 2)]
    _, *terms = lax.optimization_barrier((sent[0], *terms))
    grad_bias, summed = call(
        functools.partial(level_kernel, rows, factor),
        [shape((1, width), F32), shape((2 * rows, width), BF16)],
        [VMEM] * replicas,
    )(*terms)
    summed, loaded, near = lax.optimization_barrier((summed, sent[1], sent[2]))
    loaded = swap_level(loaded, 0)
    near = swap_level(near, 1)
    (act,) = call(
        functools.partial(pick_kernel, sections),
        [shape((share, width), BF16)],
        [VMEM] * 2,
    )(act, loaded)
    act = lax.ppermute(act, ("row", "rep"), list(zip(here, inside)))
    spread = parts // sections
    pieces = [summed] + [swap(summed, k * sections) for k in range(1, spread)]
    pieces[-1], *received = lax.optimization_barrier((pieces[-1], *received))
    (joined,) = call(
        functools.partial(join_kernel, sections),
        [shape((spread * 2 * rows, width), BF16)],
        [VMEM] * spread,
    )(*pieces)
    joined = [joined] + [swap(joined, k) for k in range(1, sections)]
    grad_self, grad_neigh = call(
        functools.partial(collect_kernel, rows, factor),
        [shape((width, width), F32)] * 2,
        [VMEM] * sections,
    )(*joined)
    grad_features, activations, grad_bias = call(
        last_kernel,
        [shape((share, width), BF16)] * 2 + [shape((1, width), F32)],
        [VMEM] * (replicas + 2),
    )(sent[0], loaded, near, *received, act, grad_bias)
    return activations, grad_features, grad_self, grad_neigh, grad_bias[0]


def solution(mesh):
    placed = (
        P("row", None),
        P(),
        P(),
        P(),
        P("row", None),
        P("row", "rep", None, None, None),
        P("row", "rep", None),
        P("row", "rep", None),
        P("row", "rep"),
    )
    return jax.shard_map(
        shards,
        mesh=mesh,
        in_specs=placed,
        out_specs=(P(("row", "rep"), None), P(("row", "rep"), None), P(), P(), P()),
        check_vma=False,
    )
```
